512 devices in a mesh: seq: 64 (over z, y), head: 8 (over x, core).
Axes of the slice: x: 4, y: 4, z: 16, core: 2. Of those that a mesh axis runs over, the one named last changes fastest.
Arguments:
- queries: bfloat16 [49152, 2048], P('seq', 'head'), may hold values from -20 to 20
- keys: bfloat16 [49152, 2048], P('seq', 'head'), may hold values from -45 to 45
- values: bfloat16 [49152, 2048], P('seq', 'head'), may hold values from -6 to 6
- cluster_ids: int32 [16, 49152], P('head', 'seq'), may hold values from 0 to 511, as said below
- out_weight: bfloat16 [2048, 2048], P('head'), may hold values from -0.125 to 0.125
Outputs:
- attended: bfloat16 [49152, 2048], P(('seq', 'head'))
- key_sums: float32 [512, 2048], P('seq', 'head')
The draws below stay inside these ranges and needn't reach their ends.
Inputs may be any that keep to these rules, and one draw needn't show every extreme that they name: `cluster_ids`: in each head, the 768 tokens of one index of seq name any cluster at most 5 times, and in each head one cluster is named exactly 5 times by the tokens of every index of seq.
All inputs are finite; a program needn't handle non-finite values.
Results may differ from the reference program's by a relative error of at most 0.017.
Values may be sent and summed in bfloat16 or wider, within the bound.
No kernel may reach another device: no remote copies, remote signals or barrier semaphores. Data moves between devices by JAX's collectives and lax.ppermute only.
A program may use at most 64 MiB of HBM per device.

```python
import math
import jax
import jax.numpy as jnp
from jax import lax

D = 2048
H = 16
HD = 128
CLUSTERS = 512
TOK_DEV = 768
TOKENS = 49152
MOST = 5
N_SEQ = 64
N_HEAD = 8


def draw_queries(key, part):
    key = jax.random.fold_in(key, 1)
    key_noise = jax.random.fold_in(key, 0)
    result = 0.8 * jnp.clip(jax.random.normal(key_noise, (TOKENS, H * HD), jnp.float32), -5.0, 5.0)
    return result.astype(jnp.bfloat16)


def draw_keys(key, part):
    key = jax.random.fold_in(key, 2)
    key_noise, key_rows, key_cols = jax.random.split(key, 3)
    row_scale = jnp.exp(jax.random.uniform(key_rows, (TOKENS, 1), jnp.float32, math.log(0.3), math.log(3.0)))
    col_scale = jnp.exp(jax.random.uniform(key_cols, (1, H * HD), jnp.float32, math.log(0.3), math.log(3.0)))
    base = jnp.clip(jax.random.normal(key_noise, (TOKENS, H * HD), jnp.float32), -5.0, 5.0)
    return (row_scale * col_scale * base).astype(jnp.bfloat16)


def draw_cluster_ids(key, part):
    key = jax.random.fold_in(key, 7)
    key_base, key_rank, key_shuffle = jax.random.split(key, 3)
    blocks = TOKENS // TOK_DEV
    total_slots = CLUSTERS * MOST
    ranking = jax.vmap(lambda single: jax.random.permutation(single, CLUSTERS))(jax.random.split(key_rank, H))
    heat = jnp.where(ranking == 0, 98304, jnp.where(ranking < CLUSTERS // 8, 32768, 0)).astype(jnp.int32)
    slot_cluster = jnp.arange(total_slots, dtype=jnp.int32) // MOST
    slot_heat = heat[:, slot_cluster]
    base = jax.random.randint(key_base, (H, blocks, total_slots), 0, 32768, jnp.int32)
    scores = (base + slot_heat[:, None, :]) * total_slots + jnp.arange(total_slots, dtype=jnp.int32)[None, None, :]
    unused, picked = lax.top_k(scores, TOK_DEV)
    chosen = (picked // MOST).astype(jnp.int32)
    shuffles = jax.vmap(lambda single: jax.random.permutation(single, TOK_DEV))(jax.random.split(key_shuffle, H * blocks))
    shuffles = shuffles.reshape(H, blocks, TOK_DEV)
    result = jnp.take_along_axis(chosen, shuffles, axis=-1)
    return result.reshape(H, TOKENS).astype(jnp.int32)


def block_scale(rng, dims, pieces, least, top_value):
    def one(axis_at, shards_of):
        heights = jax.random.uniform(jax.random.fold_in(jax.random.fold_in(rng, 6), axis_at), (shards_of,), jnp.float32, least / len(pieces), top_value / len(pieces))
        return jnp.repeat(jnp.exp(heights), dims[axis_at] // shards_of).reshape((-1,) + (1,) * (len(dims) - axis_at - 1))

    gain = one(*pieces[0])
    for cut in pieces[1:]:
        gain = gain * one(*cut)
    return gain


def scatter_about(own_key, extent, spread, reach, shards=(), held_as=jnp.bfloat16):
    drawn = spread * jax.random.normal(own_key, extent, jnp.float32)
    if shards:
        drawn = drawn * block_scale(own_key, extent, shards, -0.22, 0.18)
    return jnp.clip(drawn, -reach, reach).astype(held_as)


def setup_inputs(seed: int = 0) -> dict:
    key_of = jax.random.split(jax.random.key(seed), 6)
    return {
        "queries": draw_queries(jax.random.fold_in(key_of[5], 71), 0),
        "keys": draw_keys(jax.random.fold_in(key_of[5], 71), 0),
        "values": scatter_about(key_of[2], (TOKENS, H * HD), 1.0, 6.0, ((0, 64), (1, 8))),
        "cluster_ids": draw_cluster_ids(jax.random.fold_in(key_of[5], 71), 0),
        "out_weight": scatter_about(key_of[4], (H * HD, D), (H * HD) ** -0.5, 0.125, ((0, 8),)),
    }


def attend_group(block):
    query_block, key_block, value_block, place_block = block
    scores = jnp.einsum('gqd,gkd->gqk', query_block.astype(jnp.float32), key_block.astype(jnp.float32))
    scores = scores * (1.0 / math.sqrt(HD))
    allowed = (place_block[:, None, :] >= 0) & (place_block[:, None, :] <= place_block[:, :, None])
    scores = jnp.where(allowed, scores, -1e+30)
    highest = lax.optimization_barrier(jnp.max(scores, axis=-1, keepdims=True))
    raised = jnp.exp(scores - highest)
    weights = (raised / lax.optimization_barrier(jnp.sum(raised, axis=-1, keepdims=True))).astype(jnp.bfloat16)
    result = jnp.einsum('gqk,gkd->gqd', weights.astype(jnp.float32), value_block.astype(jnp.float32))
    return result.astype(jnp.bfloat16)

def reference(queries, keys, values, cluster_ids, out_weight):
    capacity = N_SEQ * MOST
    group_size = math.gcd(CLUSTERS, 16)
    slot_index = jnp.arange(capacity, dtype=jnp.int32)
    places = jnp.concatenate([jnp.arange(TOKENS, dtype=jnp.int32), jnp.full((1,), -1, jnp.int32)])
    head_list = []
    sum_list = []
    for head_number in range(H):
        members = cluster_ids[head_number]
        order = jnp.argsort(members, stable=True).astype(jnp.int32)
        counts = jnp.zeros((CLUSTERS,), jnp.int32).at[members].add(1)
        starts = jnp.cumsum(counts) - counts
        spots = jnp.minimum(starts[:, None] + slot_index[None, :], TOKENS - 1).astype(jnp.int32)
        live = slot_index[None, :] < counts[:, None]
        table = jnp.where(live, order[spots], TOKENS).astype(jnp.int32)
        columns = slice(head_number * HD, (head_number + 1) * HD)
        padding = jnp.zeros((1, HD), jnp.bfloat16)
        query_head = jnp.concatenate([queries[:, columns], padding])
        key_head = jnp.concatenate([keys[:, columns], padding])
        value_head = jnp.concatenate([values[:, columns], padding])
        lead = (CLUSTERS // group_size, group_size, capacity)
        gathered = (query_head[table].reshape(lead + (HD,)), key_head[table].reshape(lead + (HD,)), value_head[table].reshape(lead + (HD,)), places[table].reshape(lead))
        outputs = lax.map(attend_group, gathered).reshape(CLUSTERS * capacity, HD)
        head_out = jnp.zeros((TOKENS + 1, HD), jnp.bfloat16).at[table.reshape(-1)].set(outputs)[:TOKENS]
        head_list.append(head_out)
        key_float = keys[:, columns].astype(jnp.float32)
        unit_keys = key_float * lax.rsqrt(lax.optimization_barrier(jnp.sum(key_float * key_float, axis=-1, keepdims=True)) + 1e-06)
        sum_list.append(jnp.zeros((CLUSTERS, HD), jnp.float32).at[members].add(unit_keys))
    head_outputs = jnp.concatenate(head_list, axis=1)
    key_sums = jnp.concatenate(sum_list, axis=1)
    group_width = H // N_HEAD * HD
    total = jnp.zeros((TOKENS, D), jnp.float32)
    for group_number in range(N_HEAD):
        part = jnp.dot(head_outputs[:, group_number * group_width:(group_number + 1) * group_width], out_weight[group_number * group_width:(group_number + 1) * group_width], preferred_element_type=jnp.float32)
        rounded = lax.optimization_barrier(part.astype(jnp.bfloat16))
        total = total + rounded.astype(jnp.float32)
    return (total.astype(jnp.bfloat16), key_sums)
```

```python
import functools
import math

import jax
import jax.numpy as jnp
from jax import lax
from jax.experimental import pallas as pl
from jax.experimental.pallas import tpu as pltpu
from jax.sharding import PartitionSpec as P

CLUSTERS = 512
MOST = 5
TILE = 256
VMEM = 48 * 1024 * 1024


def pack_kernel(place_ref, q_ref, k_ref, v_ref, out_ref):
    rows, toks = out_ref.shape[0], q_ref.shape[0]
    base = pl.program_id(0) * rows
    wanted = lax.broadcasted_iota(jnp.int32, (rows, toks), 0) + base
    pick = jnp.where(wanted == place_ref[0:1, :], 1.0, 0.0).astype(jnp.bfloat16)
    for part, ref in enumerate((q_ref, k_ref, v_ref)):
        width = ref.shape[1]
        moved = jnp.dot(pick, ref[...], preferred_element_type=jnp.float32)
        out_ref[:, part * width : (part + 1) * width] = moved.astype(out_ref.dtype)


def pack(place, queries, keys, values, head, head_dim, rows_all):
    toks = queries.shape[0]
    tile = 512
    column = pl.BlockSpec((toks, head_dim), lambda i: (0, head))
    return pl.pallas_call(
        pack_kernel,
        grid=(rows_all // tile,),
        in_specs=[pl.BlockSpec((1, toks), lambda i: (0, 0)), column, column, column],
        out_specs=pl.BlockSpec((tile, 3 * head_dim), lambda i: (i, 0)),
        out_shape=jax.ShapeDtypeStruct((rows_all, 3 * head_dim), queries.dtype),
        compiler_params=pltpu.CompilerParams(vmem_limit_bytes=VMEM),
        cost_estimate=pl.CostEstimate(
            flops=6 * rows_all * toks * head_dim,
            bytes_accessed=rows_all * head_dim * 6,
            transcendentals=0,
        ),
    )(place[None, :], queries, keys, values)


def attend_kernel(room, ends_ref, ends_t_ref, x_ref, out_ref, sums_ref):
    rows, width = out_ref.shape
    sources, owned = ends_ref.shape
    factor = 1.0 / math.sqrt(width)
    spread = jnp.where(
        lax.broadcasted_iota(jnp.int32, (sources, rows), 1) // room
        == lax.broadcasted_iota(jnp.int32, (sources, rows), 0),
        1.0,
        0.0,
    ).astype(jnp.bfloat16)
    ends_row = jnp.dot(
        ends_t_ref[...].astype(jnp.bfloat16), spread, preferred_element_type=jnp.float32
    )
    slot_row = (lax.broadcasted_iota(jnp.int32, (owned, rows), 1) % room).astype(jnp.float32)
    id_row = jnp.sum(jnp.where(ends_row <= slot_row, 1.0, 0.0), axis=0, keepdims=True)
    spread_col = jnp.where(
        lax.broadcasted_iota(jnp.int32, (rows, sources), 0) // room
        == lax.broadcasted_iota(jnp.int32, (rows, sources), 1),
        1.0,
        0.0,
    ).astype(jnp.bfloat16)
    ends_col = jnp.dot(
        spread_col, ends_ref[...].astype(jnp.bfloat16), preferred_element_type=jnp.float32
    )
    slot_col = (lax.broadcasted_iota(jnp.int32, (rows, owned), 0) % room).astype(jnp.float32)
    id_col = jnp.sum(jnp.where(ends_col <= slot_col, 1.0, 0.0), axis=1, keepdims=True)

    key_float = x_ref[:, width : 2 * width].astype(jnp.float32)
    unit = key_float * lax.rsqrt(jnp.sum(key_float * key_float, axis=1, keepdims=True) + 1e-06)
    high = unit.astype(jnp.bfloat16)
    low = (unit - high.astype(jnp.float32)).astype(jnp.bfloat16)
    member = jnp.where(
        lax.broadcasted_iota(jnp.int32, (owned, rows), 0).astype(jnp.float32) == id_row, 1.0, 0.0
    ).astype(jnp.bfloat16)
    sums_ref[...] = jnp.dot(member, high, preferred_element_type=jnp.float32) + jnp.dot(
        member, low, preferred_element_type=jnp.float32
    )

    for begin in range(0, rows, TILE):
        end = begin + TILE
        query = x_ref[begin:end, 0:width]
        scores = lax.dot_general(
            query,
            x_ref[0:end, width : 2 * width],
            (((1,), (1,)), ((), ())),
            preferred_element_type=jnp.float32,
        )
        allowed = (id_col[begin:end] == id_row[:, 0:end]) & (
            lax.broadcasted_iota(jnp.int32, (TILE, end), 1)
            <= lax.broadcasted_iota(jnp.int32, (TILE, end), 0) + begin
        )
        scores = jnp.where(allowed, scores * factor, -1e30)
        highest = jnp.max(scores, axis=1, keepdims=True)
        raised = jnp.exp(scores - highest)
        total = jnp.sum(raised, axis=1, keepdims=True)
        result = jnp.dot(
            raised.astype(jnp.bfloat16),
            x_ref[0:end, 2 * width : 3 * width],
            preferred_element_type=jnp.float32,
        )
        out_ref[begin:end] = (result / total).astype(out_ref.dtype)


def attend(ends, received, room, head_dim):
    rows = received.shape[0]
    owned = ends.shape[1]
    return pl.pallas_call(
        functools.partial(attend_kernel, room),
        out_shape=(
            jax.ShapeDtypeStruct((rows, head_dim), received.dtype),
            jax.ShapeDtypeStruct((owned, head_dim), jnp.float32),
        ),
        compiler_params=pltpu.CompilerParams(vmem_limit_bytes=VMEM),
        cost_estimate=pl.CostEstimate(
            flops=2 * rows * rows * head_dim,
            bytes_accessed=rows * head_dim * 8,
            transcendentals=rows * rows // 2,
        ),
    )(ends, ends.T, received)


def unpack_kernel(place_ref, back_ref, out_ref):
    toks, rows = out_ref.shape[0], back_ref.shape[0]
    pick = jnp.where(
        lax.broadcasted_iota(jnp.int32, (toks, rows), 1) == place_ref[...], 1.0, 0.0
    ).astype(jnp.bfloat16)
    out_ref[...] = jnp.dot(pick, back_ref[...], preferred_element_type=jnp.float32).astype(
        out_ref.dtype
    )


def unpack(place, back):
    toks, (rows, width) = place.shape[0], back.shape
    tile = 256
    return pl.pallas_call(
        unpack_kernel,
        grid=(toks // tile,),
        in_specs=[
            pl.BlockSpec((tile, 1), lambda i: (i, 0)),
            pl.BlockSpec((rows, width), lambda i: (0, 0)),
        ],
        out_specs=pl.BlockSpec((tile, width), lambda i: (i, 0)),
        out_shape=jax.ShapeDtypeStruct((toks, width), back.dtype),
        compiler_params=pltpu.CompilerParams(vmem_limit_bytes=VMEM),
        cost_estimate=pl.CostEstimate(
            flops=2 * rows * toks * width,
            bytes_accessed=rows * width * 2,
            transcendentals=0,
        ),
    )(place[:, None], back)


def exchange(rows, axis):
    return lax.all_to_all(rows, axis, split_axis=0, concat_axis=0, tiled=True)


def body(queries, keys, values, cluster_ids, out_weight):
    heads, toks = cluster_ids.shape
    head_dim = queries.shape[1] // heads
    sources = lax.axis_size("seq")
    groups = lax.axis_size("head")
    owned = CLUSTERS // sources
    room = owned * MOST
    full_weight = lax.all_gather(out_weight, "head", axis=0, tiled=True)

    clusters = jnp.arange(CLUSTERS, dtype=jnp.int32)
    is_in = cluster_ids[:, None, :] == clusters[None, :, None]
    counts = jnp.sum(is_in.astype(jnp.float32), axis=2)
    by_source = lax.all_gather(counts, "seq", axis=0)

    spot = jnp.arange(toks, dtype=jnp.int32)
    same = cluster_ids[:, :, None] == cluster_ids[:, None, :]
    rank = jnp.sum((same & (spot[:, None] < spot[None, :])[None]).astype(jnp.int32), axis=1)
    before = (clusters[:, None] // owned == clusters[None, :] // owned) & (
        clusters[:, None] < clusters[None, :]
    )
    offset = jnp.sum(jnp.where(before[None], counts[:, :, None], 0.0), axis=1).astype(jnp.int32)
    start = clusters[None, :] // owned * room + offset
    place = jnp.sum(jnp.where(is_in, start[:, :, None], 0), axis=1) + rank

    sent = [
        pack(place[h], queries, keys, values, h, head_dim, sources * room) for h in range(heads)
    ]
    received = [exchange(x, "seq") for x in sent]
    mine = lax.dynamic_slice_in_dim(by_source, lax.axis_index("seq") * owned, owned, axis=2)
    ends = jnp.cumsum(mine, axis=2)
    backs, sums = [], []
    for h in range(heads):
        result, partial = attend(ends[:, h], received[h], room, head_dim)
        backs.append(exchange(result, "seq"))
        sums.append(partial)
    key_sums = jnp.concatenate(sums, axis=1)
    head_outputs = jnp.concatenate([unpack(place[h], backs[h]) for h in range(heads)], axis=1)
    parts = exchange(head_outputs, "head").reshape(groups, toks // groups, heads * head_dim)
    weight = full_weight.reshape(groups, heads * head_dim, full_weight.shape[1])
    attended = jnp.einsum("gtd,gdn->tn", parts, weight, preferred_element_type=jnp.float32)
    return attended.astype(jnp.bfloat16), key_sums


def solution(mesh):
    placed = (
        P("seq", "head"),
        P("seq", "head"),
        P("seq", "head"),
        P("head", "seq"),
        P("head", None),
    )
    return jax.shard_map(
        body,
        mesh=mesh,
        in_specs=placed,
        out_specs=(P(("seq", "head"), None), P("seq", "head")),
        check_vma=False,
    )
```

```python
import functools
import math

import jax
import jax.numpy as jnp
from jax import lax
from jax.experimental import pallas as pl
from jax.experimental.pallas import tpu as pltpu
from jax.sharding import PartitionSpec as P

CLUSTERS = 512
MOST = 5
ROOM = 40
DEALS = 3
TILE = 256
LANES = 128
PARAMS = pltpu.CompilerParams(vmem_limit_bytes=48 * 1024 * 1024)
F32 = jnp.float32
BF16 = jnp.bfloat16
I32 = jnp.int32


def iota(shape, dim):
    return lax.broadcasted_iota(I32, shape, dim)


def flags(mask):
    return jnp.where(mask, 1.0, 0.0).astype(BF16)


def dot(a, b):
    return jnp.dot(a, b, preferred_element_type=F32)


def dot_t(a, b):
    return lax.dot_general(a, b, (((1,), (1,)), ((), ())), preferred_element_type=F32)


def to_col(row):
    size = row.shape[1]
    eye = iota((size, size), 0) == iota((size, size), 1)
    return jnp.sum(jnp.where(eye, row, 0.0), axis=1, keepdims=True)


def deal(position, owners, turn):
    bits = owners.bit_length() - 1
    level = position >> bits
    spot = position & (owners - 1)
    spot = jnp.where((level & 1) == 1, owners - 1 - spot, spot)
    return (spot + level * (turn * 11)) & (owners - 1), level


def plan_kernel(
    room,
    me_ref,
    all_ref,
    own_ref,
    ids_ref,
    rank_ref,
    place_ref,
    ends_ref,
    ends_t_ref,
    sums_row_ref,
    sums_col_ref,
    over_ref,
):
    me = me_ref[0]
    owners = all_ref.shape[0]
    owned = CLUSTERS // owners
    heads = ids_ref.shape[0]
    square = (CLUSTERS, CLUSTERS)
    cluster_row = iota((1, CLUSTERS), 1).astype(F32)
    home = flags(iota((owners, CLUSTERS), 1) // owned == iota((owners, CLUSTERS), 0))
    owner_lane = iota((CLUSTERS, LANES), 1)
    counts, spots, loads = [], [], []
    for h in range(heads):
        count = all_ref[:, h * CLUSTERS : (h + 1) * CLUSTERS]
        total = jnp.sum(count.astype(F32), axis=0, keepdims=True)
        order_row = total * CLUSTERS + (CLUSTERS - 1 - cluster_row)
        order_col = to_col(order_row)
        spot_row = jnp.sum(jnp.where(order_col > order_row, 1.0, 0.0), axis=0, keepdims=True)
        spot_col = jnp.sum(jnp.where(order_row > order_col, 1.0, 0.0), axis=1, keepdims=True)
        counts.append(count)
        spots.append((spot_row.astype(I32), spot_col.astype(I32)))
        tries = []
        for turn in range(1 if h == 0 else DEALS):
            at_col, _ = deal(spots[h][1], owners, turn)
            load = dot((count.astype(F32) + home.astype(F32)).astype(BF16), flags(at_col == owner_lane))
            tries.append(load)
        loads.append(tries)
    fits = [
        jnp.max(jnp.max(loads[0][0] + load, axis=1, keepdims=True), axis=0, keepdims=True)
        <= float(room)
        for load in loads[1]
    ]
    over_ref[...] = jnp.broadcast_to(
        jnp.where(fits[0] | fits[1] | fits[2], 0.0, 1.0), over_ref.shape
    )
    at_rows, at_cols, level_rows, level_cols = [], [], [], []
    for h in range(heads):
        for axis, at, level in ((0, at_rows, level_rows), (1, at_cols, level_cols)):
            chosen, lev = deal(spots[h][axis], owners, 0)
            if h == 1:
                second, _ = deal(spots[h][axis], owners, 1)
                third, _ = deal(spots[h][axis], owners, 2)
                chosen = jnp.where(fits[0], chosen, jnp.where(fits[1], second, third))
            at.append(chosen)
            level.append(lev)

    owns = [jnp.broadcast_to(own_ref[h : h + 1, :], (8, CLUSTERS)).astype(BF16) for h in range(heads)]
    for h in range(heads):
        before = flags((at_cols[h] == at_rows[h]) & (level_cols[h] < level_rows[h]))
        offset = dot(owns[h], before)
        if h == 1:
            offset = offset + dot(owns[0], flags(at_cols[0] == at_rows[1]))
        row_id = iota((8, CLUSTERS), 0)
        table = jnp.where(row_id == 0, at_rows[h].astype(F32), offset).astype(BF16)
        toks = ids_ref.shape[1]
        member = flags(iota((CLUSTERS, toks), 0) == ids_ref[h : h + 1, :])
        found = dot(table, member).astype(I32)
        place_ref[h : h + 1, :] = found[0:1] * room + found[1:2] + rank_ref[h : h + 1, :]

    items = heads * owned
    lane = iota((CLUSTERS, LANES), 1)
    item = iota((items, CLUSTERS), 0)
    ends = jnp.zeros((owners, LANES), F32)
    ends_t = jnp.zeros((items, owners), F32)
    id_row = jnp.zeros((1, LANES), F32)
    id_col = jnp.zeros((items, 1), F32)
    for h in range(heads):
        ends += dot(counts[h], flags((at_cols[h] == me) & (level_cols[h] + h * owned <= lane)))
        ends_t += dot_t(flags((at_rows[h] == me) & (level_rows[h] + h * owned <= item)), counts[h])
        hit = (at_cols[h] == me) & (level_cols[h] + h * owned == lane)
        id_row += jnp.sum(jnp.where(hit, iota(lane.shape, 0).astype(F32), 0.0), axis=0, keepdims=True)
        hit = (at_rows[h] == me) & (level_rows[h] + h * owned == item)
        id_col += jnp.sum(jnp.where(hit, cluster_row, 0.0), axis=1, keepdims=True)
    ends_ref[...] = ends
    ends_t_ref[...] = ends_t

    back_row = id_row.astype(I32) // owned
    back_col = id_col.astype(I32) // owned
    earlier = (back_col == back_row) & (iota((items, LANES), 0) < iota((items, LANES), 1))
    queue = jnp.sum(jnp.where(earlier, 1.0, 0.0), axis=0, keepdims=True)
    used = jnp.sum(
        jnp.where(iota((owners, LANES), 0) == back_row, ends[:, items - 1 : items], 0.0),
        axis=0,
        keepdims=True,
    )
    row = back_row * room + (queue + used).astype(I32)
    sums_row_ref[...] = jnp.broadcast_to(jnp.where(iota((1, LANES), 1) < items, row, -1), sums_row_ref.shape)

    at_lane = jnp.zeros((1, LANES), F32)
    turn_lane = jnp.zeros((1, LANES), F32)
    at_item = jnp.zeros((items, 1), F32)
    turn_item = jnp.zeros((items, 1), F32)
    sent = jnp.zeros((8, LANES), F32)
    for h in range(heads):
        low = me * owned - h * owned
        hit = (iota(lane.shape, 0) == lane + low) & (lane >= h * owned) & (lane < (h + 1) * owned)
        at_lane += jnp.sum(jnp.where(hit, at_cols[h].astype(F32), 0.0), axis=0, keepdims=True)
        turn_lane += jnp.sum(
            jnp.where(hit, (level_cols[h] + h * owned).astype(F32), 0.0), axis=0, keepdims=True
        )
        hit = (iota(item.shape, 1) == item + low) & (item >= h * owned) & (item < (h + 1) * owned)
        at_item += jnp.sum(jnp.where(hit, at_rows[h].astype(F32), 0.0), axis=1, keepdims=True)
        turn_item += jnp.sum(
            jnp.where(hit, (level_rows[h] + h * owned).astype(F32), 0.0), axis=1, keepdims=True
        )
        sent += dot(owns[h], flags(at_cols[h] == lane))
    small = iota((items, LANES), 1)
    ahead = (at_lane == at_item) & (turn_lane < turn_item) & (small < items)
    queue = jnp.sum(jnp.where(ahead, 1.0, 0.0), axis=1, keepdims=True)
    used = jnp.sum(
        jnp.where(small == at_item.astype(I32), sent[0:1], 0.0), axis=1, keepdims=True
    )
    sums_col_ref[...] = jnp.broadcast_to(
        at_item.astype(I32) * room + (queue + used).astype(I32), sums_col_ref.shape
    )


def make_plan(me, everyone, own, cluster_ids, rank, room):
    heads, toks = cluster_ids.shape
    owners = everyone.shape[0]
    items = heads * CLUSTERS // owners
    vmem = pl.BlockSpec(memory_space=pltpu.VMEM)
    return pl.pallas_call(
        functools.partial(plan_kernel, room),
        in_specs=[pl.BlockSpec(memory_space=pltpu.SMEM), vmem, vmem, vmem, vmem],
        out_specs=[vmem] * 6,
        out_shape=(
            jax.ShapeDtypeStruct((heads, toks), I32),
            jax.ShapeDtypeStruct((owners, LANES), F32),
            jax.ShapeDtypeStruct((items, owners), F32),
            jax.ShapeDtypeStruct((8, LANES), I32),
            jax.ShapeDtypeStruct((items, LANES), I32),
            jax.ShapeDtypeStruct((8, LANES), F32),
        ),
        compiler_params=PARAMS,
        cost_estimate=pl.CostEstimate(flops=10**9, bytes_accessed=10**6, transcendentals=0),
    )(me, everyone, own, cluster_ids, rank)


def pack_kernel(place_ref, q_ref, k_ref, v_ref, out_ref):
    rows, toks = out_ref.shape[0], q_ref.shape[0]
    heads = place_ref.shape[0]
    width = q_ref.shape[1] // heads
    wanted = iota((rows, toks), 0) + pl.program_id(0) * rows
    picks = [flags(wanted == place_ref[h : h + 1, :]) for h in range(heads)]
    for part, ref in enumerate((q_ref, k_ref, v_ref)):
        moved = jnp.zeros((rows, width), F32)
        for h in range(heads):
            moved += dot(picks[h], ref[:, h * width : (h + 1) * width])
        out_ref[:, part * width : (part + 1) * width] = moved.astype(out_ref.dtype)


def pack(place, queries, keys, values, rows_all):
    toks, width = queries.shape
    heads = place.shape[0]
    tile = 512
    whole = pl.BlockSpec((toks, width), lambda i: (0, 0))
    return pl.pallas_call(
        pack_kernel,
        grid=(rows_all // tile,),
        in_specs=[pl.BlockSpec((heads, toks), lambda i: (0, 0)), whole, whole, whole],
        out_specs=pl.BlockSpec((tile, 3 * width // heads), lambda i: (i, 0)),
        out_shape=jax.ShapeDtypeStruct((rows_all, 3 * width // heads), queries.dtype),
        compiler_params=PARAMS,
        cost_estimate=pl.CostEstimate(
            flops=6 * rows_all * toks * width,
            bytes_accessed=rows_all * width * 3,
            transcendentals=0,
        ),
    )(place, queries, keys, values)


def row_ids(room, rows, ends_ref, ends_t_ref):
    items, sources = ends_t_ref.shape
    spread = flags(iota((sources, rows), 1) // room == iota((sources, rows), 0))
    ends_row = dot(ends_t_ref[...].astype(BF16), spread)
    slot_row = (iota((items, rows), 1) % room).astype(F32)
    id_row = jnp.sum(jnp.where(ends_row <= slot_row, 1.0, 0.0), axis=0, keepdims=True)
    spread = flags(iota((rows, sources), 0) // room == iota((rows, sources), 1))
    ends_col = dot(spread, ends_ref[...].astype(BF16))
    slot_col = (iota((rows, LANES), 0) % room).astype(F32)
    past = (ends_col <= slot_col) & (iota((rows, LANES), 1) < items)
    return id_row, jnp.sum(jnp.where(past, 1.0, 0.0), axis=1, keepdims=True)


def unit_sums(key_rows, id_row, items):
    key_float = key_rows.astype(F32)
    unit = key_float * lax.rsqrt(jnp.sum(key_float * key_float, axis=1, keepdims=True) + 1e-06)
    high = unit.astype(BF16)
    low = (unit - high.astype(F32)).astype(BF16)
    member = flags(iota((items, id_row.shape[1]), 0).astype(F32) == id_row)
    return (dot(member, high) + dot(member, low)).astype(BF16)


def weigh(pieces, values, width):
    scale = math.log2(math.e) / math.sqrt(width)
    highest = jnp.max(pieces[0], axis=1, keepdims=True)
    for scores in pieces[1:]:
        highest = jnp.maximum(highest, jnp.max(scores, axis=1, keepdims=True))
    total = jnp.zeros_like(highest)
    result = jnp.zeros((highest.shape[0], width), F32)
    for scores, value in zip(pieces, values):
        raised = jnp.exp2((scores - highest) * scale)
        total += jnp.sum(raised, axis=1, keepdims=True)
        result += dot(raised.astype(BF16), value)
    return result / total


def homeward(begin, tile, sums_row_ref, sums):
    pick = flags(iota((tile, LANES), 0) + begin == sums_row_ref[0:1, :])
    return dot(pick[:, 0 : sums.shape[0]], sums)


def attend_kernel(room, ends_ref, ends_t_ref, sums_row_ref, x_ref, out_ref):
    rows, width = out_ref.shape
    id_row, id_col = row_ids(room, rows, ends_ref, ends_t_ref)
    sums = unit_sums(x_ref[:, width : 2 * width], id_row, ends_t_ref.shape[0])
    for begin in range(0, rows, TILE):
        end = begin + TILE
        query = x_ref[begin:end, 0:width]
        at = id_col[begin:end]
        pieces, values = [], []
        if begin:
            scores = dot_t(query, x_ref[0:begin, width : 2 * width])
            pieces.append(jnp.where(at == id_row[:, 0:begin], scores, -1e30))
            values.append(x_ref[0:begin, 2 * width : 3 * width])
        scores = dot_t(query, x_ref[begin:end, width : 2 * width])
        allowed = (at == id_row[:, begin:end]) & (iota((TILE, TILE), 1) <= iota((TILE, TILE), 0))
        pieces.append(jnp.where(allowed, scores, -1e30))
        values.append(x_ref[begin:end, 2 * width : 3 * width])
        result = weigh(pieces, values, width) + homeward(begin, TILE, sums_row_ref, sums)
        out_ref[begin:end] = result.astype(out_ref.dtype)


def attend_tile_kernel(
    room, ends_ref, ends_t_ref, sums_row_ref, x_ref, out_ref, row_scr, col_scr, sums_scr
):
    tile, width = out_ref.shape
    rows = x_ref.shape[0]

    @pl.when(pl.program_id(0) == 0)
    def _():
        id_row, id_col = row_ids(room, rows, ends_ref, ends_t_ref)
        row_scr[...] = jnp.broadcast_to(id_row, row_scr.shape)
        col_scr[...] = jnp.broadcast_to(id_col, col_scr.shape)
        sums_scr[...] = unit_sums(x_ref[:, width : 2 * width], id_row, ends_t_ref.shape[0])

    begin = pl.multiple_of(pl.program_id(0) * tile, tile)
    scores = dot_t(x_ref[pl.ds(begin, tile), 0:width], x_ref[:, width : 2 * width])
    allowed = (col_scr[pl.ds(begin, tile), 0:1] == row_scr[0:1, :]) & (
        iota((tile, rows), 1) <= iota((tile, rows), 0) + begin
    )
    result = weigh([jnp.where(allowed, scores, -1e30)], [x_ref[:, 2 * width : 3 * width]], width)
    out_ref[...] = (result + homeward(begin, tile, sums_row_ref, sums_scr[...])).astype(out_ref.dtype)


def attend(ends, ends_t, sums_row, received, room):
    rows, width = received.shape[0], received.shape[1] // 3
    shape = jax.ShapeDtypeStruct((rows, width), received.dtype)
    cost = pl.CostEstimate(
        flops=2 * rows * rows * width,
        bytes_accessed=rows * width * 8,
        transcendentals=rows * rows // 2,
    )
    given = (ends, ends_t, sums_row, received)
    if rows <= 4096:
        return pl.pallas_call(
            functools.partial(attend_kernel, room),
            out_shape=shape,
            compiler_params=PARAMS,
            cost_estimate=cost,
        )(*given)
    tile = 128
    return pl.pallas_call(
        functools.partial(attend_tile_kernel, room),
        grid=(rows // tile,),
        in_specs=[pl.BlockSpec(x.shape, lambda i: (0, 0)) for x in given],
        out_specs=pl.BlockSpec((tile, width), lambda i: (i, 0)),
        out_shape=shape,
        scratch_shapes=[
            pltpu.VMEM((8, rows), F32),
            pltpu.VMEM((rows, LANES), F32),
            pltpu.VMEM((ends_t.shape[0], width), BF16),
        ],
        compiler_params=PARAMS,
        cost_estimate=cost,
    )(*given)


def unpack_kernel(place_ref, sums_col_ref, over_ref, back_ref, out_ref, sums_ref):
    toks, rows = place_ref.shape[0], back_ref.shape[0]
    width = back_ref.shape[1]
    back = back_ref[...]
    for h in range(place_ref.shape[1]):
        pick = flags(iota((toks, rows), 1) == place_ref[:, h : h + 1])
        moved = dot(pick, back)
        out_ref[0, 0:toks, h * width : (h + 1) * width] = moved.astype(out_ref.dtype)
    spare = out_ref.shape[1] - toks
    out_ref[0, toks:, :] = jnp.broadcast_to(over_ref[0:1, 0:1], (spare, out_ref.shape[2])).astype(
        out_ref.dtype
    )
    items = sums_col_ref.shape[0]
    pick = flags(iota((items, rows), 1) == sums_col_ref[:, 0:1])
    sums_ref[...] = dot(pick, back)


def unpack(place, sums_col, over, back, groups):
    (toks, heads), (rows, width) = place.shape, back.shape
    tile = toks // groups
    items = sums_col.shape[0]
    whole = lambda i: (0, 0)
    return pl.pallas_call(
        unpack_kernel,
        grid=(groups,),
        in_specs=[
            pl.BlockSpec((tile, heads), lambda i: (i, 0)),
            pl.BlockSpec(sums_col.shape, whole),
            pl.BlockSpec(over.shape, whole),
            pl.BlockSpec((rows, width), whole),
        ],
        out_specs=(
            pl.BlockSpec((1, tile + 16, heads * width), lambda i: (i, 0, 0)),
            pl.BlockSpec((items, width), whole),
        ),
        out_shape=(
            jax.ShapeDtypeStruct((groups, tile + 16, heads * width), back.dtype),
            jax.ShapeDtypeStruct((items, width), F32),
        ),
        compiler_params=PARAMS,
        cost_estimate=pl.CostEstimate(
            flops=2 * rows * toks * width * heads,
            bytes_accessed=rows * width * 2,
            transcendentals=0,
        ),
    )(place, sums_col, over, back)


def exchange(rows, axis):
    return lax.all_to_all(rows, axis, split_axis=0, concat_axis=0, tiled=True)


def routed(room, queries, keys, values, cluster_ids, rank, own, everyone):
    heads = cluster_ids.shape[0]
    owners = everyone.shape[0]
    me = lax.axis_index("seq").astype(I32)[None]
    place, ends, ends_t, sums_row, sums_col, over = make_plan(
        me, everyone, own, cluster_ids, rank, room
    )
    sent = pack(place, queries, keys, values, owners * room)
    received = exchange(sent, "seq")
    back = exchange(attend(ends, ends_t, sums_row, received, room), "seq")
    share, sums = unpack(place.T, sums_col, over, back, lax.axis_size("head"))
    parts = exchange(share, "head")
    owned = CLUSTERS // owners
    return parts, jnp.concatenate([sums[h * owned : (h + 1) * owned] for h in range(heads)], axis=1)


def project(parts, weight):
    toks = parts.shape[1] - 16
    weight = weight.reshape(parts.shape[0], parts.shape[2], weight.shape[1])
    total = jnp.einsum("gtd,gdn->tn", parts[:, :toks], weight, preferred_element_type=F32)
    return total.astype(BF16)


def body(queries, keys, values, cluster_ids, out_weight):
    heads, toks = cluster_ids.shape
    owners = lax.axis_size("seq")
    clusters = jnp.arange(CLUSTERS, dtype=I32)
    own = jnp.sum((cluster_ids[:, None, :] == clusters[None, :, None]).astype(F32), axis=2)
    told = jnp.broadcast_to(own.astype(BF16).reshape(1, 8, LANES), (owners, 8, LANES))
    everyone = exchange(told, "seq").reshape(owners, heads * CLUSTERS)
    full_weight = lax.all_gather(out_weight, "head", axis=0, tiled=True)

    spot = jnp.arange(toks, dtype=I32)
    same = cluster_ids[:, :, None] == cluster_ids[:, None, :]
    rank = jnp.sum((same & (spot[:, None] < spot[None, :])[None]).astype(I32), axis=1)
    given = (queries, keys, values, cluster_ids, rank, own, everyone)
    parts, key_sums = routed(ROOM, *given)
    full_room = -(-heads * CLUSTERS // owners * (MOST + 1) // 16) * 16

    def again():
        wide, wide_sums = routed(full_room, *given)
        return project(wide, full_weight), wide_sums

    def done():
        return project(parts, full_weight), key_sums

    return lax.cond(jnp.max(parts[:, -1, 0].astype(F32)) > 0.5, again, done)


def solution(mesh):
    placed = (
        P("seq", "head"),
        P("seq", "head"),
        P("seq", "head"),
        P("head", "seq"),
        P("head", None),
    )
    return jax.shard_map(
        body,
        mesh=mesh,
        in_specs=placed,
        out_specs=(P(("seq", "head"), None), P("seq", "head")),
        check_vma=False,
    )
```

```python
import functools
import math

import jax
import jax.numpy as jnp
from jax import lax
from jax.experimental import pallas as pl
from jax.experimental.pallas import tpu as pltpu
from jax.sharding import PartitionSpec as P

CLUSTERS = 512
MOST = 5
ROOM = 32
TILE = 256
LANES = 128
PARAMS = pltpu.CompilerParams(vmem_limit_bytes=48 * 1024 * 1024)
F32 = jnp.float32
BF16 = jnp.bfloat16
I32 = jnp.int32


def iota(shape, dim):
    return lax.broadcasted_iota(I32, shape, dim)


def flags(mask):
    return jnp.where(mask, 1.0, 0.0).astype(BF16)


def dot(a, b):
    return jnp.dot(a, b, preferred_element_type=F32)


def dot_t(a, b):
    return lax.dot_general(a, b, (((1,), (1,)), ((), ())), preferred_element_type=F32)


def to_col(row):
    size = row.shape[1]
    eye = iota((size, size), 0) == iota((size, size), 1)
    return jnp.sum(jnp.where(eye, row, 0.0), axis=1, keepdims=True)


def deal(position, owners):
    bits = owners.bit_length() - 1
    level = position >> bits
    spot = position & (owners - 1)
    return jnp.where((level & 1) == 1, owners - 1 - spot, spot), level


def match(room, counts, at_rows, at_cols):
    owners = counts[0].shape[0]
    shape = (owners, LANES)
    first = dot_t(flags(iota((owners, CLUSTERS), 0) == at_rows[0]), counts[0])
    second = dot(counts[1], flags(iota((CLUSTERS, LANES), 1) == at_cols[1]))
    most = jnp.zeros(shape, F32)
    for s in range(owners):
        most = jnp.maximum(most, first[:, s : s + 1] + second[s : s + 1, :])
    lane = iota((1, LANES), 1)
    fit = jnp.where((most <= float(room)) & (lane < owners), 1.0, 0.0)
    state = jnp.concatenate([fit, jnp.broadcast_to(lane.astype(F32), (8, LANES))], axis=0)
    eye = iota(shape, 0) == iota(shape, 1)

    def pick(mask, block):
        return jnp.sum(jnp.where(mask, block[0:owners], 0.0), axis=0, keepdims=True)

    def misfits(state):
        return float(owners) - jnp.sum(jnp.where(eye, state[0:owners], 0.0))

    def swap(step, state):
        turn = step % (owners - 1) + 1
        across = iota((LANES, LANES), 0) == (iota((LANES, LANES), 1) ^ turn)
        moved = dot(state.astype(BF16), flags(across))
        across = across[0:owners]
        gain = pick(across, state) * pick(eye, moved)
        settled = pick(eye, state) * pick(across, moved)
        return jnp.where(gain * (1.0 - settled) > 0.5, moved, state)

    def more(carry):
        step, left, _ = carry
        return (left > 0.5) & (step < 4 * (owners - 1))

    def rounds(carry):
        step, _, state = carry
        for _ in range(3):
            state = swap(step, state)
            step = step + 1
        return step, misfits(state), state

    _, left, state = lax.while_loop(more, rounds, (jnp.int32(0), misfits(state), state))
    label = state[owners : owners + 1, :]
    label_col = jnp.sum(jnp.where(eye, label, 0.0), axis=1, keepdims=True).astype(I32)
    wide = (owners, CLUSTERS)
    row = jnp.sum(
        jnp.where(label_col == at_rows[1], iota(wide, 0).astype(F32), 0.0), axis=0, keepdims=True
    )
    wide = (CLUSTERS, LANES)
    col = jnp.sum(
        jnp.where(label.astype(I32) == at_cols[1], iota(wide, 1).astype(F32), 0.0),
        axis=1,
        keepdims=True,
    )
    return row.astype(I32), col.astype(I32), jnp.where(left > 0.5, 1.0, 0.0)


def plan_kernel(
    room,
    me_ref,
    all_ref,
    own_ref,
    ids_ref,
    rank_ref,
    place_ref,
    ends_ref,
    ends_t_ref,
    sums_row_ref,
    sums_col_ref,
    over_ref,
):
    me = me_ref[0]
    owners = all_ref.shape[0]
    owned = CLUSTERS // owners
    heads = ids_ref.shape[0]
    square = (CLUSTERS, CLUSTERS)
    cluster_row = iota((1, CLUSTERS), 1).astype(F32)
    home = flags(iota((owners, CLUSTERS), 1) // owned == iota((owners, CLUSTERS), 0))
    counts, at_rows, at_cols, level_rows, level_cols = [], [], [], [], []
    for h in range(heads):
        count = all_ref[:, h * CLUSTERS : (h + 1) * CLUSTERS]
        total = jnp.sum(count.astype(F32), axis=0, keepdims=True)
        order_row = total * CLUSTERS + (CLUSTERS - 1 - cluster_row)
        order_col = to_col(order_row)
        spot_row = jnp.sum(jnp.where(order_col > order_row, 1.0, 0.0), axis=0, keepdims=True)
        spot_col = jnp.sum(jnp.where(order_row > order_col, 1.0, 0.0), axis=1, keepdims=True)
        counts.append(count)
        for spot, at, level in ((spot_row, at_rows, level_rows), (spot_col, at_cols, level_cols)):
            chosen, lev = deal(spot.astype(I32), owners)
            at.append(chosen)
            level.append(lev)
    at_rows[1], at_cols[1], over = match(
        room, [(c.astype(F32) + home.astype(F32)).astype(BF16) for c in counts], at_rows, at_cols
    )
    over_ref[...] = jnp.broadcast_to(over, over_ref.shape)

    owns = [jnp.broadcast_to(own_ref[h : h + 1, :], (8, CLUSTERS)).astype(BF16) for h in range(heads)]
    for h in range(heads):
        before = flags((at_cols[h] == at_rows[h]) & (level_cols[h] < level_rows[h]))
        offset = dot(owns[h], before)
        if h == 1:
            offset = offset + dot(owns[0], flags(at_cols[0] == at_rows[1]))
        row_id = iota((8, CLUSTERS), 0)
        table = jnp.where(row_id == 0, at_rows[h].astype(F32), offset).astype(BF16)
        toks = ids_ref.shape[1]
        member = flags(iota((CLUSTERS, toks), 0) == ids_ref[h : h + 1, :])
        found = dot(table, member).astype(I32)
        place_ref[h : h + 1, :] = found[0:1] * room + found[1:2] + rank_ref[h : h + 1, :]

    items = heads * owned
    lane = iota((CLUSTERS, LANES), 1)
    item = iota((items, CLUSTERS), 0)
    ends = jnp.zeros((owners, LANES), F32)
    ends_t = jnp.zeros((items, owners), F32)
    id_row = jnp.zeros((1, LANES), F32)
    id_col = jnp.zeros((items, 1), F32)
    for h in range(heads):
        ends += dot(counts[h], flags((at_cols[h] == me) & (level_cols[h] + h * owned <= lane)))
        ends_t += dot_t(flags((at_rows[h] == me) & (level_rows[h] + h * owned <= item)), counts[h])
        hit = (at_cols[h] == me) & (level_cols[h] + h * owned == lane)
        id_row += jnp.sum(jnp.where(hit, iota(lane.shape, 0).astype(F32), 0.0), axis=0, keepdims=True)
        hit = (at_rows[h] == me) & (level_rows[h] + h * owned == item)
        id_col += jnp.sum(jnp.where(hit, cluster_row, 0.0), axis=1, keepdims=True)
    ends_ref[...] = ends
    ends_t_ref[...] = ends_t

    back_row = id_row.astype(I32) // owned
    back_col = id_col.astype(I32) // owned
    earlier = (back_col == back_row) & (iota((items, LANES), 0) < iota((items, LANES), 1))
    queue = jnp.sum(jnp.where(earlier, 1.0, 0.0), axis=0, keepdims=True)
    used = jnp.sum(
        jnp.where(iota((owners, LANES), 0) == back_row, ends[:, items - 1 : items], 0.0),
        axis=0,
        keepdims=True,
    )
    row = back_row * room + (queue + used).astype(I32)
    sums_row_ref[...] = jnp.broadcast_to(jnp.where(iota((1, LANES), 1) < items, row, -1), sums_row_ref.shape)

    at_lane = jnp.zeros((1, LANES), F32)
    turn_lane = jnp.zeros((1, LANES), F32)
    at_item = jnp.zeros((items, 1), F32)
    turn_item = jnp.zeros((items, 1), F32)
    sent = jnp.zeros((8, LANES), F32)
    for h in range(heads):
        low = me * owned - h * owned
        hit = (iota(lane.shape, 0) == lane + low) & (lane >= h * owned) & (lane < (h + 1) * owned)
        at_lane += jnp.sum(jnp.where(hit, at_cols[h].astype(F32), 0.0), axis=0, keepdims=True)
        turn_lane += jnp.sum(
            jnp.where(hit, (level_cols[h] + h * owned).astype(F32), 0.0), axis=0, keepdims=True
        )
        hit = (iota(item.shape, 1) == item + low) & (item >= h * owned) & (item < (h + 1) * owned)
        at_item += jnp.sum(jnp.where(hit, at_rows[h].astype(F32), 0.0), axis=1, keepdims=True)
        turn_item += jnp.sum(
            jnp.where(hit, (level_rows[h] + h * owned).astype(F32), 0.0), axis=1, keepdims=True
        )
        sent += dot(owns[h], flags(at_cols[h] == lane))
    small = iota((items, LANES), 1)
    ahead = (at_lane == at_item) & (turn_lane < turn_item) & (small < items)
    queue = jnp.sum(jnp.where(ahead, 1.0, 0.0), axis=1, keepdims=True)
    used = jnp.sum(
        jnp.where(small == at_item.astype(I32), sent[0:1], 0.0), axis=1, keepdims=True
    )
    sums_col_ref[...] = jnp.broadcast_to(
        at_item.astype(I32) * room + (queue + used).astype(I32), sums_col_ref.shape
    )


def make_plan(me, everyone, own, cluster_ids, rank, room):
    heads, toks = cluster_ids.shape
    owners = everyone.shape[0]
    items = heads * CLUSTERS // owners
    vmem = pl.BlockSpec(memory_space=pltpu.VMEM)
    return pl.pallas_call(
        functools.partial(plan_kernel, room),
        in_specs=[pl.BlockSpec(memory_space=pltpu.SMEM), vmem, vmem, vmem, vmem],
        out_specs=[vmem] * 6,
        out_shape=(
            jax.ShapeDtypeStruct((heads, toks), I32),
            jax.ShapeDtypeStruct((owners, LANES), F32),
            jax.ShapeDtypeStruct((items, owners), F32),
            jax.ShapeDtypeStruct((8, LANES), I32),
            jax.ShapeDtypeStruct((items, LANES), I32),
            jax.ShapeDtypeStruct((8, LANES), F32),
        ),
        compiler_params=PARAMS,
        cost_estimate=pl.CostEstimate(flops=10**9, bytes_accessed=10**6, transcendentals=0),
    )(me, everyone, own, cluster_ids, rank)


def pack_kernel(place_ref, q_ref, k_ref, v_ref, out_ref):
    rows, toks = out_ref.shape[0], q_ref.shape[0]
    heads = place_ref.shape[0]
    width = q_ref.shape[1] // heads
    wanted = iota((rows, toks), 0) + pl.program_id(0) * rows
    picks = [flags(wanted == place_ref[h : h + 1, :]) for h in range(heads)]
    for part, ref in enumerate((q_ref, k_ref, v_ref)):
        moved = jnp.zeros((rows, width), F32)
        for h in range(heads):
            moved += dot(picks[h], ref[:, h * width : (h + 1) * width])
        out_ref[:, part * width : (part + 1) * width] = moved.astype(out_ref.dtype)


def pack(place, queries, keys, values, rows_all):
    toks, width = queries.shape
    heads = place.shape[0]
    tile = 512
    whole = pl.BlockSpec((toks, width), lambda i: (0, 0))
    return pl.pallas_call(
        pack_kernel,
        grid=(rows_all // tile,),
        in_specs=[pl.BlockSpec((heads, toks), lambda i: (0, 0)), whole, whole, whole],
        out_specs=pl.BlockSpec((tile, 3 * width // heads), lambda i: (i, 0)),
        out_shape=jax.ShapeDtypeStruct((rows_all, 3 * width // heads), queries.dtype),
        compiler_params=PARAMS,
        cost_estimate=pl.CostEstimate(
            flops=6 * rows_all * toks * width,
            bytes_accessed=rows_all * width * 3,
            transcendentals=0,
        ),
    )(place, queries, keys, values)


def row_ids(room, rows, ends_ref, ends_t_ref):
    items, sources = ends_t_ref.shape
    spread = flags(iota((sources, rows), 1) // room == iota((sources, rows), 0))
    ends_row = dot(ends_t_ref[...].astype(BF16), spread)
    slot_row = (iota((items, rows), 1) % room).astype(F32)
    id_row = jnp.sum(jnp.where(ends_row <= slot_row, 1.0, 0.0), axis=0, keepdims=True)
    spread = flags(iota((rows, sources), 0) // room == iota((rows, sources), 1))
    ends_col = dot(spread, ends_ref[...].astype(BF16))
    slot_col = (iota((rows, LANES), 0) % room).astype(F32)
    past = (ends_col <= slot_col) & (iota((rows, LANES), 1) < items)
    return id_row, jnp.sum(jnp.where(past, 1.0, 0.0), axis=1, keepdims=True)


def unit_sums(key_rows, id_row, items):
    key_float = key_rows.astype(F32)
    unit = key_float * lax.rsqrt(jnp.sum(key_float * key_float, axis=1, keepdims=True) + 1e-06)
    high = unit.astype(BF16)
    low = (unit - high.astype(F32)).astype(BF16)
    member = flags(iota((items, id_row.shape[1]), 0).astype(F32) == id_row)
    return (dot(member, high) + dot(member, low)).astype(BF16)


def weigh(pieces, values, width):
    scale = math.log2(math.e) / math.sqrt(width)
    highest = jnp.max(pieces[0], axis=1, keepdims=True)
    for scores in pieces[1:]:
        highest = jnp.maximum(highest, jnp.max(scores, axis=1, keepdims=True))
    total = jnp.zeros_like(highest)
    result = jnp.zeros((highest.shape[0], width), F32)
    for scores, value in zip(pieces, values):
        raised = jnp.exp2((scores - highest) * scale)
        total += jnp.sum(raised, axis=1, keepdims=True)
        result += dot(raised.astype(BF16), value)
    return result / total


def homeward(begin, tile, sums_row_ref, sums):
    pick = flags(iota((tile, LANES), 0) + begin == sums_row_ref[0:1, :])
    return dot(pick[:, 0 : sums.shape[0]], sums)


def attend_kernel(room, ends_ref, ends_t_ref, sums_row_ref, x_ref, out_ref):
    rows, width = out_ref.shape
    id_row, id_col = row_ids(room, rows, ends_ref, ends_t_ref)
    sums = unit_sums(x_ref[:, width : 2 * width], id_row, ends_t_ref.shape[0])
    for begin in range(0, rows, TILE):
        end = begin + TILE
        query = x_ref[begin:end, 0:width]
        at = id_col[begin:end]
        pieces, values = [], []
        if begin:
            scores = dot_t(query, x_ref[0:begin, width : 2 * width])
            pieces.append(jnp.where(at == id_row[:, 0:begin], scores, -1e30))
            values.append(x_ref[0:begin, 2 * width : 3 * width])
        scores = dot_t(query, x_ref[begin:end, width : 2 * width])
        allowed = (at == id_row[:, begin:end]) & (iota((TILE, TILE), 1) <= iota((TILE, TILE), 0))
        pieces.append(jnp.where(allowed, scores, -1e30))
        values.append(x_ref[begin:end, 2 * width : 3 * width])
        result = weigh(pieces, values, width) + homeward(begin, TILE, sums_row_ref, sums)
        out_ref[begin:end] = result.astype(out_ref.dtype)


def attend_tile_kernel(
    room, ends_ref, ends_t_ref, sums_row_ref, x_ref, out_ref, row_scr, col_scr, sums_scr
):
    tile, width = out_ref.shape
    rows = x_ref.shape[0]

    @pl.when(pl.program_id(0) == 0)
    def _():
        id_row, id_col = row_ids(room, rows, ends_ref, ends_t_ref)
        row_scr[...] = jnp.broadcast_to(id_row, row_scr.shape)
        col_scr[...] = jnp.broadcast_to(id_col, col_scr.shape)
        sums_scr[...] = unit_sums(x_ref[:, width : 2 * width], id_row, ends_t_ref.shape[0])

    begin = pl.multiple_of(pl.program_id(0) * tile, tile)
    scores = dot_t(x_ref[pl.ds(begin, tile), 0:width], x_ref[:, width : 2 * width])
    allowed = (col_scr[pl.ds(begin, tile), 0:1] == row_scr[0:1, :]) & (
        iota((tile, rows), 1) <= iota((tile, rows), 0) + begin
    )
    result = weigh([jnp.where(allowed, scores, -1e30)], [x_ref[:, 2 * width : 3 * width]], width)
    out_ref[...] = (result + homeward(begin, tile, sums_row_ref, sums_scr[...])).astype(out_ref.dtype)


def attend(ends, ends_t, sums_row, received, room):
    rows, width = received.shape[0], received.shape[1] // 3
    shape = jax.ShapeDtypeStruct((rows, width), received.dtype)
    cost = pl.CostEstimate(
        flops=2 * rows * rows * width,
        bytes_accessed=rows * width * 8,
        transcendentals=rows * rows // 2,
    )
    given = (ends, ends_t, sums_row, received)
    if rows <= 4096:
        return pl.pallas_call(
            functools.partial(attend_kernel, room),
            out_shape=shape,
            compiler_params=PARAMS,
            cost_estimate=cost,
        )(*given)
    tile = 128
    return pl.pallas_call(
        functools.partial(attend_tile_kernel, room),
        grid=(rows // tile,),
        in_specs=[pl.BlockSpec(x.shape, lambda i: (0, 0)) for x in given],
        out_specs=pl.BlockSpec((tile, width), lambda i: (i, 0)),
        out_shape=shape,
        scratch_shapes=[
            pltpu.VMEM((8, rows), F32),
            pltpu.VMEM((rows, LANES), F32),
            pltpu.VMEM((ends_t.shape[0], width), BF16),
        ],
        compiler_params=PARAMS,
        cost_estimate=cost,
    )(*given)


def unpack_kernel(place_ref, sums_col_ref, over_ref, back_ref, out_ref, sums_ref):
    toks, rows = place_ref.shape[0], back_ref.shape[0]
    width = back_ref.shape[1]
    back = back_ref[...]
    for h in range(place_ref.shape[1]):
        pick = flags(iota((toks, rows), 1) == place_ref[:, h : h + 1])
        moved = dot(pick, back)
        out_ref[0, 0:toks, h * width : (h + 1) * width] = moved.astype(out_ref.dtype)
    spare = out_ref.shape[1] - toks
    out_ref[0, toks:, :] = jnp.broadcast_to(over_ref[0:1, 0:1], (spare, out_ref.shape[2])).astype(
        out_ref.dtype
    )
    items = sums_col_ref.shape[0]
    pick = flags(iota((items, rows), 1) == sums_col_ref[:, 0:1])
    sums_ref[...] = dot(pick, back)


def unpack(place, sums_col, over, back, groups):
    (toks, heads), (rows, width) = place.shape, back.shape
    tile = toks // groups
    items = sums_col.shape[0]
    whole = lambda i: (0, 0)
    return pl.pallas_call(
        unpack_kernel,
        grid=(groups,),
        in_specs=[
            pl.BlockSpec((tile, heads), lambda i: (i, 0)),
            pl.BlockSpec(sums_col.shape, whole),
            pl.BlockSpec(over.shape, whole),
            pl.BlockSpec((rows, width), whole),
        ],
        out_specs=(
            pl.BlockSpec((1, tile + 16, heads * width), lambda i: (i, 0, 0)),
            pl.BlockSpec((items, width), whole),
        ),
        out_shape=(
            jax.ShapeDtypeStruct((groups, tile + 16, heads * width), back.dtype),
            jax.ShapeDtypeStruct((items, width), F32),
        ),
        compiler_params=PARAMS,
        cost_estimate=pl.CostEstimate(
            flops=2 * rows * toks * width * heads,
            bytes_accessed=rows * width * 2,
            transcendentals=0,
        ),
    )(place, sums_col, over, back)


def exchange(rows, axis):
    return lax.all_to_all(rows, axis, split_axis=0, concat_axis=0, tiled=True)


def routed(room, queries, keys, values, cluster_ids, rank, own, everyone):
    heads = cluster_ids.shape[0]
    owners = everyone.shape[0]
    me = lax.axis_index("seq").astype(I32)[None]
    place, ends, ends_t, sums_row, sums_col, over = make_plan(
        me, everyone, own, cluster_ids, rank, room
    )
    sent = pack(place, queries, keys, values, owners * room)
    received = exchange(sent, "seq")
    back = exchange(attend(ends, ends_t, sums_row, received, room), "seq")
    share, sums = unpack(place.T, sums_col, over, back, lax.axis_size("head"))
    parts = exchange(share, "head")
    owned = CLUSTERS // owners
    return parts, jnp.concatenate([sums[h * owned : (h + 1) * owned] for h in range(heads)], axis=1)


def project(parts, weight):
    toks = parts.shape[1] - 16
    weight = weight.reshape(parts.shape[0], parts.shape[2], weight.shape[1])
    total = jnp.einsum("gtd,gdn->tn", parts[:, :toks], weight, preferred_element_type=F32)
    return total.astype(BF16)


def body(queries, keys, values, cluster_ids, out_weight):
    heads, toks = cluster_ids.shape
    owners = lax.axis_size("seq")
    clusters = jnp.arange(CLUSTERS, dtype=I32)
    own = jnp.sum((cluster_ids[:, None, :] == clusters[None, :, None]).astype(F32), axis=2)
    told = jnp.broadcast_to(own.astype(BF16).reshape(1, 8, LANES), (owners, 8, LANES))
    everyone = exchange(told, "seq").reshape(owners, heads * CLUSTERS)
    full_weight = lax.all_gather(out_weight, "head", axis=0, tiled=True)

    spot = jnp.arange(toks, dtype=I32)
    same = cluster_ids[:, :, None] == cluster_ids[:, None, :]
    rank = jnp.sum((same & (spot[:, None] < spot[None, :])[None]).astype(I32), axis=1)
    given = (queries, keys, values, cluster_ids, rank, own, everyone)
    parts, key_sums = routed(ROOM, *given)
    full_room = -(-heads * CLUSTERS // owners * (MOST + 1) // 16) * 16

    def again():
        wide, wide_sums = routed(full_room, *given)
        return project(wide, full_weight), wide_sums

    def done():
        return project(parts, full_weight), key_sums

    return lax.cond(jnp.max(parts[:, -1, 0].astype(F32)) > 0.5, again, done)


def solution(mesh):
    placed = (
        P("seq", "head"),
        P("seq", "head"),
        P("seq", "head"),
        P("head", "seq"),
        P("head", None),
    )
    return jax.shard_map(
        body,
        mesh=mesh,
        in_specs=placed,
        out_specs=(P(("seq", "head"), None), P("seq", "head")),
        check_vma=False,
    )
```

```python
import functools
import math

import jax
import jax.numpy as jnp
from jax import lax
from jax.experimental import pallas as pl
from jax.experimental.pallas import tpu as pltpu
from jax.sharding import PartitionSpec as P

CLUSTERS = 512
MOST = 5
ROOM = 32
TILE = 256
FAR = 2.0**100
LANES = 128
PARAMS = pltpu.CompilerParams(vmem_limit_bytes=48 * 1024 * 1024)
F32 = jnp.float32
BF16 = jnp.bfloat16
I32 = jnp.int32


def iota(shape, dim):
    return lax.broadcasted_iota(I32, shape, dim)


def flags(mask):
    return jnp.where(mask, 1.0, 0.0).astype(BF16)


def dot(a, b):
    return jnp.dot(a, b, preferred_element_type=F32)


def dot_t(a, b):
    return lax.dot_general(a, b, (((1,), (1,)), ((), ())), preferred_element_type=F32)


def shift_of(room):
    return room.bit_length() - 1


def to_col(row):
    size = row.shape[1]
    eye = iota((size, size), 0) == iota((size, size), 1)
    return jnp.sum(jnp.where(eye, row, 0.0), axis=1, keepdims=True)


def deal(position, owners, turn):
    bits = owners.bit_length() - 1
    level = position >> bits
    spot = position & (owners - 1)
    spot = jnp.where((level & 1) == 1, owners - 1 - spot, spot)
    return (spot + level * (turn * 11)) & (owners - 1), level


def match(room, counts, spot_rows, spot_cols, scr):
    set_scr, flip_scr, move_scr, row_scr, col_scr, first_scr, first_t_scr, state_scr, turned_scr = scr
    owners = counts[0].shape[0]
    shape = (owners, LANES)
    square = (LANES, LANES)
    tall = (CLUSTERS, LANES)
    wide = (owners, CLUSTERS)
    rows, cols, level_rows, level_cols = [], [], [], []
    for h in range(2):
        for spot, at, levels in ((spot_rows, rows, level_rows), (spot_cols, cols, level_cols)):
            chosen, level = deal(spot[h], owners, 0)
            at.append(chosen)
            levels.append(level)
    count_scr = counts[1]
    row_scr[...] = jnp.broadcast_to(spot_rows[1], row_scr.shape)
    col_scr[...] = jnp.broadcast_to(spot_cols[1], col_scr.shape)
    first_t_scr[...] = dot_t(flags(iota(wide, 0) == rows[0]), counts[0][...])
    eye = flags(iota((CLUSTERS, CLUSTERS), 0) == iota((CLUSTERS, CLUSTERS), 1))
    flip_scr[...] = dot_t(eye, counts[1][...]).astype(BF16)
    set_scr[...] = flags(iota(tall, 1) == cols[0])
    first_scr[...] = dot(counts[0][...], set_scr[...])

    def misfits():
        eye = iota(shape, 0) == iota(shape, 1)
        return float(owners) - jnp.sum(jnp.where(eye, state_scr[0:owners, :], 0.0))

    def fits(by_row, by_lane):
        most = jnp.zeros(shape, F32)
        for s in range(owners):
            most = jnp.maximum(most, by_row[:, s : s + 1] + by_lane[s : s + 1, :])
        return jnp.where((most <= float(room)) & (iota(shape, 1) < owners), 1.0, 0.0)

    def trade(step):
        eye = iota(shape, 0) == iota(shape, 1)
        fit = state_scr[0:owners, :]
        pairs = fit * turned_scr[0:owners, :]
        fine = jnp.where(eye, fit, 0.0)
        fine_row = jnp.sum(fine, axis=0, keepdims=True)
        fine_col = jnp.sum(fine, axis=1, keepdims=True)

        def granted(asker, asked, bad, good, axis):
            order = (asker * 37 + asked * 11 + step * 7) & (owners - 1)
            asks = pairs * (1.0 - bad) * good * (order + 1).astype(F32)
            asks = jnp.where(asks == jnp.max(asks, axis=axis, keepdims=True), asks, 0.0)
            asks = jnp.where(asks == jnp.max(asks, axis=1 - axis, keepdims=True), asks, 0.0)
            return jnp.minimum(asks, 1.0)

        both = granted(iota(shape, 0), iota(shape, 1), fine_col, fine_row, 1)
        both += granted(iota(shape, 1), iota(shape, 0), fine_row, fine_col, 0)
        settled = 1.0 - jnp.sum(both, axis=0, keepdims=True)
        move_scr[...] = jnp.where(
            iota(square, 0) == iota(square, 1), settled, 0.0
        ).astype(BF16)
        move_scr[0:owners, :] = (both + jnp.where(eye, settled, 0.0)).astype(BF16)
        state_scr[...] = dot(state_scr[...].astype(BF16), move_scr[...])
        turned_scr[...] = dot(move_scr[...], turned_scr[...].astype(BF16))

    def attempt(carry):
        turn, _ = carry
        at_row, _ = deal(row_scr[0:1, :], owners, turn)
        at_col, _ = deal(col_scr[...], owners, turn)
        set_scr[...] = flags(iota(tall, 1) == at_col)
        second = dot(count_scr[...], set_scr[...])
        second_t = dot(flags(iota(wide, 0) == at_row), flip_scr[...])
        state_scr[...] = iota(square, 1).astype(F32)
        state_scr[0:owners, :] = fits(first_t_scr[...], second)
        turned_scr[...] = jnp.zeros(square, F32)
        turned_scr[0:owners, :] = fits(second_t, first_scr[...])

        def trades(carry):
            step, _ = carry
            trade(step)
            return step + 1, misfits()

        _, left = lax.while_loop(
            lambda c: (c[1] > 0.5) & (c[0] < 6), trades, (jnp.int32(0), misfits())
        )
        return turn + 1, left

    turn, left = lax.while_loop(
        lambda c: (c[1] > 0.5) & (c[0] < 8), attempt, (jnp.int32(0), jnp.float32(1.0))
    )
    label = state_scr[owners : owners + 1, :]
    eye = iota(shape, 0) == iota(shape, 1)
    label_col = jnp.sum(jnp.where(eye, label, 0.0), axis=1, keepdims=True).astype(I32)
    at_row, _ = deal(row_scr[0:1, :], owners, turn - 1)
    at_col, _ = deal(col_scr[...], owners, turn - 1)
    row = jnp.where(label_col == at_row, iota(wide, 0).astype(F32), 0.0)
    rows[1] = jnp.sum(row, axis=0, keepdims=True).astype(I32)
    col = jnp.where(label.astype(I32) == at_col, iota(tall, 1).astype(F32), 0.0)
    cols[1] = jnp.sum(col, axis=1, keepdims=True).astype(I32)
    return rows, cols, level_rows, level_cols, left


def plan_kernel(
    room,
    me_ref,
    all_ref,
    own_ref,
    ids_ref,
    rank_ref,
    place_ref,
    ends_ref,
    ends_t_ref,
    sums_row_ref,
    sums_col_ref,
    first_ref,
    over_ref,
    *scratch,
):
    me = me_ref[0]
    owners = all_ref.shape[0]
    owned = CLUSTERS // owners
    heads = ids_ref.shape[0]
    cluster_row = iota((1, CLUSTERS), 1).astype(F32)
    home = flags(iota((owners, CLUSTERS), 1) // owned == iota((owners, CLUSTERS), 0))
    counts, spot_rows, spot_cols = [], [], []
    for h in range(heads):
        count = all_ref[:, h * CLUSTERS : (h + 1) * CLUSTERS]
        total = jnp.sum(count.astype(F32), axis=0, keepdims=True)
        order_row = total * CLUSTERS + (CLUSTERS - 1 - cluster_row)
        order_col = to_col(order_row)
        spot_row = jnp.sum(jnp.where(order_col > order_row, 1.0, 0.0), axis=0, keepdims=True)
        spot_col = jnp.sum(jnp.where(order_row > order_col, 1.0, 0.0), axis=1, keepdims=True)
        counts.append(count)
        spot_rows.append(spot_row.astype(I32))
        spot_cols.append(spot_col.astype(I32))
    for scr, count in zip(scratch[:heads], counts):
        scr[...] = (count.astype(F32) + home.astype(F32)).astype(BF16)
    at_rows, at_cols, level_rows, level_cols, left = match(
        room, scratch[:heads], spot_rows, spot_cols, scratch[heads:]
    )
    over_ref[...] = jnp.full(over_ref.shape, jnp.where(left > 0.5, 1.0, 0.0))

    owns = [jnp.broadcast_to(own_ref[h : h + 1, :], (8, CLUSTERS)).astype(BF16) for h in range(heads)]
    for h in range(heads):
        before = flags((at_cols[h] == at_rows[h]) & (level_cols[h] < level_rows[h]))
        offset = dot(owns[h], before)
        if h == 1:
            offset = offset + dot(owns[0], flags(at_cols[0] == at_rows[1]))
        row_id = iota((8, CLUSTERS), 0)
        table = jnp.where(row_id == 0, at_rows[h].astype(F32), offset).astype(BF16)
        toks = ids_ref.shape[1]
        member = flags(iota((CLUSTERS, toks), 0) == ids_ref[h : h + 1, :])
        found = dot(table, member).astype(I32)
        place_ref[h : h + 1, :] = found[0:1] * room + found[1:2] + rank_ref[h : h + 1, :]

    items = heads * owned
    lane = iota((CLUSTERS, LANES), 1)
    item = iota((items, CLUSTERS), 0)
    ends = jnp.zeros((owners, LANES), F32)
    ends_t = jnp.zeros((items, owners), F32)
    id_row = jnp.zeros((1, LANES), F32)
    id_col = jnp.zeros((items, 1), F32)
    for h in range(heads):
        ends += dot(counts[h], flags((at_cols[h] == me) & (level_cols[h] + h * owned <= lane)))
        ends_t += dot_t(flags((at_rows[h] == me) & (level_rows[h] + h * owned <= item)), counts[h])
        hit = (at_cols[h] == me) & (level_cols[h] + h * owned == lane)
        id_row += jnp.sum(jnp.where(hit, iota(lane.shape, 0).astype(F32), 0.0), axis=0, keepdims=True)
        hit = (at_rows[h] == me) & (level_rows[h] + h * owned == item)
        id_col += jnp.sum(jnp.where(hit, cluster_row, 0.0), axis=1, keepdims=True)
    ends_ref[...] = ends
    ends_t_ref[...] = ends_t

    back_row = id_row.astype(I32) // owned
    back_col = id_col.astype(I32) // owned
    earlier = (back_col == back_row) & (iota((items, LANES), 0) < iota((items, LANES), 1))
    queue = jnp.sum(jnp.where(earlier, 1.0, 0.0), axis=0, keepdims=True)
    used = jnp.sum(
        jnp.where(iota((owners, LANES), 0) == back_row, ends[:, items - 1 : items], 0.0),
        axis=0,
        keepdims=True,
    )
    row = back_row * room + (queue + used).astype(I32)
    sums_row_ref[...] = jnp.broadcast_to(jnp.where(iota((1, LANES), 1) < items, row, -1), sums_row_ref.shape)

    at_lane = jnp.zeros((1, LANES), F32)
    turn_lane = jnp.zeros((1, LANES), F32)
    at_item = jnp.zeros((items, 1), F32)
    turn_item = jnp.zeros((items, 1), F32)
    sent = jnp.zeros((8, LANES), F32)
    for h in range(heads):
        low = me * owned - h * owned
        hit = (iota(lane.shape, 0) == lane + low) & (lane >= h * owned) & (lane < (h + 1) * owned)
        at_lane += jnp.sum(jnp.where(hit, at_cols[h].astype(F32), 0.0), axis=0, keepdims=True)
        turn_lane += jnp.sum(
            jnp.where(hit, (level_cols[h] + h * owned).astype(F32), 0.0), axis=0, keepdims=True
        )
        hit = (iota(item.shape, 1) == item + low) & (item >= h * owned) & (item < (h + 1) * owned)
        at_item += jnp.sum(jnp.where(hit, at_rows[h].astype(F32), 0.0), axis=1, keepdims=True)
        turn_item += jnp.sum(
            jnp.where(hit, (level_rows[h] + h * owned).astype(F32), 0.0), axis=1, keepdims=True
        )
        sent += dot(owns[h], flags(at_cols[h] == lane))
        if h == 0:
            first_ref[...] = sent
    small = iota((items, LANES), 1)
    ahead = (at_lane == at_item) & (turn_lane < turn_item) & (small < items)
    queue = jnp.sum(jnp.where(ahead, 1.0, 0.0), axis=1, keepdims=True)
    used = jnp.sum(
        jnp.where(small == at_item.astype(I32), sent[0:1], 0.0), axis=1, keepdims=True
    )
    sums_col_ref[...] = jnp.broadcast_to(
        at_item.astype(I32) * room + (queue + used).astype(I32), sums_col_ref.shape
    )


def make_plan(me, everyone, own, cluster_ids, rank, room):
    heads, toks = cluster_ids.shape
    owners = everyone.shape[0]
    items = heads * CLUSTERS // owners
    vmem = pl.BlockSpec(memory_space=pltpu.VMEM)
    return pl.pallas_call(
        functools.partial(plan_kernel, room),
        in_specs=[pl.BlockSpec(memory_space=pltpu.SMEM), vmem, vmem, vmem, vmem],
        out_specs=[vmem] * 7,
        out_shape=(
            jax.ShapeDtypeStruct((heads, toks), I32),
            jax.ShapeDtypeStruct((owners, LANES), F32),
            jax.ShapeDtypeStruct((items, owners), F32),
            jax.ShapeDtypeStruct((8, LANES), I32),
            jax.ShapeDtypeStruct((items, LANES), I32),
            jax.ShapeDtypeStruct((8, LANES), F32),
            jax.ShapeDtypeStruct((8, LANES), F32),
        ),
        scratch_shapes=[
            pltpu.VMEM((owners, CLUSTERS), BF16),
            pltpu.VMEM((owners, CLUSTERS), BF16),
            pltpu.VMEM((CLUSTERS, LANES), BF16),
            pltpu.VMEM((CLUSTERS, owners), BF16),
            pltpu.VMEM((LANES, LANES), BF16),
            pltpu.VMEM((8, CLUSTERS), I32),
            pltpu.VMEM((CLUSTERS, LANES), I32),
            pltpu.VMEM((owners, LANES), F32),
            pltpu.VMEM((owners, owners), F32),
            pltpu.VMEM((LANES, LANES), F32),
            pltpu.VMEM((LANES, LANES), F32),
        ],
        compiler_params=PARAMS,
        cost_estimate=pl.CostEstimate(flops=10**9, bytes_accessed=10**6, transcendentals=0),
    )(me, everyone, own, cluster_ids, rank)


def pack_kernel(room, place_ref, first_ref, q_ref, k_ref, v_ref, out_ref):
    rows, toks = out_ref.shape[0], q_ref.shape[0]
    width = out_ref.shape[1] // 3
    base = pl.program_id(0) * rows
    wanted = iota((rows, toks), 0) + base
    pick = flags((wanted == place_ref[0:1, :]) | (wanted == place_ref[1:2, :]))
    place = iota((rows, LANES), 0) + base
    here = (place >> shift_of(room)) == iota((rows, LANES), 1)
    first = jnp.sum(jnp.where(here, first_ref[0:1, :], 0.0), axis=1, keepdims=True)
    is_first = (place[:, 0:1] & (room - 1)).astype(F32) < first
    for part, ref in enumerate((q_ref, k_ref, v_ref)):
        moved = dot(pick, ref[...])
        moved = jnp.where(is_first, moved[:, 0:width], moved[:, width:])
        out_ref[:, part * width : (part + 1) * width] = moved.astype(out_ref.dtype)


def pack(place, first, queries, keys, values, room, owners):
    toks, width = queries.shape
    heads = place.shape[0]
    rows_all = owners * room
    tile = 512
    whole = pl.BlockSpec((toks, width), lambda i: (0, 0))
    return pl.pallas_call(
        functools.partial(pack_kernel, room),
        grid=(rows_all // tile,),
        in_specs=[
            pl.BlockSpec((heads, toks), lambda i: (0, 0)),
            pl.BlockSpec(first.shape, lambda i: (0, 0)),
            whole,
            whole,
            whole,
        ],
        out_specs=pl.BlockSpec((tile, 3 * width // heads), lambda i: (i, 0)),
        out_shape=jax.ShapeDtypeStruct((rows_all, 3 * width // heads), queries.dtype),
        compiler_params=PARAMS,
        cost_estimate=pl.CostEstimate(
            flops=6 * rows_all * toks * width,
            bytes_accessed=rows_all * width * 3,
            transcendentals=0,
        ),
    )(place, first, queries, keys, values)


def ids_along(room, rows, ends_t_ref):
    items, sources = ends_t_ref.shape
    spread = flags((iota((sources, rows), 1) >> shift_of(room)) == iota((sources, rows), 0))
    ends_row = dot(ends_t_ref[...].astype(BF16), spread)
    slot_row = (iota((items, rows), 1) & (room - 1)).astype(F32)
    return jnp.sum(jnp.where(ends_row <= slot_row, 1.0, 0.0), axis=0, keepdims=True)


def ids_down(room, rows, items, ends_ref):
    sources = ends_ref.shape[0]
    spread = flags((iota((rows, sources), 0) >> shift_of(room)) == iota((rows, sources), 1))
    lane = iota(ends_ref.shape, 1)
    ends = jnp.where(lane < items, ends_ref[...], float(2 * LANES))
    starts = jnp.where(lane == 0, 0.0, pltpu.roll(ends, 1, 1))
    bounds = dot(spread, jnp.concatenate([starts, ends], axis=1).astype(BF16))
    slot = (iota((rows, LANES), 0) & (room - 1)).astype(F32)
    return (bounds[:, 0:LANES] <= slot) & (slot < bounds[:, LANES:])


def unit_sums(key_rows, id_row, items):
    key_float = key_rows.astype(F32)
    unit = key_float * lax.rsqrt(jnp.sum(key_float * key_float, axis=1, keepdims=True) + 1e-06)
    high = unit.astype(BF16)
    low = (unit - high.astype(F32)).astype(BF16)
    member = flags(iota((items, id_row.shape[1]), 0).astype(F32) == id_row)
    return (dot(member, high) + dot(member, low)).astype(BF16)


def weigh(pieces, values, width):
    scale = math.log2(math.e) / math.sqrt(width)
    highest = jnp.max(pieces[0], axis=1, keepdims=True)
    for scores in pieces[1:]:
        highest = jnp.maximum(highest, jnp.max(scores, axis=1, keepdims=True))
    total = jnp.zeros_like(highest)
    result = jnp.zeros((highest.shape[0], width), F32)
    for scores, value in zip(pieces, values):
        raised = jnp.exp2((scores - highest) * scale)
        total += jnp.sum(raised, axis=1, keepdims=True)
        result += dot(raised.astype(BF16), value)
    return result / total


def homeward(begin, tile, sums_row_ref, sums):
    pick = flags(iota((tile, LANES), 0) + begin == sums_row_ref[0:1, :])
    return dot(pick[:, 0 : sums.shape[0]], sums)


def fill(room, ends_ref, ends_t_ref, x_ref, query_scr, key_scr, value_scr):
    rows, width = x_ref.shape[0], x_ref.shape[1] // 3
    items = ends_t_ref.shape[0]
    inside = ids_down(room, rows, items, ends_ref)
    query_scr[:, 0:width] = x_ref[:, 0:width]
    query_scr[:, width:] = jnp.where(inside, 0.0, -FAR).astype(BF16)
    key_scr[:, 0:width] = x_ref[:, width : 2 * width]
    key_scr[:, width:] = flags(inside)
    value_scr[:, 0:width] = x_ref[:, 2 * width : 3 * width]
    value_scr[:, width:] = jnp.ones((rows, LANES), BF16)
    return unit_sums(x_ref[:, width : 2 * width], ids_along(room, rows, ends_t_ref), items)


def weigh(pieces, values, width):
    scale = math.log2(math.e) / math.sqrt(width)
    highest = jnp.max(pieces[0], axis=1, keepdims=True)
    for scores in pieces[1:]:
        highest = jnp.maximum(highest, jnp.max(scores, axis=1, keepdims=True))
    result = jnp.zeros((highest.shape[0], width + LANES), F32)
    for scores, value in zip(pieces, values):
        raised = jnp.exp2((scores - highest) * scale)
        result += dot(raised.astype(BF16), value)
    return result[:, 0:width] / result[:, width : width + 1]


def homeward(begin, tile, sums_row_ref, sums):
    pick = flags(iota((tile, LANES), 0) + begin == sums_row_ref[0:1, :])
    return dot(pick[:, 0 : sums.shape[0]], sums)


def attend_kernel(
    room, ends_ref, ends_t_ref, sums_row_ref, x_ref, out_ref, query_scr, key_scr, value_scr
):
    rows, width = out_ref.shape
    sums = fill(room, ends_ref, ends_t_ref, x_ref, query_scr, key_scr, value_scr)
    for begin in range(0, rows, TILE):
        end = begin + TILE
        query = query_scr[begin:end, :]
        pieces, values = [], []
        if begin:
            pieces.append(dot_t(query, key_scr[0:begin, :]))
            values.append(value_scr[0:begin, :])
        scores = dot_t(query, key_scr[begin:end, :])
        allowed = iota((TILE, TILE), 1) <= iota((TILE, TILE), 0)
        pieces.append(jnp.where(allowed, scores, -FAR))
        values.append(value_scr[begin:end, :])
        result = weigh(pieces, values, width) + homeward(begin, TILE, sums_row_ref, sums)
        out_ref[begin:end] = result.astype(out_ref.dtype)


def attend_tile_kernel(
    room,
    ends_ref,
    ends_t_ref,
    sums_row_ref,
    x_ref,
    out_ref,
    query_scr,
    key_scr,
    value_scr,
    sums_scr,
):
    tile, width = out_ref.shape
    rows = x_ref.shape[0]

    @pl.when(pl.program_id(0) == 0)
    def _():
        sums_scr[...] = fill(room, ends_ref, ends_t_ref, x_ref, query_scr, key_scr, value_scr)

    begin = pl.multiple_of(pl.program_id(0) * tile, tile)
    scores = dot_t(query_scr[pl.ds(begin, tile), :], key_scr[...])
    allowed = iota((tile, rows), 1) <= iota((tile, rows), 0) + begin
    result = weigh([jnp.where(allowed, scores, -FAR)], [value_scr[...]], width)
    out_ref[...] = (result + homeward(begin, tile, sums_row_ref, sums_scr[...])).astype(out_ref.dtype)


def attend(ends, ends_t, sums_row, received, room):
    rows, width = received.shape[0], received.shape[1] // 3
    shape = jax.ShapeDtypeStruct((rows, width), received.dtype)
    cost = pl.CostEstimate(
        flops=2 * rows * rows * width,
        bytes_accessed=rows * width * 8,
        transcendentals=rows * rows // 2,
    )
    given = (ends, ends_t, sums_row, received)
    filled = [pltpu.VMEM((rows, width + LANES), BF16)] * 3
    if rows <= 4096:
        return pl.pallas_call(
            functools.partial(attend_kernel, room),
            out_shape=shape,
            scratch_shapes=filled,
            compiler_params=PARAMS,
            cost_estimate=cost,
        )(*given)
    tile = 128
    return pl.pallas_call(
        functools.partial(attend_tile_kernel, room),
        grid=(rows // tile,),
        in_specs=[pl.BlockSpec(x.shape, lambda i: (0, 0)) for x in given],
        out_specs=pl.BlockSpec((tile, width), lambda i: (i, 0)),
        out_shape=shape,
        scratch_shapes=filled + [pltpu.VMEM((ends_t.shape[0], width), BF16)],
        compiler_params=PARAMS,
        cost_estimate=cost,
    )(*given)


def unpack_kernel(place_ref, sums_col_ref, over_ref, back_ref, out_ref, sums_ref):
    toks, heads = place_ref.shape
    rows, width = back_ref.shape
    groups = out_ref.shape[0]
    share = toks // groups
    back = back_ref[...]
    for h in range(heads):
        pick = flags(iota((toks, rows), 1) == place_ref[:, h : h + 1])
        moved = dot(pick, back).astype(out_ref.dtype)
        for g in range(groups):
            out_ref[g, 0:share, h * width : (h + 1) * width] = moved[g * share : (g + 1) * share]
    spare = out_ref.shape[1] - share
    for g in range(groups):
        out_ref[g, share:, :] = jnp.broadcast_to(
            over_ref[0:1, 0:1], (spare, out_ref.shape[2])
        ).astype(out_ref.dtype)

    @pl.when(pl.program_id(0) == 0)
    def _():
        items = sums_col_ref.shape[0]
        pick = flags(iota((items, rows), 1) == sums_col_ref[:, 0:1])
        sums_ref[...] = dot(pick, back)


def unpack(place, sums_col, over, back, groups):
    (toks, heads), (rows, width) = place.shape, back.shape
    share = toks // groups
    items = sums_col.shape[0]
    steps = max(1, min(groups, groups * rows // 8192))
    whole = lambda i: (0, 0)
    return pl.pallas_call(
        unpack_kernel,
        grid=(steps,),
        in_specs=[
            pl.BlockSpec((toks // steps, heads), lambda i: (i, 0)),
            pl.BlockSpec(sums_col.shape, whole),
            pl.BlockSpec(over.shape, whole),
            pl.BlockSpec((rows, width), whole),
        ],
        out_specs=(
            pl.BlockSpec((groups // steps, share + 16, heads * width), lambda i: (i, 0, 0)),
            pl.BlockSpec((items, width), whole),
        ),
        out_shape=(
            jax.ShapeDtypeStruct((groups, share + 16, heads * width), back.dtype),
            jax.ShapeDtypeStruct((items, width), F32),
        ),
        compiler_params=PARAMS,
        cost_estimate=pl.CostEstimate(
            flops=2 * rows * toks * width * heads,
            bytes_accessed=rows * width * 2,
            transcendentals=0,
        ),
    )(place, sums_col, over, back)


def exchange(rows, axis):
    return lax.all_to_all(rows, axis, split_axis=0, concat_axis=0, tiled=True)


def routed(room, queries, keys, values, cluster_ids, rank, own, everyone):
    heads = cluster_ids.shape[0]
    owners = everyone.shape[0]
    me = lax.axis_index("seq").astype(I32)[None]
    place, ends, ends_t, sums_row, sums_col, first, over = make_plan(
        me, everyone, own, cluster_ids, rank, room
    )
    sent = pack(place, first, queries, keys, values, room, owners)
    received = exchange(sent, "seq")
    back = exchange(attend(ends, ends_t, sums_row, received, room), "seq")
    share, sums = unpack(place.T, sums_col, over, back, lax.axis_size("head"))
    parts = exchange(share, "head")
    owned = CLUSTERS // owners
    return parts, jnp.concatenate([sums[h * owned : (h + 1) * owned] for h in range(heads)], axis=1)


def project(parts, weight):
    toks = parts.shape[1] - 16
    weight = weight.reshape(parts.shape[0], parts.shape[2], weight.shape[1])
    total = jnp.einsum("gtd,gdn->tn", parts[:, :toks], weight, preferred_element_type=F32)
    return total.astype(BF16)


def body(queries, keys, values, cluster_ids, out_weight):
    heads, toks = cluster_ids.shape
    owners = lax.axis_size("seq")
    clusters = jnp.arange(CLUSTERS, dtype=I32)
    own = jnp.sum((cluster_ids[:, None, :] == clusters[None, :, None]).astype(F32), axis=2)
    told = jnp.broadcast_to(own.astype(BF16).reshape(1, 8, LANES), (owners, 8, LANES))
    everyone = exchange(told, "seq").reshape(owners, heads * CLUSTERS)
    full_weight = lax.all_gather(out_weight, "head", axis=0, tiled=True)

    spot = jnp.arange(toks, dtype=I32)
    same = cluster_ids[:, :, None] == cluster_ids[:, None, :]
    rank = jnp.sum((same & (spot[:, None] < spot[None, :])[None]).astype(I32), axis=1)
    given = (queries, keys, values, cluster_ids, rank, own, everyone)
    parts, key_sums = routed(ROOM, *given)
    full_room = 1 << (heads * CLUSTERS // owners * (MOST + 1) - 1).bit_length()

    def again():
        wide, wide_sums = routed(full_room, *given)
        return project(wide, full_weight), wide_sums

    def done():
        return project(parts, full_weight), key_sums

    return lax.cond(jnp.max(parts[:, -1, 0].astype(F32)) > 0.5, again, done)


def solution(mesh):
    placed = (
        P("seq", "head"),
        P("seq", "head"),
        P("seq", "head"),
        P("head", "seq"),
        P("head", None),
    )
    return jax.shard_map(
        body,
        mesh=mesh,
        in_specs=placed,
        out_specs=(P(("seq", "head"), None), P("seq", "head")),
        check_vma=False,
    )
```

```python
import functools
import math

import jax
import jax.numpy as jnp
from jax import lax
from jax.experimental import pallas as pl
from jax.experimental.pallas import tpu as pltpu
from jax.sharding import PartitionSpec as P

CLUSTERS = 512
MOST = 5
ROOM = 32
TILE = 256
FAR = 2.0**100
LANES = 128
PARAMS = pltpu.CompilerParams(vmem_limit_bytes=40 * 1024 * 1024)
F32 = jnp.float32
BF16 = jnp.bfloat16
I32 = jnp.int32


def iota(shape, dim):
    return lax.broadcasted_iota(I32, shape, dim)


def flags(mask):
    return jnp.where(mask, 1.0, 0.0).astype(BF16)


def dot(a, b):
    return jnp.dot(a, b, preferred_element_type=F32)


def dot_t(a, b):
    return lax.dot_general(a, b, (((1,), (1,)), ((), ())), preferred_element_type=F32)


def shift_of(room):
    return room.bit_length() - 1


def to_col(row):
    size = row.shape[1]
    eye = iota((size, size), 0) == iota((size, size), 1)
    return jnp.sum(jnp.where(eye, row, 0.0), axis=1, keepdims=True)


def deal(position, owners, turn):
    bits = owners.bit_length() - 1
    level = position >> bits
    spot = position & (owners - 1)
    spot = jnp.where((level & 1) == 1, owners - 1 - spot, spot)
    return (spot + level * (turn * 11)) & (owners - 1), level


def match(room, counts, spot_rows, spot_cols, scr):
    set_scr, flip_scr, move_scr, row_scr, col_scr, first_scr, first_t_scr, state_scr, turned_scr = scr
    owners = counts[0].shape[0]
    shape = (owners, LANES)
    square = (LANES, LANES)
    tall = (CLUSTERS, LANES)
    wide = (owners, CLUSTERS)
    rows, cols, level_rows, level_cols = [], [], [], []
    for h in range(2):
        for spot, at, levels in ((spot_rows, rows, level_rows), (spot_cols, cols, level_cols)):
            chosen, level = deal(spot[h], owners, 0)
            at.append(chosen)
            levels.append(level)
    count_scr = counts[1]
    row_scr[...] = jnp.broadcast_to(spot_rows[1], row_scr.shape)
    col_scr[...] = jnp.broadcast_to(spot_cols[1], col_scr.shape)
    first_t_scr[...] = dot_t(flags(iota(wide, 0) == rows[0]), counts[0][...])
    eye = flags(iota((CLUSTERS, CLUSTERS), 0) == iota((CLUSTERS, CLUSTERS), 1))
    flip_scr[...] = dot_t(eye, counts[1][...]).astype(BF16)
    set_scr[...] = flags(iota(tall, 1) == cols[0])
    first_scr[...] = dot(counts[0][...], set_scr[...])

    def misfits():
        eye = iota(shape, 0) == iota(shape, 1)
        return float(owners) - jnp.sum(jnp.where(eye, state_scr[0:owners, :], 0.0))

    def fits(by_row, by_lane):
        most = jnp.zeros(shape, F32)
        for s in range(owners):
            most = jnp.maximum(most, by_row[:, s : s + 1] + by_lane[s : s + 1, :])
        return jnp.where((most <= float(room)) & (iota(shape, 1) < owners), 1.0, 0.0)

    def trade(step):
        eye = iota(shape, 0) == iota(shape, 1)
        fit = state_scr[0:owners, :]
        pairs = fit * turned_scr[0:owners, :]
        fine = jnp.where(eye, fit, 0.0)
        fine_row = jnp.sum(fine, axis=0, keepdims=True)
        fine_col = jnp.sum(fine, axis=1, keepdims=True)

        def granted(asker, asked, bad, good, axis):
            order = (asker * 37 + asked * 11 + step * 7) & (owners - 1)
            asks = pairs * (1.0 - bad) * good * (order + 1).astype(F32)
            asks = jnp.where(asks == jnp.max(asks, axis=axis, keepdims=True), asks, 0.0)
            asks = jnp.where(asks == jnp.max(asks, axis=1 - axis, keepdims=True), asks, 0.0)
            return jnp.minimum(asks, 1.0)

        both = granted(iota(shape, 0), iota(shape, 1), fine_col, fine_row, 1)
        both += granted(iota(shape, 1), iota(shape, 0), fine_row, fine_col, 0)
        settled = 1.0 - jnp.sum(both, axis=0, keepdims=True)
        move_scr[...] = jnp.where(
            iota(square, 0) == iota(square, 1), settled, 0.0
        ).astype(BF16)
        move_scr[0:owners, :] = (both + jnp.where(eye, settled, 0.0)).astype(BF16)
        state_scr[...] = dot(state_scr[...].astype(BF16), move_scr[...])
        turned_scr[...] = dot(move_scr[...], turned_scr[...].astype(BF16))

    def attempt(carry):
        turn, _ = carry
        at_row, _ = deal(row_scr[0:1, :], owners, turn)
        at_col, _ = deal(col_scr[...], owners, turn)
        set_scr[...] = flags(iota(tall, 1) == at_col)
        second = dot(count_scr[...], set_scr[...])
        second_t = dot(flags(iota(wide, 0) == at_row), flip_scr[...])
        state_scr[...] = iota(square, 1).astype(F32)
        state_scr[0:owners, :] = fits(first_t_scr[...], second)
        turned_scr[...] = jnp.zeros(square, F32)
        turned_scr[0:owners, :] = fits(second_t, first_scr[...])

        def trades(carry):
            step, _ = carry
            trade(step)
            return step + 1, misfits()

        _, left = lax.while_loop(
            lambda c: (c[1] > 0.5) & (c[0] < 6), trades, (jnp.int32(0), misfits())
        )
        return turn + 1, left

    turn, left = lax.while_loop(
        lambda c: (c[1] > 0.5) & (c[0] < 8), attempt, (jnp.int32(0), jnp.float32(1.0))
    )
    label = state_scr[owners : owners + 1, :]
    eye = iota(shape, 0) == iota(shape, 1)
    label_col = jnp.sum(jnp.where(eye, label, 0.0), axis=1, keepdims=True).astype(I32)
    at_row, _ = deal(row_scr[0:1, :], owners, turn - 1)
    at_col, _ = deal(col_scr[...], owners, turn - 1)
    row = jnp.where(label_col == at_row, iota(wide, 0).astype(F32), 0.0)
    rows[1] = jnp.sum(row, axis=0, keepdims=True).astype(I32)
    col = jnp.where(label.astype(I32) == at_col, iota(tall, 1).astype(F32), 0.0)
    cols[1] = jnp.sum(col, axis=1, keepdims=True).astype(I32)
    return rows, cols, level_rows, level_cols, left


def plan_kernel(
    room, all_ref, own_ref, ids_ref, rank_ref, place_ref, rows_ref, cols_ref, first_ref, over_ref, *scratch
):
    owners = all_ref.shape[0]
    owned = CLUSTERS // owners
    heads = ids_ref.shape[0]
    cluster_row = iota((1, CLUSTERS), 1).astype(F32)
    home = flags(iota((owners, CLUSTERS), 1) // owned == iota((owners, CLUSTERS), 0))
    counts, spot_rows, spot_cols = [], [], []
    for h in range(heads):
        count = all_ref[:, h * CLUSTERS : (h + 1) * CLUSTERS]
        total = jnp.sum(count.astype(F32), axis=0, keepdims=True)
        order_row = total * CLUSTERS + (CLUSTERS - 1 - cluster_row)
        order_col = to_col(order_row)
        spot_row = jnp.sum(jnp.where(order_col > order_row, 1.0, 0.0), axis=0, keepdims=True)
        spot_col = jnp.sum(jnp.where(order_row > order_col, 1.0, 0.0), axis=1, keepdims=True)
        counts.append(count)
        spot_rows.append(spot_row.astype(I32))
        spot_cols.append(spot_col.astype(I32))
    for scr, count in zip(scratch[:heads], counts):
        scr[...] = (count.astype(F32) + home.astype(F32)).astype(BF16)
    at_rows, at_cols, level_rows, level_cols, left = match(
        room, scratch[:heads], spot_rows, spot_cols, scratch[heads:]
    )
    over_ref[...] = jnp.full(over_ref.shape, jnp.where(left > 0.5, 1.0, 0.0))

    owns = [jnp.broadcast_to(own_ref[h : h + 1, :], (8, CLUSTERS)).astype(BF16) for h in range(heads)]
    for h in range(heads):
        before = flags((at_cols[h] == at_rows[h]) & (level_cols[h] < level_rows[h]))
        offset = dot(owns[h], before)
        if h == 1:
            offset = offset + dot(owns[0], flags(at_cols[0] == at_rows[1]))
        row_id = iota((8, CLUSTERS), 0)
        table = jnp.where(row_id == 0, at_rows[h].astype(F32), offset).astype(BF16)
        toks = ids_ref.shape[1]
        member = flags(iota((CLUSTERS, toks), 0) == ids_ref[h : h + 1, :])
        found = dot(table, member).astype(I32)
        place_ref[h : h + 1, :] = found[0:1] * room + found[1:2] + rank_ref[h : h + 1, :]

    rows_ref[...] = jnp.concatenate(at_rows + level_rows + [jnp.zeros((4, CLUSTERS), I32)], axis=0)
    column = iota((CLUSTERS, LANES), 1)
    found = jnp.zeros((CLUSTERS, LANES), I32)
    for i, values in enumerate(at_cols + level_cols):
        found = jnp.where(column == i, values, found)
    cols_ref[...] = found
    set_scr = scratch[heads]
    set_scr[...] = flags(at_cols[0] == column)
    first_ref[...] = dot(owns[0], set_scr[...])


def arrive_kernel(
    room,
    me_ref,
    all_ref,
    own_ref,
    rows_ref,
    cols_ref,
    sums_row_ref,
    sums_col_ref,
    query_ref,
    key_ref,
    member_ref,
):
    me = me_ref[0]
    owners = all_ref.shape[0]
    owned = CLUSTERS // owners
    heads = own_ref.shape[0]
    cluster_row = iota((1, CLUSTERS), 1).astype(F32)
    counts = [all_ref[:, h * CLUSTERS : (h + 1) * CLUSTERS] for h in range(heads)]
    owns = [jnp.broadcast_to(own_ref[h : h + 1, :], (8, CLUSTERS)).astype(BF16) for h in range(heads)]
    at_rows = [rows_ref[h : h + 1, :] for h in range(heads)]
    level_rows = [rows_ref[heads + h : heads + h + 1, :] for h in range(heads)]
    at_cols = [cols_ref[:, h : h + 1] for h in range(heads)]
    level_cols = [cols_ref[:, heads + h : heads + h + 1] for h in range(heads)]

    items = heads * owned
    lane = iota((CLUSTERS, LANES), 1)
    item = iota((items, CLUSTERS), 0)
    ends = jnp.zeros((owners, LANES), F32)
    ends_t = jnp.zeros((items, owners), F32)
    id_row = jnp.zeros((1, LANES), F32)
    id_col = jnp.zeros((items, 1), F32)
    for h in range(heads):
        ends += dot(counts[h], flags((at_cols[h] == me) & (level_cols[h] + h * owned <= lane)))
        ends_t += dot_t(flags((at_rows[h] == me) & (level_rows[h] + h * owned <= item)), counts[h])
        hit = (at_cols[h] == me) & (level_cols[h] + h * owned == lane)
        id_row += jnp.sum(jnp.where(hit, iota(lane.shape, 0).astype(F32), 0.0), axis=0, keepdims=True)
        hit = (at_rows[h] == me) & (level_rows[h] + h * owned == item)
        id_col += jnp.sum(jnp.where(hit, cluster_row, 0.0), axis=1, keepdims=True)
    rows = key_ref.shape[0]
    inside = ids_down(room, rows, items, ends)
    query_ref[...] = jnp.where(inside, 0.0, -FAR).astype(BF16)
    key_ref[...] = flags(inside)
    id_along = ids_along(room, rows, ends_t)
    member_ref[...] = flags(iota((items, rows), 0).astype(F32) == id_along)

    back_row = id_row.astype(I32) // owned
    back_col = id_col.astype(I32) // owned
    earlier = (back_col == back_row) & (iota((items, LANES), 0) < iota((items, LANES), 1))
    queue = jnp.sum(jnp.where(earlier, 1.0, 0.0), axis=0, keepdims=True)
    used = jnp.sum(
        jnp.where(iota((owners, LANES), 0) == back_row, ends[:, items - 1 : items], 0.0),
        axis=0,
        keepdims=True,
    )
    row = back_row * room + (queue + used).astype(I32)
    sums_row_ref[...] = jnp.broadcast_to(jnp.where(iota((1, LANES), 1) < items, row, -1), sums_row_ref.shape)

    at_lane = jnp.zeros((1, LANES), F32)
    turn_lane = jnp.zeros((1, LANES), F32)
    at_item = jnp.zeros((items, 1), F32)
    turn_item = jnp.zeros((items, 1), F32)
    sent = jnp.zeros((8, LANES), F32)
    for h in range(heads):
        low = me * owned - h * owned
        hit = (iota(lane.shape, 0) == lane + low) & (lane >= h * owned) & (lane < (h + 1) * owned)
        at_lane += jnp.sum(jnp.where(hit, at_cols[h].astype(F32), 0.0), axis=0, keepdims=True)
        turn_lane += jnp.sum(
            jnp.where(hit, (level_cols[h] + h * owned).astype(F32), 0.0), axis=0, keepdims=True
        )
        hit = (iota(item.shape, 1) == item + low) & (item >= h * owned) & (item < (h + 1) * owned)
        at_item += jnp.sum(jnp.where(hit, at_rows[h].astype(F32), 0.0), axis=1, keepdims=True)
        turn_item += jnp.sum(
            jnp.where(hit, (level_rows[h] + h * owned).astype(F32), 0.0), axis=1, keepdims=True
        )
        sent += dot(owns[h], flags(at_cols[h] == lane))
    small = iota((items, LANES), 1)
    ahead = (at_lane == at_item) & (turn_lane < turn_item) & (small < items)
    queue = jnp.sum(jnp.where(ahead, 1.0, 0.0), axis=1, keepdims=True)
    used = jnp.sum(
        jnp.where(small == at_item.astype(I32), sent[0:1], 0.0), axis=1, keepdims=True
    )
    sums_col_ref[...] = jnp.broadcast_to(
        at_item.astype(I32) * room + (queue + used).astype(I32), sums_col_ref.shape
    )


def make_plan(everyone, own, cluster_ids, rank, room):
    heads, toks = cluster_ids.shape
    owners = everyone.shape[0]
    return pl.pallas_call(
        functools.partial(plan_kernel, room),
        out_shape=(
            jax.ShapeDtypeStruct((heads, toks), I32),
            jax.ShapeDtypeStruct((8, CLUSTERS), I32),
            jax.ShapeDtypeStruct((CLUSTERS, LANES), I32),
            jax.ShapeDtypeStruct((8, LANES), F32),
            jax.ShapeDtypeStruct((8, LANES), F32),
        ),
        scratch_shapes=[
            pltpu.VMEM((owners, CLUSTERS), BF16),
            pltpu.VMEM((owners, CLUSTERS), BF16),
            pltpu.VMEM((CLUSTERS, LANES), BF16),
            pltpu.VMEM((CLUSTERS, owners), BF16),
            pltpu.VMEM((LANES, LANES), BF16),
            pltpu.VMEM((8, CLUSTERS), I32),
            pltpu.VMEM((CLUSTERS, LANES), I32),
            pltpu.VMEM((owners, LANES), F32),
            pltpu.VMEM((owners, owners), F32),
            pltpu.VMEM((LANES, LANES), F32),
            pltpu.VMEM((LANES, LANES), F32),
        ],
        compiler_params=PARAMS,
        cost_estimate=pl.CostEstimate(flops=10**9, bytes_accessed=10**6, transcendentals=0),
    )(everyone, own, cluster_ids, rank)


def arrive(me, everyone, own, rows, cols, room):
    owners = everyone.shape[0]
    items = own.shape[0] * CLUSTERS // owners
    vmem = pl.BlockSpec(memory_space=pltpu.VMEM)
    return pl.pallas_call(
        functools.partial(arrive_kernel, room),
        in_specs=[pl.BlockSpec(memory_space=pltpu.SMEM)] + [vmem] * 4,
        out_specs=[vmem] * 5,
        out_shape=(
            jax.ShapeDtypeStruct((8, LANES), I32),
            jax.ShapeDtypeStruct((items, LANES), I32),
            jax.ShapeDtypeStruct((owners * room, LANES), BF16),
            jax.ShapeDtypeStruct((owners * room, LANES), BF16),
            jax.ShapeDtypeStruct((items, owners * room), BF16),
        ),
        compiler_params=PARAMS,
        cost_estimate=pl.CostEstimate(flops=10**9, bytes_accessed=10**6, transcendentals=0),
    )(me, everyone, own, rows, cols)


def pack_kernel(room, place_ref, first_ref, q_ref, k_ref, v_ref, out_ref):
    rows, toks = out_ref.shape[0], q_ref.shape[0]
    width = out_ref.shape[1] // 3
    base = pl.program_id(0) * rows
    wanted = iota((rows, toks), 0) + base
    pick = flags((wanted == place_ref[0:1, :]) | (wanted == place_ref[1:2, :]))
    place = iota((rows, LANES), 0) + base
    here = (place >> shift_of(room)) == iota((rows, LANES), 1)
    first = jnp.sum(jnp.where(here, first_ref[0:1, :], 0.0), axis=1, keepdims=True)
    is_first = (place[:, 0:1] & (room - 1)).astype(F32) < first
    for part, ref in enumerate((q_ref, k_ref, v_ref)):
        moved = dot(pick, ref[...])
        moved = jnp.where(is_first, moved[:, 0:width], moved[:, width:])
        out_ref[:, part * width : (part + 1) * width] = moved.astype(out_ref.dtype)


def pack(place, first, queries, keys, values, room, owners):
    toks, width = queries.shape
    heads = place.shape[0]
    rows_all = owners * room
    tile = 512
    whole = pl.BlockSpec((toks, width), lambda i: (0, 0))
    return pl.pallas_call(
        functools.partial(pack_kernel, room),
        grid=(rows_all // tile,),
        in_specs=[
            pl.BlockSpec((heads, toks), lambda i: (0, 0)),
            pl.BlockSpec(first.shape, lambda i: (0, 0)),
            whole,
            whole,
            whole,
        ],
        out_specs=pl.BlockSpec((tile, 3 * width // heads), lambda i: (i, 0)),
        out_shape=jax.ShapeDtypeStruct((rows_all, 3 * width // heads), queries.dtype),
        compiler_params=PARAMS,
        cost_estimate=pl.CostEstimate(
            flops=6 * rows_all * toks * width,
            bytes_accessed=rows_all * width * 3,
            transcendentals=0,
        ),
    )(place, first, queries, keys, values)


def ids_along(room, rows, ends_t):
    items, sources = ends_t.shape
    spread = flags((iota((sources, rows), 1) >> shift_of(room)) == iota((sources, rows), 0))
    ends_row = dot(ends_t.astype(BF16), spread)
    slot_row = (iota((items, rows), 1) & (room - 1)).astype(F32)
    return jnp.sum(jnp.where(ends_row <= slot_row, 1.0, 0.0), axis=0, keepdims=True)


def ids_down(room, rows, items, ends):
    sources = ends.shape[0]
    spread = flags((iota((rows, sources), 0) >> shift_of(room)) == iota((rows, sources), 1))
    lane = iota(ends.shape, 1)
    ends = jnp.where(lane < items, ends, float(2 * LANES))
    starts = jnp.where(lane == 0, 0.0, pltpu.roll(ends, 1, 1))
    bounds = dot(spread, jnp.concatenate([starts, ends], axis=1).astype(BF16))
    slot = (iota((rows, LANES), 0) & (room - 1)).astype(F32)
    return (bounds[:, 0:LANES] <= slot) & (slot < bounds[:, LANES:])


def unit_sums(key_rows, member):
    key_float = key_rows.astype(F32)
    unit = key_float * lax.rsqrt(jnp.sum(key_float * key_float, axis=1, keepdims=True) + 1e-06)
    high = unit.astype(BF16)
    low = (unit - high.astype(F32)).astype(BF16)
    return (dot(member, high) + dot(member, low)).astype(BF16)


def fill(query_ref, key_ref, member_ref, x_ref, query_scr, key_scr, value_scr):
    rows, width = x_ref.shape[0], x_ref.shape[1] // 3
    query_scr[:, 0:width] = x_ref[:, 0:width]
    query_scr[:, width:] = query_ref[...]
    key_scr[:, 0:width] = x_ref[:, width : 2 * width]
    key_scr[:, width:] = key_ref[...]
    value_scr[:, 0:width] = x_ref[:, 2 * width : 3 * width]
    value_scr[:, width:] = jnp.ones((rows, LANES), BF16)
    return unit_sums(x_ref[:, width : 2 * width], member_ref[...])


def weigh(pieces, values, width):
    scale = math.log2(math.e) / math.sqrt(width)
    highest = jnp.max(pieces[0], axis=1, keepdims=True)
    for scores in pieces[1:]:
        highest = jnp.maximum(highest, jnp.max(scores, axis=1, keepdims=True))
    result = jnp.zeros((highest.shape[0], width + LANES), F32)
    for scores, value in zip(pieces, values):
        raised = jnp.exp2((scores - highest) * scale)
        result += dot(raised.astype(BF16), value)
    return result[:, 0:width] / result[:, width : width + 1]


def homeward(begin, tile, sums_row_ref, sums):
    pick = flags(iota((tile, LANES), 0) + begin == sums_row_ref[0:1, :])
    return dot(pick[:, 0 : sums.shape[0]], sums)


def attend_kernel(
    query_ref, key_ref, member_ref, sums_row_ref, x_ref, out_ref, query_scr, key_scr, value_scr
):
    rows, width = out_ref.shape
    sums = fill(query_ref, key_ref, member_ref, x_ref, query_scr, key_scr, value_scr)
    for begin in range(0, rows, TILE):
        end = begin + TILE
        query = query_scr[begin:end, :]
        pieces, values = [], []
        if begin:
            pieces.append(dot_t(query, key_scr[0:begin, :]))
            values.append(value_scr[0:begin, :])
        scores = dot_t(query, key_scr[begin:end, :])
        allowed = iota((TILE, TILE), 1) <= iota((TILE, TILE), 0)
        pieces.append(jnp.where(allowed, scores, -FAR))
        values.append(value_scr[begin:end, :])
        result = weigh(pieces, values, width) + homeward(begin, TILE, sums_row_ref, sums)
        out_ref[begin:end] = result.astype(out_ref.dtype)


def attend_tile_kernel(
    query_ref,
    key_ref,
    member_ref,
    sums_row_ref,
    x_ref,
    out_ref,
    query_scr,
    key_scr,
    value_scr,
    sums_scr,
):
    tile, width = out_ref.shape
    rows = x_ref.shape[0]

    @pl.when(pl.program_id(0) == 0)
    def _():
        sums_scr[...] = fill(query_ref, key_ref, member_ref, x_ref, query_scr, key_scr, value_scr)

    begin = pl.multiple_of(pl.program_id(0) * tile, tile)
    scores = dot_t(query_scr[pl.ds(begin, tile), :], key_scr[...])
    allowed = iota((tile, rows), 1) <= iota((tile, rows), 0) + begin
    result = weigh([jnp.where(allowed, scores, -FAR)], [value_scr[...]], width)
    out_ref[...] = (result + homeward(begin, tile, sums_row_ref, sums_scr[...])).astype(out_ref.dtype)


def attend(query_far, key_far, member, sums_row, received):
    rows, width = received.shape[0], received.shape[1] // 3
    shape = jax.ShapeDtypeStruct((rows, width), received.dtype)
    cost = pl.CostEstimate(
        flops=2 * rows * rows * width,
        bytes_accessed=rows * width * 8,
        transcendentals=rows * rows // 2,
    )
    given = (query_far, key_far, member, sums_row, received)
    filled = [pltpu.VMEM((rows, width + LANES), BF16)] * 3
    if rows <= 4096:
        return pl.pallas_call(
            attend_kernel,
            out_shape=shape,
            scratch_shapes=filled,
            compiler_params=PARAMS,
            cost_estimate=cost,
        )(*given)
    tile = 128
    return pl.pallas_call(
        attend_tile_kernel,
        grid=(rows // tile,),
        in_specs=[pl.BlockSpec(x.shape, lambda i: (0, 0)) for x in given],
        out_specs=pl.BlockSpec((tile, width), lambda i: (i, 0)),
        out_shape=shape,
        scratch_shapes=filled + [pltpu.VMEM((member.shape[0], width), BF16)],
        compiler_params=PARAMS,
        cost_estimate=cost,
    )(*given)


def unpack_kernel(place_ref, sums_col_ref, over_ref, back_ref, out_ref, sums_ref):
    toks, heads = place_ref.shape
    rows, width = back_ref.shape
    groups = out_ref.shape[0]
    share = toks // groups
    back = back_ref[...]
    for h in range(heads):
        pick = flags(iota((toks, rows), 1) == place_ref[:, h : h + 1])
        moved = dot(pick, back).astype(out_ref.dtype)
        for g in range(groups):
            out_ref[g, 0:share, h * width : (h + 1) * width] = moved[g * share : (g + 1) * share]
    spare = out_ref.shape[1] - share
    for g in range(groups):
        out_ref[g, share:, :] = jnp.broadcast_to(
            over_ref[0:1, 0:1], (spare, out_ref.shape[2])
        ).astype(out_ref.dtype)

    @pl.when(pl.program_id(0) == 0)
    def _():
        items = sums_col_ref.shape[0]
        pick = flags(iota((items, rows), 1) == sums_col_ref[:, 0:1])
        sums_ref[...] = dot(pick, back)


def unpack(place, sums_col, over, back, groups):
    (toks, heads), (rows, width) = place.shape, back.shape
    share = toks // groups
    items = sums_col.shape[0]
    steps = max(1, min(groups, groups * rows // 8192))
    whole = lambda i: (0, 0)
    return pl.pallas_call(
        unpack_kernel,
        grid=(steps,),
        in_specs=[
            pl.BlockSpec((toks // steps, heads), lambda i: (i, 0)),
            pl.BlockSpec(sums_col.shape, whole),
            pl.BlockSpec(over.shape, whole),
            pl.BlockSpec((rows, width), whole),
        ],
        out_specs=(
            pl.BlockSpec((groups // steps, share + 16, heads * width), lambda i: (i, 0, 0)),
            pl.BlockSpec((items, width), whole),
        ),
        out_shape=(
            jax.ShapeDtypeStruct((groups, share + 16, heads * width), back.dtype),
            jax.ShapeDtypeStruct((items, width), F32),
        ),
        compiler_params=PARAMS,
        cost_estimate=pl.CostEstimate(
            flops=2 * rows * toks * width * heads,
            bytes_accessed=rows * width * 2,
            transcendentals=0,
        ),
    )(place, sums_col, over, back)


def exchange(rows, axis):
    return lax.all_to_all(rows, axis, split_axis=0, concat_axis=0, tiled=True)


def routed(room, queries, keys, values, cluster_ids, rank, own, everyone):
    heads = cluster_ids.shape[0]
    owners = everyone.shape[0]
    me = lax.axis_index("seq").astype(I32)[None]
    place, rows, cols, first, over = make_plan(everyone, own, cluster_ids, rank, room)
    received = exchange(pack(place, first, queries, keys, values, room, owners), "seq")
    sums_row, sums_col, query_far, key_far, member = arrive(me, everyone, own, rows, cols, room)
    back = exchange(attend(query_far, key_far, member, sums_row, received), "seq")
    share, sums = unpack(place.T, sums_col, over, back, lax.axis_size("head"))
    parts = exchange(share, "head")
    owned = CLUSTERS // owners
    sums = jnp.concatenate([sums[h * owned : (h + 1) * owned] for h in range(heads)], axis=1)
    return parts, sums


def project_kernel(parts_ref, weight_ref, out_ref, total_scr):
    step, toks = pl.program_id(0), out_ref.shape[0]
    part = dot(parts_ref[0, 0:toks, :], weight_ref[...])

    @pl.when(step == 0)
    def _():
        total_scr[...] = part

    @pl.when(step > 0)
    def _():
        total_scr[...] += part

    @pl.when(step == pl.num_programs(0) - 1)
    def _():
        out_ref[...] = total_scr[...].astype(out_ref.dtype)


def project(parts, weight):
    groups, toks, width = parts.shape
    toks -= 16
    deep, wide = weight.shape
    return pl.pallas_call(
        project_kernel,
        grid=(groups,),
        in_specs=[
            pl.BlockSpec((1,) + parts.shape[1:], lambda i: (i, 0, 0)),
            pl.BlockSpec((width, wide), lambda i: (i, 0)),
        ],
        out_specs=pl.BlockSpec((toks, wide), lambda i: (0, 0)),
        out_shape=jax.ShapeDtypeStruct((toks, wide), BF16),
        scratch_shapes=[pltpu.VMEM((toks, wide), F32)],
        compiler_params=pltpu.CompilerParams(vmem_limit_bytes=16 * 1024 * 1024),
        cost_estimate=pl.CostEstimate(
            flops=2 * toks * deep * wide, bytes_accessed=deep * wide * 2, transcendentals=0
        ),
    )(parts, weight)


def body(queries, keys, values, cluster_ids, out_weight):
    heads, toks = cluster_ids.shape
    owners = lax.axis_size("seq")
    clusters = jnp.arange(CLUSTERS, dtype=I32)
    own = jnp.sum((cluster_ids[:, None, :] == clusters[None, :, None]).astype(F32), axis=2)
    told = jnp.broadcast_to(own.astype(BF16).reshape(1, 8, LANES), (owners, 8, LANES))
    everyone = exchange(told, "seq").reshape(owners, heads * CLUSTERS)
    full_weight = lax.all_gather(out_weight, "head", axis=0, tiled=True)

    spot = jnp.arange(toks, dtype=I32)
    same = cluster_ids[:, :, None] == cluster_ids[:, None, :]
    rank = jnp.sum((same & (spot[:, None] < spot[None, :])[None]).astype(I32), axis=1)
    given = (queries, keys, values, cluster_ids, rank, own, everyone)
    parts, key_sums = routed(ROOM, *given)
    full_room = 1 << (heads * CLUSTERS // owners * (MOST + 1) - 1).bit_length()

    def again():
        wide, wide_sums = routed(full_room, *given)
        return project(wide, full_weight), wide_sums

    def done():
        return project(parts, full_weight), key_sums

    return lax.cond(jnp.max(parts[:, -1, 0].astype(F32)) > 0.5, again, done)


def solution(mesh):
    placed = (
        P("seq", "head"),
        P("seq", "head"),
        P("seq", "head"),
        P("head", "seq"),
        P("head", None),
    )
    return jax.shard_map(
        body,
        mesh=mesh,
        in_specs=placed,
        out_specs=(P(("seq", "head"), None), P("seq", "head")),
        check_vma=False,
    )
```

```python
import functools
import math

import jax
import jax.numpy as jnp
from jax import lax
from jax.experimental import pallas as pl
from jax.experimental.pallas import tpu as pltpu
from jax.sharding import PartitionSpec as P

CLUSTERS = 512
MOST = 5
ROOM = 32
TILE = 256
FAR = 2.0**100
LANES = 128
PARAMS = pltpu.CompilerParams(vmem_limit_bytes=40 * 1024 * 1024)
F32 = jnp.float32
BF16 = jnp.bfloat16
I32 = jnp.int32


def iota(shape, dim):
    return lax.broadcasted_iota(I32, shape, dim)


def flags(mask):
    return jnp.where(mask, 1.0, 0.0).astype(BF16)


def dot(a, b):
    return jnp.dot(a, b, preferred_element_type=F32)


def dot_t(a, b):
    return lax.dot_general(a, b, (((1,), (1,)), ((), ())), preferred_element_type=F32)


def shift_of(room):
    return room.bit_length() - 1


def to_col(row):
    size = row.shape[1]
    eye = iota((size, size), 0) == iota((size, size), 1)
    return jnp.sum(jnp.where(eye, row, 0.0), axis=1, keepdims=True)


def deal(position, owners, turn):
    bits = owners.bit_length() - 1
    level = position >> bits
    spot = position & (owners - 1)
    spot = jnp.where((level & 1) == 1, owners - 1 - spot, spot)
    return (spot + level * (turn * 11)) & (owners - 1), level


def match(room, counts, spot_rows, spot_cols, scr):
    set_scr, flip_scr, move_scr, row_scr, col_scr, first_scr, first_t_scr, state_scr, turned_scr = scr
    owners = counts[0].shape[0]
    shape = (owners, LANES)
    square = (LANES, LANES)
    tall = (CLUSTERS, LANES)
    wide = (owners, CLUSTERS)
    rows, cols, level_rows, level_cols = [], [], [], []
    for h in range(2):
        for spot, at, levels in ((spot_rows, rows, level_rows), (spot_cols, cols, level_cols)):
            chosen, level = deal(spot[h], owners, 0)
            at.append(chosen)
            levels.append(level)
    count_scr = counts[1]
    row_scr[...] = jnp.broadcast_to(spot_rows[1], row_scr.shape)
    col_scr[...] = jnp.broadcast_to(spot_cols[1], col_scr.shape)
    first_t_scr[...] = dot_t(flags(iota(wide, 0) == rows[0]), counts[0][...])
    eye = flags(iota((CLUSTERS, CLUSTERS), 0) == iota((CLUSTERS, CLUSTERS), 1))
    flip_scr[...] = dot_t(eye, counts[1][...]).astype(BF16)
    set_scr[...] = flags(iota(tall, 1) == cols[0])
    first_scr[...] = dot(counts[0][...], set_scr[...])

    def misfits():
        eye = iota(shape, 0) == iota(shape, 1)
        return float(owners) - jnp.sum(jnp.where(eye, state_scr[0:owners, :], 0.0))

    def fits(by_row, by_lane):
        most = jnp.zeros(shape, F32)
        for s in range(owners):
            most = jnp.maximum(most, by_row[:, s : s + 1] + by_lane[s : s + 1, :])
        return jnp.where((most <= float(room)) & (iota(shape, 1) < owners), 1.0, 0.0)

    def trade(step):
        eye = iota(shape, 0) == iota(shape, 1)
        fit = state_scr[0:owners, :]
        pairs = fit * turned_scr[0:owners, :]
        fine = jnp.where(eye, fit, 0.0)
        fine_row = jnp.sum(fine, axis=0, keepdims=True)
        fine_col = jnp.sum(fine, axis=1, keepdims=True)

        def granted(asker, asked, bad, good, axis):
            order = (asker * 37 + asked * 11 + step * 7) & (owners - 1)
            asks = pairs * (1.0 - bad) * good * (order + 1).astype(F32)
            asks = jnp.where(asks == jnp.max(asks, axis=axis, keepdims=True), asks, 0.0)
            asks = jnp.where(asks == jnp.max(asks, axis=1 - axis, keepdims=True), asks, 0.0)
            return jnp.minimum(asks, 1.0)

        both = granted(iota(shape, 0), iota(shape, 1), fine_col, fine_row, 1)
        both += granted(iota(shape, 1), iota(shape, 0), fine_row, fine_col, 0)
        settled = 1.0 - jnp.sum(both, axis=0, keepdims=True)
        move_scr[...] = jnp.where(
            iota(square, 0) == iota(square, 1), settled, 0.0
        ).astype(BF16)
        move_scr[0:owners, :] = (both + jnp.where(eye, settled, 0.0)).astype(BF16)
        state_scr[...] = dot(state_scr[...].astype(BF16), move_scr[...])
        turned_scr[...] = dot(move_scr[...], turned_scr[...].astype(BF16))

    def attempt(carry):
        turn, _ = carry
        at_row, _ = deal(row_scr[0:1, :], owners, turn)
        at_col, _ = deal(col_scr[...], owners, turn)
        set_scr[...] = flags(iota(tall, 1) == at_col)
        second = dot(count_scr[...], set_scr[...])
        second_t = dot(flags(iota(wide, 0) == at_row), flip_scr[...])
        state_scr[...] = iota(square, 1).astype(F32)
        state_scr[0:owners, :] = fits(first_t_scr[...], second)
        turned_scr[...] = jnp.zeros(square, F32)
        turned_scr[0:owners, :] = fits(second_t, first_scr[...])

        def trades(carry):
            step, _ = carry
            trade(step)
            return step + 1, misfits()

        _, left = lax.while_loop(
            lambda c: (c[1] > 0.5) & (c[0] < 6), trades, (jnp.int32(0), misfits())
        )
        return turn + 1, left

    turn, left = lax.while_loop(
        lambda c: (c[1] > 0.5) & (c[0] < 8), attempt, (jnp.int32(0), jnp.float32(1.0))
    )
    label = state_scr[owners : owners + 1, :]
    eye = iota(shape, 0) == iota(shape, 1)
    label_col = jnp.sum(jnp.where(eye, label, 0.0), axis=1, keepdims=True).astype(I32)
    at_row, _ = deal(row_scr[0:1, :], owners, turn - 1)
    at_col, _ = deal(col_scr[...], owners, turn - 1)
    row = jnp.where(label_col == at_row, iota(wide, 0).astype(F32), 0.0)
    rows[1] = jnp.sum(row, axis=0, keepdims=True).astype(I32)
    col = jnp.where(label.astype(I32) == at_col, iota(tall, 1).astype(F32), 0.0)
    cols[1] = jnp.sum(col, axis=1, keepdims=True).astype(I32)
    return rows, cols, level_rows, level_cols, left


def plan_kernel(
    room, all_ref, own_ref, ids_ref, rank_ref, place_ref, rows_ref, cols_ref, first_ref, over_ref, *scratch
):
    owners = all_ref.shape[0]
    owned = CLUSTERS // owners
    heads = ids_ref.shape[0]
    cluster_row = iota((1, CLUSTERS), 1).astype(F32)
    home = flags(iota((owners, CLUSTERS), 1) // owned == iota((owners, CLUSTERS), 0))
    counts, spot_rows, spot_cols = [], [], []
    for h in range(heads):
        count = all_ref[:, h * CLUSTERS : (h + 1) * CLUSTERS]
        total = jnp.sum(count.astype(F32), axis=0, keepdims=True)
        order_row = total * CLUSTERS + (CLUSTERS - 1 - cluster_row)
        order_col = to_col(order_row)
        spot_row = jnp.sum(jnp.where(order_col > order_row, 1.0, 0.0), axis=0, keepdims=True)
        spot_col = jnp.sum(jnp.where(order_row > order_col, 1.0, 0.0), axis=1, keepdims=True)
        counts.append(count)
        spot_rows.append(spot_row.astype(I32))
        spot_cols.append(spot_col.astype(I32))
    for scr, count in zip(scratch[:heads], counts):
        scr[...] = (count.astype(F32) + home.astype(F32)).astype(BF16)
    at_rows, at_cols, level_rows, level_cols, left = match(
        room, scratch[:heads], spot_rows, spot_cols, scratch[heads:]
    )
    over_ref[...] = jnp.full(over_ref.shape, jnp.where(left > 0.5, 1.0, 0.0))

    owns = [jnp.broadcast_to(own_ref[h : h + 1, :], (8, CLUSTERS)).astype(BF16) for h in range(heads)]
    for h in range(heads):
        before = flags((at_cols[h] == at_rows[h]) & (level_cols[h] < level_rows[h]))
        offset = dot(owns[h], before)
        if h == 1:
            offset = offset + dot(owns[0], flags(at_cols[0] == at_rows[1]))
        row_id = iota((8, CLUSTERS), 0)
        table = jnp.where(row_id == 0, at_rows[h].astype(F32), offset).astype(BF16)
        toks = ids_ref.shape[1]
        member = flags(iota((CLUSTERS, toks), 0) == ids_ref[h : h + 1, :])
        found = dot(table, member).astype(I32)
        place_ref[h : h + 1, :] = found[0:1] * room + found[1:2] + rank_ref[h : h + 1, :]

    rows_ref[...] = jnp.concatenate(at_rows + level_rows + [jnp.zeros((4, CLUSTERS), I32)], axis=0)
    column = iota((CLUSTERS, LANES), 1)
    found = jnp.zeros((CLUSTERS, LANES), I32)
    for i, values in enumerate(at_cols + level_cols):
        found = jnp.where(column == i, values, found)
    cols_ref[...] = found
    set_scr = scratch[heads]
    set_scr[...] = flags(at_cols[0] == column)
    first_ref[...] = dot(owns[0], set_scr[...])


def arrive_kernel(
    room,
    me_ref,
    all_ref,
    own_ref,
    rows_ref,
    cols_ref,
    sums_row_ref,
    sums_col_ref,
    query_ref,
    key_ref,
    member_ref,
):
    me = me_ref[0]
    owners = all_ref.shape[0]
    owned = CLUSTERS // owners
    heads = own_ref.shape[0]
    cluster_row = iota((1, CLUSTERS), 1).astype(F32)
    counts = [all_ref[:, h * CLUSTERS : (h + 1) * CLUSTERS] for h in range(heads)]
    owns = [jnp.broadcast_to(own_ref[h : h + 1, :], (8, CLUSTERS)).astype(BF16) for h in range(heads)]
    at_rows = [rows_ref[h : h + 1, :] for h in range(heads)]
    level_rows = [rows_ref[heads + h : heads + h + 1, :] for h in range(heads)]
    at_cols = [cols_ref[:, h : h + 1] for h in range(heads)]
    level_cols = [cols_ref[:, heads + h : heads + h + 1] for h in range(heads)]

    items = heads * owned
    lane = iota((CLUSTERS, LANES), 1)
    item = iota((items, CLUSTERS), 0)
    ends = jnp.zeros((owners, LANES), F32)
    ends_t = jnp.zeros((items, owners), F32)
    id_row = jnp.zeros((1, LANES), F32)
    id_col = jnp.zeros((items, 1), F32)
    for h in range(heads):
        ends += dot(counts[h], flags((at_cols[h] == me) & (level_cols[h] + h * owned <= lane)))
        ends_t += dot_t(flags((at_rows[h] == me) & (level_rows[h] + h * owned <= item)), counts[h])
        hit = (at_cols[h] == me) & (level_cols[h] + h * owned == lane)
        id_row += jnp.sum(jnp.where(hit, iota(lane.shape, 0).astype(F32), 0.0), axis=0, keepdims=True)
        hit = (at_rows[h] == me) & (level_rows[h] + h * owned == item)
        id_col += jnp.sum(jnp.where(hit, cluster_row, 0.0), axis=1, keepdims=True)
    rows = key_ref.shape[0]
    inside = ids_down(room, rows, items, ends)
    query_ref[...] = jnp.where(inside, 0.0, -FAR).astype(BF16)
    key_ref[...] = flags(inside)
    id_along = ids_along(room, rows, ends_t)
    member_ref[...] = flags(iota((items, rows), 0).astype(F32) == id_along)

    back_row = id_row.astype(I32) // owned
    back_col = id_col.astype(I32) // owned
    earlier = (back_col == back_row) & (iota((items, LANES), 0) < iota((items, LANES), 1))
    queue = jnp.sum(jnp.where(earlier, 1.0, 0.0), axis=0, keepdims=True)
    used = jnp.sum(
        jnp.where(iota((owners, LANES), 0) == back_row, ends[:, items - 1 : items], 0.0),
        axis=0,
        keepdims=True,
    )
    row = back_row * room + (queue + used).astype(I32)
    sums_row_ref[...] = jnp.broadcast_to(jnp.where(iota((1, LANES), 1) < items, row, -1), sums_row_ref.shape)

    at_lane = jnp.zeros((1, LANES), F32)
    turn_lane = jnp.zeros((1, LANES), F32)
    at_item = jnp.zeros((items, 1), F32)
    turn_item = jnp.zeros((items, 1), F32)
    sent = jnp.zeros((8, LANES), F32)
    for h in range(heads):
        low = me * owned - h * owned
        hit = (iota(lane.shape, 0) == lane + low) & (lane >= h * owned) & (lane < (h + 1) * owned)
        at_lane += jnp.sum(jnp.where(hit, at_cols[h].astype(F32), 0.0), axis=0, keepdims=True)
        turn_lane += jnp.sum(
            jnp.where(hit, (level_cols[h] + h * owned).astype(F32), 0.0), axis=0, keepdims=True
        )
        hit = (iota(item.shape, 1) == item + low) & (item >= h * owned) & (item < (h + 1) * owned)
        at_item += jnp.sum(jnp.where(hit, at_rows[h].astype(F32), 0.0), axis=1, keepdims=True)
        turn_item += jnp.sum(
            jnp.where(hit, (level_rows[h] + h * owned).astype(F32), 0.0), axis=1, keepdims=True
        )
        sent += dot(owns[h], flags(at_cols[h] == lane))
    small = iota((items, LANES), 1)
    ahead = (at_lane == at_item) & (turn_lane < turn_item) & (small < items)
    queue = jnp.sum(jnp.where(ahead, 1.0, 0.0), axis=1, keepdims=True)
    used = jnp.sum(
        jnp.where(small == at_item.astype(I32), sent[0:1], 0.0), axis=1, keepdims=True
    )
    sums_col_ref[...] = jnp.broadcast_to(
        at_item.astype(I32) * room + (queue + used).astype(I32), sums_col_ref.shape
    )


def make_plan(everyone, own, cluster_ids, rank, room):
    heads, toks = cluster_ids.shape
    owners = everyone.shape[0]
    return pl.pallas_call(
        functools.partial(plan_kernel, room),
        out_shape=(
            jax.ShapeDtypeStruct((heads, toks), I32),
            jax.ShapeDtypeStruct((8, CLUSTERS), I32),
            jax.ShapeDtypeStruct((CLUSTERS, LANES), I32),
            jax.ShapeDtypeStruct((8, LANES), F32),
            jax.ShapeDtypeStruct((8, LANES), F32),
        ),
        scratch_shapes=[
            pltpu.VMEM((owners, CLUSTERS), BF16),
            pltpu.VMEM((owners, CLUSTERS), BF16),
            pltpu.VMEM((CLUSTERS, LANES), BF16),
            pltpu.VMEM((CLUSTERS, owners), BF16),
            pltpu.VMEM((LANES, LANES), BF16),
            pltpu.VMEM((8, CLUSTERS), I32),
            pltpu.VMEM((CLUSTERS, LANES), I32),
            pltpu.VMEM((owners, LANES), F32),
            pltpu.VMEM((owners, owners), F32),
            pltpu.VMEM((LANES, LANES), F32),
            pltpu.VMEM((LANES, LANES), F32),
        ],
        compiler_params=PARAMS,
        cost_estimate=pl.CostEstimate(flops=10**9, bytes_accessed=10**6, transcendentals=0),
    )(everyone, own, cluster_ids, rank)


def arrive(me, everyone, own, rows, cols, room):
    owners = everyone.shape[0]
    items = own.shape[0] * CLUSTERS // owners
    vmem = pl.BlockSpec(memory_space=pltpu.VMEM)
    return pl.pallas_call(
        functools.partial(arrive_kernel, room),
        in_specs=[pl.BlockSpec(memory_space=pltpu.SMEM)] + [vmem] * 4,
        out_specs=[vmem] * 5,
        out_shape=(
            jax.ShapeDtypeStruct((8, LANES), I32),
            jax.ShapeDtypeStruct((items, LANES), I32),
            jax.ShapeDtypeStruct((owners * room, LANES), BF16),
            jax.ShapeDtypeStruct((owners * room, LANES), BF16),
            jax.ShapeDtypeStruct((items, owners * room), BF16),
        ),
        compiler_params=PARAMS,
        cost_estimate=pl.CostEstimate(flops=10**9, bytes_accessed=10**6, transcendentals=0),
    )(me, everyone, own, rows, cols)


def pack_kernel(room, place_ref, first_ref, q_ref, k_ref, v_ref, out_ref):
    rows, toks = out_ref.shape[0], q_ref.shape[0]
    width = out_ref.shape[1] // 3
    base = pl.program_id(0) * rows
    wanted = iota((rows, toks), 0) + base
    pick = flags((wanted == place_ref[0:1, :]) | (wanted == place_ref[1:2, :]))
    place = iota((rows, LANES), 0) + base
    here = (place >> shift_of(room)) == iota((rows, LANES), 1)
    first = jnp.sum(jnp.where(here, first_ref[0:1, :], 0.0), axis=1, keepdims=True)
    is_first = (place[:, 0:1] & (room - 1)).astype(F32) < first
    for part, ref in enumerate((q_ref, k_ref, v_ref)):
        moved = dot(pick, ref[...])
        moved = jnp.where(is_first, moved[:, 0:width], moved[:, width:])
        out_ref[:, part * width : (part + 1) * width] = moved.astype(out_ref.dtype)


def pack(place, first, queries, keys, values, room, owners):
    toks, width = queries.shape
    heads = place.shape[0]
    rows_all = owners * room
    tile = 512
    whole = pl.BlockSpec((toks, width), lambda i: (0, 0))
    return pl.pallas_call(
        functools.partial(pack_kernel, room),
        grid=(rows_all // tile,),
        in_specs=[
            pl.BlockSpec((heads, toks), lambda i: (0, 0)),
            pl.BlockSpec(first.shape, lambda i: (0, 0)),
            whole,
            whole,
            whole,
        ],
        out_specs=pl.BlockSpec((tile, 3 * width // heads), lambda i: (i, 0)),
        out_shape=jax.ShapeDtypeStruct((rows_all, 3 * width // heads), queries.dtype),
        compiler_params=PARAMS,
        cost_estimate=pl.CostEstimate(
            flops=6 * rows_all * toks * width,
            bytes_accessed=rows_all * width * 3,
            transcendentals=0,
        ),
    )(place, first, queries, keys, values)


def ids_along(room, rows, ends_t):
    items, sources = ends_t.shape
    spread = flags((iota((sources, rows), 1) >> shift_of(room)) == iota((sources, rows), 0))
    ends_row = dot(ends_t.astype(BF16), spread)
    slot_row = (iota((items, rows), 1) & (room - 1)).astype(F32)
    return jnp.sum(jnp.where(ends_row <= slot_row, 1.0, 0.0), axis=0, keepdims=True)


def ids_down(room, rows, items, ends):
    sources = ends.shape[0]
    spread = flags((iota((rows, sources), 0) >> shift_of(room)) == iota((rows, sources), 1))
    lane = iota(ends.shape, 1)
    ends = jnp.where(lane < items, ends, float(2 * LANES))
    starts = jnp.where(lane == 0, 0.0, pltpu.roll(ends, 1, 1))
    bounds = dot(spread, jnp.concatenate([starts, ends], axis=1).astype(BF16))
    slot = (iota((rows, LANES), 0) & (room - 1)).astype(F32)
    return (bounds[:, 0:LANES] <= slot) & (slot < bounds[:, LANES:])


def unit_sums(key_rows, member):
    key_float = key_rows.astype(F32)
    unit = key_float * lax.rsqrt(jnp.sum(key_float * key_float, axis=1, keepdims=True) + 1e-06)
    high = unit.astype(BF16)
    low = (unit - high.astype(F32)).astype(BF16)
    return (dot(member, high) + dot(member, low)).astype(BF16)


def fill(query_ref, key_ref, member_ref, x_ref, query_scr, key_scr, value_scr):
    rows, width = x_ref.shape[0], x_ref.shape[1] // 3
    query_scr[:, 0:width] = x_ref[:, 0:width]
    query_scr[:, width:] = query_ref[...]
    key_scr[:, 0:width] = x_ref[:, width : 2 * width]
    key_scr[:, width:] = key_ref[...]
    value_scr[:, 0:width] = x_ref[:, 2 * width : 3 * width]
    value_scr[:, width:] = jnp.ones((rows, LANES), BF16)
    return unit_sums(x_ref[:, width : 2 * width], member_ref[...])


def weigh(pieces, values, width):
    scale = math.log2(math.e) / math.sqrt(width)
    highest = jnp.max(pieces[0], axis=1, keepdims=True)
    for scores in pieces[1:]:
        highest = jnp.maximum(highest, jnp.max(scores, axis=1, keepdims=True))
    result = jnp.zeros((highest.shape[0], width + LANES), F32)
    for scores, value in zip(pieces, values):
        raised = jnp.exp2((scores - highest) * scale)
        result += dot(raised.astype(BF16), value)
    return result[:, 0:width] / result[:, width : width + 1]


def homeward(begin, tile, sums_row_ref, sums):
    pick = flags(iota((tile, LANES), 0) + begin == sums_row_ref[0:1, :])
    return dot(pick[:, 0 : sums.shape[0]], sums)


def attend_kernel(
    query_ref, key_ref, member_ref, sums_row_ref, x_ref, out_ref, query_scr, key_scr, value_scr
):
    rows, width = out_ref.shape
    sums = fill(query_ref, key_ref, member_ref, x_ref, query_scr, key_scr, value_scr)
    for begin in range(0, rows, TILE):
        end = begin + TILE
        query = query_scr[begin:end, :]
        pieces, values = [], []
        if begin:
            pieces.append(dot_t(query, key_scr[0:begin, :]))
            values.append(value_scr[0:begin, :])
        scores = dot_t(query, key_scr[begin:end, :])
        allowed = iota((TILE, TILE), 1) <= iota((TILE, TILE), 0)
        pieces.append(jnp.where(allowed, scores, -FAR))
        values.append(value_scr[begin:end, :])
        result = weigh(pieces, values, width) + homeward(begin, TILE, sums_row_ref, sums)
        out_ref[begin:end] = result.astype(out_ref.dtype)


def attend_tile_kernel(
    query_ref,
    key_ref,
    member_ref,
    sums_row_ref,
    x_ref,
    out_ref,
    query_scr,
    key_scr,
    value_scr,
    sums_scr,
):
    tile, width = out_ref.shape
    rows = x_ref.shape[0]

    @pl.when(pl.program_id(0) == 0)
    def _():
        sums_scr[...] = fill(query_ref, key_ref, member_ref, x_ref, query_scr, key_scr, value_scr)

    begin = pl.multiple_of(pl.program_id(0) * tile, tile)
    scores = dot_t(query_scr[pl.ds(begin, tile), :], key_scr[...])
    allowed = iota((tile, rows), 1) <= iota((tile, rows), 0) + begin
    result = weigh([jnp.where(allowed, scores, -FAR)], [value_scr[...]], width)
    out_ref[...] = (result + homeward(begin, tile, sums_row_ref, sums_scr[...])).astype(out_ref.dtype)


def attend(query_far, key_far, member, sums_row, received):
    rows, width = received.shape[0], received.shape[1] // 3
    shape = jax.ShapeDtypeStruct((rows, width), received.dtype)
    cost = pl.CostEstimate(
        flops=2 * rows * rows * width,
        bytes_accessed=rows * width * 8,
        transcendentals=rows * rows // 2,
    )
    given = (query_far, key_far, member, sums_row, received)
    filled = [pltpu.VMEM((rows, width + LANES), BF16)] * 3
    if rows <= 4096:
        return pl.pallas_call(
            attend_kernel,
            out_shape=shape,
            scratch_shapes=filled,
            compiler_params=PARAMS,
            cost_estimate=cost,
        )(*given)
    tile = 128
    return pl.pallas_call(
        attend_tile_kernel,
        grid=(rows // tile,),
        in_specs=[pl.BlockSpec(x.shape, lambda i: (0, 0)) for x in given],
        out_specs=pl.BlockSpec((tile, width), lambda i: (i, 0)),
        out_shape=shape,
        scratch_shapes=filled + [pltpu.VMEM((member.shape[0], width), BF16)],
        compiler_params=PARAMS,
        cost_estimate=cost,
    )(*given)


def unpack_kernel(place_ref, sums_col_ref, over_ref, back_ref, out_ref, sums_ref):
    toks, heads = place_ref.shape
    rows, width = back_ref.shape
    groups = out_ref.shape[0]
    share = toks // groups
    back = back_ref[...]
    for h in range(heads):
        pick = flags(iota((toks, rows), 1) == place_ref[:, h : h + 1])
        moved = dot(pick, back).astype(out_ref.dtype)
        for g in range(groups):
            out_ref[g, 0:share, h * width : (h + 1) * width] = moved[g * share : (g + 1) * share]
    spare = out_ref.shape[1] - share
    for g in range(groups):
        out_ref[g, share:, :] = jnp.broadcast_to(
            over_ref[0:1, 0:1], (spare, out_ref.shape[2])
        ).astype(out_ref.dtype)

    @pl.when(pl.program_id(0) == 0)
    def _():
        items = sums_col_ref.shape[0]
        pick = flags(iota((items, rows), 1) == sums_col_ref[:, 0:1])
        sums_ref[...] = dot(pick, back)


def unpack(place, sums_col, over, back, groups):
    (toks, heads), (rows, width) = place.shape, back.shape
    share = toks // groups
    items = sums_col.shape[0]
    steps = max(1, min(groups, groups * rows // 8192))
    whole = lambda i: (0, 0)
    return pl.pallas_call(
        unpack_kernel,
        grid=(steps,),
        in_specs=[
            pl.BlockSpec((toks // steps, heads), lambda i: (i, 0)),
            pl.BlockSpec(sums_col.shape, whole),
            pl.BlockSpec(over.shape, whole),
            pl.BlockSpec((rows, width), whole),
        ],
        out_specs=(
            pl.BlockSpec((groups // steps, share + 16, heads * width), lambda i: (i, 0, 0)),
            pl.BlockSpec((items, width), whole),
        ),
        out_shape=(
            jax.ShapeDtypeStruct((groups, share + 16, heads * width), back.dtype),
            jax.ShapeDtypeStruct((items, width), F32),
        ),
        compiler_params=PARAMS,
        cost_estimate=pl.CostEstimate(
            flops=2 * rows * toks * width * heads,
            bytes_accessed=rows * width * 2,
            transcendentals=0,
        ),
    )(place, sums_col, over, back)


def exchange(rows, axis):
    return lax.all_to_all(rows, axis, split_axis=0, concat_axis=0, tiled=True)


def routed(room, queries, keys, values, cluster_ids, rank, own, everyone):
    heads = cluster_ids.shape[0]
    owners = everyone.shape[0]
    me = lax.axis_index("seq").astype(I32)[None]
    place, rows, cols, first, over = make_plan(everyone, own, cluster_ids, rank, room)
    received = exchange(pack(place, first, queries, keys, values, room, owners), "seq")
    sums_row, sums_col, query_far, key_far, member = arrive(me, everyone, own, rows, cols, room)
    back = exchange(attend(query_far, key_far, member, sums_row, received), "seq")
    share, sums = unpack(place.T, sums_col, over, back, lax.axis_size("head"))
    parts = exchange(share, "head")
    owned = CLUSTERS // owners
    sums = jnp.concatenate([sums[h * owned : (h + 1) * owned] for h in range(heads)], axis=1)
    return parts, sums


def project(parts, weight):
    toks = parts.shape[1] - 16
    weight = weight.reshape(parts.shape[0], parts.shape[2], weight.shape[1])
    total = jnp.einsum("gtd,gdn->tn", parts[:, :toks], weight, preferred_element_type=F32)
    return total.astype(BF16)


def body(queries, keys, values, cluster_ids, out_weight):
    heads, toks = cluster_ids.shape
    owners = lax.axis_size("seq")
    clusters = jnp.arange(CLUSTERS, dtype=I32)
    own = jnp.sum((cluster_ids[:, None, :] == clusters[None, :, None]).astype(F32), axis=2)
    told = jnp.broadcast_to(own.astype(BF16).reshape(1, 8, LANES), (owners, 8, LANES))
    everyone = exchange(told, "seq").reshape(owners, heads * CLUSTERS)
    full_weight = lax.all_gather(out_weight, "head", axis=0, tiled=True)

    spot = jnp.arange(toks, dtype=I32)
    same = cluster_ids[:, :, None] == cluster_ids[:, None, :]
    rank = jnp.sum((same & (spot[:, None] < spot[None, :])[None]).astype(I32), axis=1)
    given = (queries, keys, values, cluster_ids, rank, own, everyone)
    parts, key_sums = routed(ROOM, *given)
    full_room = 1 << (heads * CLUSTERS // owners * (MOST + 1) - 1).bit_length()

    def again():
        wide, wide_sums = routed(full_room, *given)
        return project(wide, full_weight), wide_sums

    def done():
        return project(parts, full_weight), key_sums

    return lax.cond(jnp.max(parts[:, -1, 0].astype(F32)) > 0.5, again, done)


def solution(mesh):
    placed = (
        P("seq", "head"),
        P("seq", "head"),
        P("seq", "head"),
        P("head", "seq"),
        P("head", None),
    )
    return jax.shard_map(
        body,
        mesh=mesh,
        in_specs=placed,
        out_specs=(P(("seq", "head"), None), P("seq", "head")),
        check_vma=False,
    )
```

```python
import functools
import math

import jax
import jax.numpy as jnp
from jax import lax
from jax.experimental import pallas as pl
from jax.experimental.pallas import tpu as pltpu
from jax.sharding import PartitionSpec as P

CLUSTERS = 512
MOST = 5
ROOM = 32
TILE = 256
FAR = 2.0**100
LANES = 128
PARAMS = pltpu.CompilerParams(vmem_limit_bytes=40 * 1024 * 1024)
F32 = jnp.float32
BF16 = jnp.bfloat16
I32 = jnp.int32


def iota(shape, dim):
    return lax.broadcasted_iota(I32, shape, dim)


def flags(mask):
    return jnp.where(mask, 1.0, 0.0).astype(BF16)


def dot(a, b):
    return jnp.dot(a, b, preferred_element_type=F32)


def dot_t(a, b):
    return lax.dot_general(a, b, (((1,), (1,)), ((), ())), preferred_element_type=F32)


def shift_of(room):
    return room.bit_length() - 1


def to_col(row):
    size = row.shape[1]
    eye = iota((size, size), 0) == iota((size, size), 1)
    return jnp.sum(jnp.where(eye, row, 0.0), axis=1, keepdims=True)


def deal(position, owners, turn):
    bits = owners.bit_length() - 1
    level = position >> bits
    spot = position & (owners - 1)
    spot = jnp.where((level & 1) == 1, owners - 1 - spot, spot)
    return (spot + level * (turn * 11)) & (owners - 1), level


def match(room, counts, spot_rows, spot_cols, scr):
    set_scr, flip_scr, move_scr, row_scr, col_scr, first_scr, first_t_scr, state_scr, turned_scr = scr
    owners = counts[0].shape[0]
    shape = (owners, LANES)
    square = (LANES, LANES)
    tall = (CLUSTERS, LANES)
    wide = (owners, CLUSTERS)
    rows, cols, level_rows, level_cols = [], [], [], []
    for h in range(2):
        for spot, at, levels in ((spot_rows, rows, level_rows), (spot_cols, cols, level_cols)):
            chosen, level = deal(spot[h], owners, 0)
            at.append(chosen)
            levels.append(level)
    count_scr = counts[1]
    row_scr[...] = jnp.broadcast_to(spot_rows[1], row_scr.shape)
    col_scr[...] = jnp.broadcast_to(spot_cols[1], col_scr.shape)
    first_t_scr[...] = dot_t(flags(iota(wide, 0) == rows[0]), counts[0][...])
    eye = flags(iota((CLUSTERS, CLUSTERS), 0) == iota((CLUSTERS, CLUSTERS), 1))
    flip_scr[...] = dot_t(eye, counts[1][...]).astype(BF16)
    set_scr[...] = flags(iota(tall, 1) == cols[0])
    first_scr[...] = dot(counts[0][...], set_scr[...])

    def misfits():
        eye = iota(shape, 0) == iota(shape, 1)
        return float(owners) - jnp.sum(jnp.where(eye, state_scr[0:owners, :], 0.0))

    def fits(by_row, by_lane):
        most = jnp.zeros(shape, F32)
        for s in range(owners):
            most = jnp.maximum(most, by_row[:, s : s + 1] + by_lane[s : s + 1, :])
        return jnp.where((most <= float(room)) & (iota(shape, 1) < owners), 1.0, 0.0)

    def trade(step):
        eye = iota(shape, 0) == iota(shape, 1)
        fit = state_scr[0:owners, :]
        pairs = fit * turned_scr[0:owners, :]
        fine = jnp.where(eye, fit, 0.0)
        fine_row = jnp.sum(fine, axis=0, keepdims=True)
        fine_col = jnp.sum(fine, axis=1, keepdims=True)

        def granted(asker, asked, bad, good, axis):
            order = (asker * 37 + asked * 11 + step * 7) & (owners - 1)
            asks = pairs * (1.0 - bad) * good * (order + 1).astype(F32)
            asks = jnp.where(asks == jnp.max(asks, axis=axis, keepdims=True), asks, 0.0)
            asks = jnp.where(asks == jnp.max(asks, axis=1 - axis, keepdims=True), asks, 0.0)
            return jnp.minimum(asks, 1.0)

        both = granted(iota(shape, 0), iota(shape, 1), fine_col, fine_row, 1)
        both += granted(iota(shape, 1), iota(shape, 0), fine_row, fine_col, 0)
        settled = 1.0 - jnp.sum(both, axis=0, keepdims=True)
        move_scr[...] = jnp.where(
            iota(square, 0) == iota(square, 1), settled, 0.0
        ).astype(BF16)
        move_scr[0:owners, :] = (both + jnp.where(eye, settled, 0.0)).astype(BF16)
        state_scr[...] = dot(state_scr[...].astype(BF16), move_scr[...])
        turned_scr[...] = dot(move_scr[...], turned_scr[...].astype(BF16))

    def attempt(carry):
        turn, _ = carry
        at_row, _ = deal(row_scr[0:1, :], owners, turn)
        at_col, _ = deal(col_scr[...], owners, turn)
        set_scr[...] = flags(iota(tall, 1) == at_col)
        second = dot(count_scr[...], set_scr[...])
        second_t = dot(flags(iota(wide, 0) == at_row), flip_scr[...])
        state_scr[...] = iota(square, 1).astype(F32)
        state_scr[0:owners, :] = fits(first_t_scr[...], second)
        turned_scr[...] = jnp.zeros(square, F32)
        turned_scr[0:owners, :] = fits(second_t, first_scr[...])

        def trades(carry):
            step, _ = carry
            trade(step)
            return step + 1, misfits()

        _, left = lax.while_loop(
            lambda c: (c[1] > 0.5) & (c[0] < 6), trades, (jnp.int32(0), misfits())
        )
        return turn + 1, left

    turn, left = lax.while_loop(
        lambda c: (c[1] > 0.5) & (c[0] < 8), attempt, (jnp.int32(0), jnp.float32(1.0))
    )
    label = state_scr[owners : owners + 1, :]
    eye = iota(shape, 0) == iota(shape, 1)
    label_col = jnp.sum(jnp.where(eye, label, 0.0), axis=1, keepdims=True).astype(I32)
    at_row, _ = deal(row_scr[0:1, :], owners, turn - 1)
    at_col, _ = deal(col_scr[...], owners, turn - 1)
    row = jnp.where(label_col == at_row, iota(wide, 0).astype(F32), 0.0)
    rows[1] = jnp.sum(row, axis=0, keepdims=True).astype(I32)
    col = jnp.where(label.astype(I32) == at_col, iota(tall, 1).astype(F32), 0.0)
    cols[1] = jnp.sum(col, axis=1, keepdims=True).astype(I32)
    return rows, cols, level_rows, level_cols, left


def plan_kernel(
    room, all_ref, own_ref, ids_ref, rank_ref, place_ref, rows_ref, cols_ref, first_ref, over_ref, *scratch
):
    owners = all_ref.shape[0]
    owned = CLUSTERS // owners
    heads = ids_ref.shape[0]
    cluster_row = iota((1, CLUSTERS), 1).astype(F32)
    home = flags(iota((owners, CLUSTERS), 1) // owned == iota((owners, CLUSTERS), 0))
    counts, spot_rows, spot_cols = [], [], []
    for h in range(heads):
        count = all_ref[:, h * CLUSTERS : (h + 1) * CLUSTERS]
        total = jnp.sum(count.astype(F32), axis=0, keepdims=True)
        order_row = total * CLUSTERS + (CLUSTERS - 1 - cluster_row)
        order_col = to_col(order_row)
        spot_row = jnp.sum(jnp.where(order_col > order_row, 1.0, 0.0), axis=0, keepdims=True)
        spot_col = jnp.sum(jnp.where(order_row > order_col, 1.0, 0.0), axis=1, keepdims=True)
        counts.append(count)
        spot_rows.append(spot_row.astype(I32))
        spot_cols.append(spot_col.astype(I32))
    for scr, count in zip(scratch[:heads], counts):
        scr[...] = (count.astype(F32) + home.astype(F32)).astype(BF16)
    at_rows, at_cols, level_rows, level_cols, left = match(
        room, scratch[:heads], spot_rows, spot_cols, scratch[heads:]
    )
    over_ref[...] = jnp.full(over_ref.shape, jnp.where(left > 0.5, 1.0, 0.0))

    owns = [jnp.broadcast_to(own_ref[h : h + 1, :], (8, CLUSTERS)).astype(BF16) for h in range(heads)]
    for h in range(heads):
        before = flags((at_cols[h] == at_rows[h]) & (level_cols[h] < level_rows[h]))
        offset = dot(owns[h], before)
        if h == 1:
            offset = offset + dot(owns[0], flags(at_cols[0] == at_rows[1]))
        row_id = iota((8, CLUSTERS), 0)
        table = jnp.where(row_id == 0, at_rows[h].astype(F32), offset).astype(BF16)
        toks = ids_ref.shape[1]
        member = flags(iota((CLUSTERS, toks), 0) == ids_ref[h : h + 1, :])
        found = dot(table, member).astype(I32)
        place_ref[h : h + 1, :] = found[0:1] * room + found[1:2] + rank_ref[h : h + 1, :]

    rows_ref[...] = jnp.concatenate(at_rows + level_rows + [jnp.zeros((4, CLUSTERS), I32)], axis=0)
    column = iota((CLUSTERS, LANES), 1)
    found = jnp.zeros((CLUSTERS, LANES), I32)
    for i, values in enumerate(at_cols + level_cols):
        found = jnp.where(column == i, values, found)
    cols_ref[...] = found
    set_scr = scratch[heads]
    set_scr[...] = flags(at_cols[0] == column)
    first_ref[...] = dot(owns[0], set_scr[...])


def arrive_kernel(
    room,
    me_ref,
    all_ref,
    own_ref,
    rows_ref,
    cols_ref,
    sums_row_ref,
    sums_col_ref,
    query_ref,
    key_ref,
    member_ref,
):
    me = me_ref[0]
    owners = all_ref.shape[0]
    owned = CLUSTERS // owners
    heads = own_ref.shape[0]
    cluster_row = iota((1, CLUSTERS), 1).astype(F32)
    counts = [all_ref[:, h * CLUSTERS : (h + 1) * CLUSTERS] for h in range(heads)]
    owns = [jnp.broadcast_to(own_ref[h : h + 1, :], (8, CLUSTERS)).astype(BF16) for h in range(heads)]
    at_rows = [rows_ref[h : h + 1, :] for h in range(heads)]
    level_rows = [rows_ref[heads + h : heads + h + 1, :] for h in range(heads)]
    at_cols = [cols_ref[:, h : h + 1] for h in range(heads)]
    level_cols = [cols_ref[:, heads + h : heads + h + 1] for h in range(heads)]

    items = heads * owned
    lane = iota((CLUSTERS, LANES), 1)
    item = iota((items, CLUSTERS), 0)
    ends = jnp.zeros((owners, LANES), F32)
    ends_t = jnp.zeros((items, owners), F32)
    id_row = jnp.zeros((1, LANES), F32)
    id_col = jnp.zeros((items, 1), F32)
    for h in range(heads):
        ends += dot(counts[h], flags((at_cols[h] == me) & (level_cols[h] + h * owned <= lane)))
        ends_t += dot_t(flags((at_rows[h] == me) & (level_rows[h] + h * owned <= item)), counts[h])
        hit = (at_cols[h] == me) & (level_cols[h] + h * owned == lane)
        id_row += jnp.sum(jnp.where(hit, iota(lane.shape, 0).astype(F32), 0.0), axis=0, keepdims=True)
        hit = (at_rows[h] == me) & (level_rows[h] + h * owned == item)
        id_col += jnp.sum(jnp.where(hit, cluster_row, 0.0), axis=1, keepdims=True)
    rows = key_ref.shape[0]
    inside = ids_down(room, rows, items, ends)
    query_ref[...] = jnp.where(inside, 0.0, -FAR).astype(BF16)
    key_ref[...] = flags(inside)
    id_along = ids_along(room, rows, ends_t)
    member_ref[...] = flags(iota((items, rows), 0).astype(F32) == id_along)

    back_row = id_row.astype(I32) // owned
    back_col = id_col.astype(I32) // owned
    earlier = (back_col == back_row) & (iota((items, LANES), 0) < iota((items, LANES), 1))
    queue = jnp.sum(jnp.where(earlier, 1.0, 0.0), axis=0, keepdims=True)
    used = jnp.sum(
        jnp.where(iota((owners, LANES), 0) == back_row, ends[:, items - 1 : items], 0.0),
        axis=0,
        keepdims=True,
    )
    row = back_row * room + (queue + used).astype(I32)
    sums_row_ref[...] = jnp.broadcast_to(jnp.where(iota((1, LANES), 1) < items, row, -1), sums_row_ref.shape)

    at_lane = jnp.zeros((1, LANES), F32)
    turn_lane = jnp.zeros((1, LANES), F32)
    at_item = jnp.zeros((items, 1), F32)
    turn_item = jnp.zeros((items, 1), F32)
    sent = jnp.zeros((8, LANES), F32)
    for h in range(heads):
        low = me * owned - h * owned
        hit = (iota(lane.shape, 0) == lane + low) & (lane >= h * owned) & (lane < (h + 1) * owned)
        at_lane += jnp.sum(jnp.where(hit, at_cols[h].astype(F32), 0.0), axis=0, keepdims=True)
        turn_lane += jnp.sum(
            jnp.where(hit, (level_cols[h] + h * owned).astype(F32), 0.0), axis=0, keepdims=True
        )
        hit = (iota(item.shape, 1) == item + low) & (item >= h * owned) & (item < (h + 1) * owned)
        at_item += jnp.sum(jnp.where(hit, at_rows[h].astype(F32), 0.0), axis=1, keepdims=True)
        turn_item += jnp.sum(
            jnp.where(hit, (level_rows[h] + h * owned).astype(F32), 0.0), axis=1, keepdims=True
        )
        sent += dot(owns[h], flags(at_cols[h] == lane))
    small = iota((items, LANES), 1)
    ahead = (at_lane == at_item) & (turn_lane < turn_item) & (small < items)
    queue = jnp.sum(jnp.where(ahead, 1.0, 0.0), axis=1, keepdims=True)
    used = jnp.sum(
        jnp.where(small == at_item.astype(I32), sent[0:1], 0.0), axis=1, keepdims=True
    )
    sums_col_ref[...] = jnp.broadcast_to(
        at_item.astype(I32) * room + (queue + used).astype(I32), sums_col_ref.shape
    )


def make_plan(everyone, own, cluster_ids, rank, room):
    heads, toks = cluster_ids.shape
    owners = everyone.shape[0]
    return pl.pallas_call(
        functools.partial(plan_kernel, room),
        out_shape=(
            jax.ShapeDtypeStruct((heads, toks), I32),
            jax.ShapeDtypeStruct((8, CLUSTERS), I32),
            jax.ShapeDtypeStruct((CLUSTERS, LANES), I32),
            jax.ShapeDtypeStruct((8, LANES), F32),
            jax.ShapeDtypeStruct((8, LANES), F32),
        ),
        scratch_shapes=[
            pltpu.VMEM((owners, CLUSTERS), BF16),
            pltpu.VMEM((owners, CLUSTERS), BF16),
            pltpu.VMEM((CLUSTERS, LANES), BF16),
            pltpu.VMEM((CLUSTERS, owners), BF16),
            pltpu.VMEM((LANES, LANES), BF16),
            pltpu.VMEM((8, CLUSTERS), I32),
            pltpu.VMEM((CLUSTERS, LANES), I32),
            pltpu.VMEM((owners, LANES), F32),
            pltpu.VMEM((owners, owners), F32),
            pltpu.VMEM((LANES, LANES), F32),
            pltpu.VMEM((LANES, LANES), F32),
        ],
        compiler_params=PARAMS,
        cost_estimate=pl.CostEstimate(flops=10**9, bytes_accessed=10**6, transcendentals=0),
    )(everyone, own, cluster_ids, rank)


def arrive(me, everyone, own, rows, cols, room):
    owners = everyone.shape[0]
    items = own.shape[0] * CLUSTERS // owners
    vmem = pl.BlockSpec(memory_space=pltpu.VMEM)
    return pl.pallas_call(
        functools.partial(arrive_kernel, room),
        in_specs=[pl.BlockSpec(memory_space=pltpu.SMEM)] + [vmem] * 4,
        out_specs=[vmem] * 5,
        out_shape=(
            jax.ShapeDtypeStruct((8, LANES), I32),
            jax.ShapeDtypeStruct((items, LANES), I32),
            jax.ShapeDtypeStruct((owners * room, LANES), BF16),
            jax.ShapeDtypeStruct((owners * room, LANES), BF16),
            jax.ShapeDtypeStruct((items, owners * room), BF16),
        ),
        compiler_params=PARAMS,
        cost_estimate=pl.CostEstimate(flops=10**9, bytes_accessed=10**6, transcendentals=0),
    )(me, everyone, own, rows, cols)


def of_first(room, rows, base, first_ref):
    place = iota((rows, LANES), 0) + base
    here = (place >> shift_of(room)) == iota((rows, LANES), 1)
    first = jnp.sum(jnp.where(here, first_ref[0:1, :], 0.0), axis=1, keepdims=True)
    return (place[:, 0:1] & (room - 1)).astype(F32) < first


def pack_kernel(room, place_ref, first_ref, q_ref, k_ref, v_ref, out_ref):
    rows, toks = out_ref.shape[0], q_ref.shape[0]
    width = out_ref.shape[1] // 3
    base = pl.program_id(0) * rows
    wanted = iota((rows, toks), 0) + base
    pick = flags((wanted == place_ref[0:1, :]) | (wanted == place_ref[1:2, :]))
    is_first = of_first(room, rows, base, first_ref)
    for part, ref in enumerate((q_ref, k_ref, v_ref)):
        moved = dot(pick, ref[...])
        moved = jnp.where(is_first, moved[:, 0:width], moved[:, width:])
        out_ref[:, part * width : (part + 1) * width] = moved.astype(out_ref.dtype)


def pack(place, first, queries, keys, values, room, owners):
    toks, width = queries.shape
    heads = place.shape[0]
    rows_all = owners * room
    tile = 512
    whole = pl.BlockSpec((toks, width), lambda i: (0, 0))
    return pl.pallas_call(
        functools.partial(pack_kernel, room),
        grid=(rows_all // tile,),
        in_specs=[
            pl.BlockSpec((heads, toks), lambda i: (0, 0)),
            pl.BlockSpec(first.shape, lambda i: (0, 0)),
            whole,
            whole,
            whole,
        ],
        out_specs=pl.BlockSpec((tile, 3 * width // heads), lambda i: (i, 0)),
        out_shape=jax.ShapeDtypeStruct((rows_all, 3 * width // heads), queries.dtype),
        compiler_params=PARAMS,
        cost_estimate=pl.CostEstimate(
            flops=6 * rows_all * toks * width,
            bytes_accessed=rows_all * width * 3,
            transcendentals=0,
        ),
    )(place, first, queries, keys, values)


def ids_along(room, rows, ends_t):
    items, sources = ends_t.shape
    spread = flags((iota((sources, rows), 1) >> shift_of(room)) == iota((sources, rows), 0))
    ends_row = dot(ends_t.astype(BF16), spread)
    slot_row = (iota((items, rows), 1) & (room - 1)).astype(F32)
    return jnp.sum(jnp.where(ends_row <= slot_row, 1.0, 0.0), axis=0, keepdims=True)


def ids_down(room, rows, items, ends):
    sources = ends.shape[0]
    spread = flags((iota((rows, sources), 0) >> shift_of(room)) == iota((rows, sources), 1))
    lane = iota(ends.shape, 1)
    ends = jnp.where(lane < items, ends, float(2 * LANES))
    starts = jnp.where(lane == 0, 0.0, pltpu.roll(ends, 1, 1))
    bounds = dot(spread, jnp.concatenate([starts, ends], axis=1).astype(BF16))
    slot = (iota((rows, LANES), 0) & (room - 1)).astype(F32)
    return (bounds[:, 0:LANES] <= slot) & (slot < bounds[:, LANES:])


def unit_sums(key_rows, member):
    key_float = key_rows.astype(F32)
    unit = key_float * lax.rsqrt(jnp.sum(key_float * key_float, axis=1, keepdims=True) + 1e-06)
    high = unit.astype(BF16)
    low = (unit - high.astype(F32)).astype(BF16)
    return (dot(member, high) + dot(member, low)).astype(BF16)


def fill(query_ref, key_ref, member_ref, x_ref, query_scr, key_scr, value_scr):
    rows, width = x_ref.shape[0], x_ref.shape[1] // 3
    query_scr[:, 0:width] = x_ref[:, 0:width]
    query_scr[:, width:] = query_ref[...]
    key_scr[:, 0:width] = x_ref[:, width : 2 * width]
    key_scr[:, width:] = key_ref[...]
    value_scr[:, 0:width] = x_ref[:, 2 * width : 3 * width]
    value_scr[:, width:] = jnp.ones((rows, LANES), BF16)
    return unit_sums(x_ref[:, width : 2 * width], member_ref[...])


def weigh(pieces, values, width):
    scale = math.log2(math.e) / math.sqrt(width)
    highest = jnp.max(pieces[0], axis=1, keepdims=True)
    for scores in pieces[1:]:
        highest = jnp.maximum(highest, jnp.max(scores, axis=1, keepdims=True))
    result = jnp.zeros((highest.shape[0], width + LANES), F32)
    for scores, value in zip(pieces, values):
        raised = jnp.exp2((scores - highest) * scale)
        result += dot(raised.astype(BF16), value)
    return result[:, 0:width] / result[:, width : width + 1]


def homeward(begin, tile, sums_row_ref, sums):
    pick = flags(iota((tile, LANES), 0) + begin == sums_row_ref[0:1, :])
    return dot(pick[:, 0 : sums.shape[0]], sums)


def attend_kernel(
    query_ref, key_ref, member_ref, sums_row_ref, x_ref, out_ref, query_scr, key_scr, value_scr
):
    rows, width = out_ref.shape
    sums = fill(query_ref, key_ref, member_ref, x_ref, query_scr, key_scr, value_scr)

    def scores_of(begin):
        end = begin + TILE
        query = query_scr[begin:end, :]
        pieces = [dot_t(query, key_scr[0:begin, :])] if begin else []
        scores = dot_t(query, key_scr[begin:end, :])
        allowed = iota((TILE, TILE), 1) <= iota((TILE, TILE), 0)
        return pieces + [jnp.where(allowed, scores, -FAR)]

    ahead = scores_of(0)
    for begin in range(0, rows, TILE):
        end = begin + TILE
        pieces = ahead
        ahead = scores_of(end) if end < rows else None
        values = [value_scr[0:begin, :]] if begin else []
        values.append(value_scr[begin:end, :])
        result = weigh(pieces, values, width) + homeward(begin, TILE, sums_row_ref, sums)
        out_ref[begin:end] = result.astype(out_ref.dtype)


def attend_tile_kernel(
    query_ref,
    key_ref,
    member_ref,
    sums_row_ref,
    x_ref,
    out_ref,
    query_scr,
    key_scr,
    value_scr,
    sums_scr,
):
    tile, width = out_ref.shape
    rows = x_ref.shape[0]

    @pl.when(pl.program_id(0) == 0)
    def _():
        sums_scr[...] = fill(query_ref, key_ref, member_ref, x_ref, query_scr, key_scr, value_scr)

    begin = pl.multiple_of(pl.program_id(0) * tile, tile)
    scores = dot_t(query_scr[pl.ds(begin, tile), :], key_scr[...])
    allowed = iota((tile, rows), 1) <= iota((tile, rows), 0) + begin
    result = weigh([jnp.where(allowed, scores, -FAR)], [value_scr[...]], width)
    out_ref[...] = (result + homeward(begin, tile, sums_row_ref, sums_scr[...])).astype(out_ref.dtype)


def attend(query_far, key_far, member, sums_row, received):
    rows, width = received.shape[0], received.shape[1] // 3
    shape = jax.ShapeDtypeStruct((rows, width), received.dtype)
    cost = pl.CostEstimate(
        flops=2 * rows * rows * width,
        bytes_accessed=rows * width * 8,
        transcendentals=rows * rows // 2,
    )
    given = (query_far, key_far, member, sums_row, received)
    filled = [pltpu.VMEM((rows, width + LANES), BF16)] * 3
    if rows <= 4096:
        return pl.pallas_call(
            attend_kernel,
            out_shape=shape,
            scratch_shapes=filled,
            compiler_params=PARAMS,
            cost_estimate=cost,
        )(*given)
    tile = 128
    return pl.pallas_call(
        attend_tile_kernel,
        grid=(rows // tile,),
        in_specs=[pl.BlockSpec(x.shape, lambda i: (0, 0)) for x in given],
        out_specs=pl.BlockSpec((tile, width), lambda i: (i, 0)),
        out_shape=shape,
        scratch_shapes=filled + [pltpu.VMEM((member.shape[0], width), BF16)],
        compiler_params=PARAMS,
        cost_estimate=cost,
    )(*given)


def unpack_kernel(
    room, place_ref, sums_col_ref, first_ref, over_ref, back_ref, out_ref, sums_ref, pair_scr
):
    toks, heads = place_ref.shape
    rows, width = back_ref.shape
    groups, share, _ = out_ref.shape

    @pl.when(pl.program_id(0) == 0)
    def _():
        back = back_ref[...]
        is_first = of_first(room, rows, 0, first_ref)
        pair_scr[:, 0:width] = jnp.where(is_first, back.astype(F32), 0.0).astype(BF16)
        pair_scr[:, width:] = jnp.where(is_first, 0.0, back.astype(F32)).astype(BF16)
        items = sums_col_ref.shape[0]
        pick = flags(iota((items, rows), 1) == sums_col_ref[:, 0:1])
        sums_ref[...] = dot(pick, back)

    wanted = iota((toks, rows), 1)
    pick = flags((wanted == place_ref[:, 0:1]) | (wanted == place_ref[:, 1:2]))
    moved = dot(pick, pair_scr[...])
    moved = jnp.where(over_ref[0:1, 0:1] > 0.5, jnp.nan, moved).astype(out_ref.dtype)
    for g in range(groups):
        out_ref[g] = moved[g * share : (g + 1) * share]


def unpack(place, sums_col, first, over, back, groups, room):
    (toks, heads), (rows, width) = place.shape, back.shape
    share = toks // groups
    items = sums_col.shape[0]
    steps = max(1, min(groups, groups * rows // 8192))
    whole = lambda i: (0, 0)
    return pl.pallas_call(
        functools.partial(unpack_kernel, room),
        grid=(steps,),
        in_specs=[
            pl.BlockSpec((toks // steps, heads), lambda i: (i, 0)),
            pl.BlockSpec(sums_col.shape, whole),
            pl.BlockSpec(first.shape, whole),
            pl.BlockSpec(over.shape, whole),
            pl.BlockSpec((rows, width), whole),
        ],
        out_specs=(
            pl.BlockSpec((groups // steps, share, heads * width), lambda i: (i, 0, 0)),
            pl.BlockSpec((items, width), whole),
        ),
        out_shape=(
            jax.ShapeDtypeStruct((groups, share, heads * width), back.dtype),
            jax.ShapeDtypeStruct((items, width), F32),
        ),
        scratch_shapes=[pltpu.VMEM((rows, heads * width), BF16)],
        compiler_params=PARAMS,
        cost_estimate=pl.CostEstimate(
            flops=2 * rows * toks * width * heads,
            bytes_accessed=rows * width * 2,
            transcendentals=0,
        ),
    )(place, sums_col, first, over, back)


def exchange(rows, axis):
    return lax.all_to_all(rows, axis, split_axis=0, concat_axis=0, tiled=True)


def routed(room, queries, keys, values, cluster_ids, rank, own, everyone):
    heads = cluster_ids.shape[0]
    owners = everyone.shape[0]
    me = lax.axis_index("seq").astype(I32)[None]
    place, rows, cols, first, over = make_plan(everyone, own, cluster_ids, rank, room)
    received = exchange(pack(place, first, queries, keys, values, room, owners), "seq")
    sums_row, sums_col, query_far, key_far, member = arrive(me, everyone, own, rows, cols, room)
    back = exchange(attend(query_far, key_far, member, sums_row, received), "seq")
    share, sums = unpack(place.T, sums_col, first, over, back, lax.axis_size("head"), room)
    parts = exchange(share, "head")
    owned = CLUSTERS // owners
    sums = jnp.concatenate([sums[h * owned : (h + 1) * owned] for h in range(heads)], axis=1)
    return parts, sums


def project(parts, weight):
    weight = weight.reshape(parts.shape[0], parts.shape[2], weight.shape[1])
    total = jnp.einsum("gtd,gdn->tn", parts, weight, preferred_element_type=F32)
    return total.astype(BF16)


def body(queries, keys, values, cluster_ids, out_weight):
    heads, toks = cluster_ids.shape
    owners = lax.axis_size("seq")
    clusters = jnp.arange(CLUSTERS, dtype=I32)
    own = jnp.sum((cluster_ids[:, None, :] == clusters[None, :, None]).astype(F32), axis=2)
    told = jnp.broadcast_to(own.astype(BF16).reshape(1, 8, LANES), (owners, 8, LANES))
    everyone = exchange(told, "seq").reshape(owners, heads * CLUSTERS)
    full_weight = lax.all_gather(out_weight, "head", axis=0, tiled=True)

    spot = jnp.arange(toks, dtype=I32)
    same = cluster_ids[:, :, None] == cluster_ids[:, None, :]
    rank = jnp.sum((same & (spot[:, None] < spot[None, :])[None]).astype(I32), axis=1)
    given = (queries, keys, values, cluster_ids, rank, own, everyone)
    parts, key_sums = routed(ROOM, *given)
    full_room = 1 << (heads * CLUSTERS // owners * (MOST + 1) - 1).bit_length()

    def again():
        wide, wide_sums = routed(full_room, *given)
        return project(wide, full_weight), wide_sums

    def done():
        return project(parts, full_weight), key_sums

    return lax.cond(jnp.any(jnp.isnan(parts[:, 0, 0])), again, done)


def solution(mesh):
    placed = (
        P("seq", "head"),
        P("seq", "head"),
        P("seq", "head"),
        P("head", "seq"),
        P("head", None),
    )
    return jax.shard_map(
        body,
        mesh=mesh,
        in_specs=placed,
        out_specs=(P(("seq", "head"), None), P("seq", "head")),
        check_vma=False,
    )
```

```python
import functools
import math

import jax
import jax.numpy as jnp
from jax import lax
from jax.experimental import pallas as pl
from jax.experimental.pallas import tpu as pltpu
from jax.sharding import PartitionSpec as P

CLUSTERS = 512
MOST = 5
ROOM = 32
TILE = 256
FAR = 2.0**100
LANES = 128
PARAMS = pltpu.CompilerParams(vmem_limit_bytes=40 * 1024 * 1024)
F32 = jnp.float32
BF16 = jnp.bfloat16
I32 = jnp.int32


def iota(shape, dim):
    return lax.broadcasted_iota(I32, shape, dim)


def flags(mask):
    return jnp.where(mask, 1.0, 0.0).astype(BF16)


def dot(a, b):
    return jnp.dot(a, b, preferred_element_type=F32)


def dot_t(a, b):
    return lax.dot_general(a, b, (((1,), (1,)), ((), ())), preferred_element_type=F32)


def shift_of(room):
    return room.bit_length() - 1


def to_col(row):
    size = row.shape[1]
    eye = iota((size, size), 0) == iota((size, size), 1)
    return jnp.sum(jnp.where(eye, row, 0.0), axis=1, keepdims=True)


def deal(position, owners, turn):
    bits = owners.bit_length() - 1
    level = position >> bits
    spot = position & (owners - 1)
    spot = jnp.where((level & 1) == 1, owners - 1 - spot, spot)
    return (spot + level * (turn * 11)) & (owners - 1), level


def match(room, counts, spot_rows, spot_cols, scr):
    set_scr, flip_scr, move_scr, row_scr, col_scr, first_scr, first_t_scr, state_scr, turned_scr = scr
    owners = counts[0].shape[0]
    shape = (owners, LANES)
    square = (LANES, LANES)
    tall = (CLUSTERS, LANES)
    wide = (owners, CLUSTERS)
    rows, cols, level_rows, level_cols = [], [], [], []
    for h in range(2):
        for spot, at, levels in ((spot_rows, rows, level_rows), (spot_cols, cols, level_cols)):
            chosen, level = deal(spot[h], owners, 0)
            at.append(chosen)
            levels.append(level)
    count_scr = counts[1]
    row_scr[...] = jnp.broadcast_to(spot_rows[1], row_scr.shape)
    col_scr[...] = jnp.broadcast_to(spot_cols[1], col_scr.shape)
    first_t_scr[...] = dot_t(flags(iota(wide, 0) == rows[0]), counts[0][...])
    eye = flags(iota((CLUSTERS, CLUSTERS), 0) == iota((CLUSTERS, CLUSTERS), 1))
    flip_scr[...] = dot_t(eye, counts[1][...]).astype(BF16)
    set_scr[...] = flags(iota(tall, 1) == cols[0])
    first_scr[...] = dot(counts[0][...], set_scr[...])

    def misfits():
        eye = iota(shape, 0) == iota(shape, 1)
        return float(owners) - jnp.sum(jnp.where(eye, state_scr[0:owners, :], 0.0))

    def fits(by_row, by_lane):
        most = jnp.zeros(shape, F32)
        for s in range(owners):
            most = jnp.maximum(most, by_row[:, s : s + 1] + by_lane[s : s + 1, :])
        return jnp.where((most <= float(room)) & (iota(shape, 1) < owners), 1.0, 0.0)

    def trade(step):
        eye = iota(shape, 0) == iota(shape, 1)
        fit = state_scr[0:owners, :]
        pairs = fit * turned_scr[0:owners, :]
        fine = jnp.where(eye, fit, 0.0)
        fine_row = jnp.sum(fine, axis=0, keepdims=True)
        fine_col = jnp.sum(fine, axis=1, keepdims=True)

        def granted(asker, asked, bad, good, axis):
            order = (asker * 37 + asked * 11 + step * 7) & (owners - 1)
            asks = pairs * (1.0 - bad) * good * (order + 1).astype(F32)
            asks = jnp.where(asks == jnp.max(asks, axis=axis, keepdims=True), asks, 0.0)
            asks = jnp.where(asks == jnp.max(asks, axis=1 - axis, keepdims=True), asks, 0.0)
            return jnp.minimum(asks, 1.0)

        both = granted(iota(shape, 0), iota(shape, 1), fine_col, fine_row, 1)
        both += granted(iota(shape, 1), iota(shape, 0), fine_row, fine_col, 0)
        settled = 1.0 - jnp.sum(both, axis=0, keepdims=True)
        move_scr[...] = jnp.where(
            iota(square, 0) == iota(square, 1), settled, 0.0
        ).astype(BF16)
        move_scr[0:owners, :] = (both + jnp.where(eye, settled, 0.0)).astype(BF16)
        state_scr[...] = dot(state_scr[...].astype(BF16), move_scr[...])
        turned_scr[...] = dot(move_scr[...], turned_scr[...].astype(BF16))

    def attempt(carry):
        turn, _ = carry
        at_row, _ = deal(row_scr[0:1, :], owners, turn)
        at_col, _ = deal(col_scr[...], owners, turn)
        set_scr[...] = flags(iota(tall, 1) == at_col)
        second = dot(count_scr[...], set_scr[...])
        second_t = dot(flags(iota(wide, 0) == at_row), flip_scr[...])
        state_scr[...] = iota(square, 1).astype(F32)
        state_scr[0:owners, :] = fits(first_t_scr[...], second)
        turned_scr[...] = jnp.zeros(square, F32)
        turned_scr[0:owners, :] = fits(second_t, first_scr[...])

        def trades(carry):
            step, _ = carry
            trade(step)
            return step + 1, misfits()

        _, left = lax.while_loop(
            lambda c: (c[1] > 0.5) & (c[0] < 6), trades, (jnp.int32(0), misfits())
        )
        return turn + 1, left

    turn, left = lax.while_loop(
        lambda c: (c[1] > 0.5) & (c[0] < 8), attempt, (jnp.int32(0), jnp.float32(1.0))
    )
    label = state_scr[owners : owners + 1, :]
    eye = iota(shape, 0) == iota(shape, 1)
    label_col = jnp.sum(jnp.where(eye, label, 0.0), axis=1, keepdims=True).astype(I32)
    at_row, _ = deal(row_scr[0:1, :], owners, turn - 1)
    at_col, _ = deal(col_scr[...], owners, turn - 1)
    row = jnp.where(label_col == at_row, iota(wide, 0).astype(F32), 0.0)
    rows[1] = jnp.sum(row, axis=0, keepdims=True).astype(I32)
    col = jnp.where(label.astype(I32) == at_col, iota(tall, 1).astype(F32), 0.0)
    cols[1] = jnp.sum(col, axis=1, keepdims=True).astype(I32)
    return rows, cols, level_rows, level_cols, left


def plan_kernel(
    room, all_ref, own_ref, ids_ref, rank_ref, place_ref, rows_ref, cols_ref, first_ref, over_ref, *scratch
):
    owners = all_ref.shape[0]
    owned = CLUSTERS // owners
    heads = ids_ref.shape[0]
    cluster_row = iota((1, CLUSTERS), 1).astype(F32)
    home = flags(iota((owners, CLUSTERS), 1) // owned == iota((owners, CLUSTERS), 0))
    counts, spot_rows, spot_cols = [], [], []
    for h in range(heads):
        count = all_ref[:, h * CLUSTERS : (h + 1) * CLUSTERS]
        total = jnp.sum(count.astype(F32), axis=0, keepdims=True)
        order_row = total * CLUSTERS + (CLUSTERS - 1 - cluster_row)
        order_col = to_col(order_row)
        spot_row = jnp.sum(jnp.where(order_col > order_row, 1.0, 0.0), axis=0, keepdims=True)
        spot_col = jnp.sum(jnp.where(order_row > order_col, 1.0, 0.0), axis=1, keepdims=True)
        counts.append(count)
        spot_rows.append(spot_row.astype(I32))
        spot_cols.append(spot_col.astype(I32))
    for scr, count in zip(scratch[:heads], counts):
        scr[...] = (count.astype(F32) + home.astype(F32)).astype(BF16)
    at_rows, at_cols, level_rows, level_cols, left = match(
        room, scratch[:heads], spot_rows, spot_cols, scratch[heads:]
    )
    over_ref[...] = jnp.full(over_ref.shape, jnp.where(left > 0.5, 1.0, 0.0))

    owns = [jnp.broadcast_to(own_ref[h : h + 1, :], (8, CLUSTERS)).astype(BF16) for h in range(heads)]
    for h in range(heads):
        before = flags((at_cols[h] == at_rows[h]) & (level_cols[h] < level_rows[h]))
        offset = dot(owns[h], before)
        if h == 1:
            offset = offset + dot(owns[0], flags(at_cols[0] == at_rows[1]))
        row_id = iota((8, CLUSTERS), 0)
        table = jnp.where(row_id == 0, at_rows[h].astype(F32), offset).astype(BF16)
        toks = ids_ref.shape[1]
        member = flags(iota((CLUSTERS, toks), 0) == ids_ref[h : h + 1, :])
        found = dot(table, member).astype(I32)
        place_ref[h : h + 1, :] = found[0:1] * room + found[1:2] + rank_ref[h : h + 1, :]

    rows_ref[...] = jnp.concatenate(at_rows + level_rows + [jnp.zeros((4, CLUSTERS), I32)], axis=0)
    column = iota((CLUSTERS, LANES), 1)
    found = jnp.zeros((CLUSTERS, LANES), I32)
    for i, values in enumerate(at_cols + level_cols):
        found = jnp.where(column == i, values, found)
    cols_ref[...] = found
    set_scr = scratch[heads]
    set_scr[...] = flags(at_cols[0] == column)
    first_ref[...] = dot(owns[0], set_scr[...])


def arrive_kernel(
    room,
    me_ref,
    all_ref,
    own_ref,
    rows_ref,
    cols_ref,
    sums_row_ref,
    sums_col_ref,
    query_ref,
    key_ref,
    member_ref,
):
    me = me_ref[0]
    owners = all_ref.shape[0]
    owned = CLUSTERS // owners
    heads = own_ref.shape[0]
    cluster_row = iota((1, CLUSTERS), 1).astype(F32)
    counts = [all_ref[:, h * CLUSTERS : (h + 1) * CLUSTERS] for h in range(heads)]
    owns = [jnp.broadcast_to(own_ref[h : h + 1, :], (8, CLUSTERS)).astype(BF16) for h in range(heads)]
    at_rows = [rows_ref[h : h + 1, :] for h in range(heads)]
    level_rows = [rows_ref[heads + h : heads + h + 1, :] for h in range(heads)]
    at_cols = [cols_ref[:, h : h + 1] for h in range(heads)]
    level_cols = [cols_ref[:, heads + h : heads + h + 1] for h in range(heads)]

    items = heads * owned
    lane = iota((CLUSTERS, LANES), 1)
    item = iota((items, CLUSTERS), 0)
    ends = jnp.zeros((owners, LANES), F32)
    ends_t = jnp.zeros((items, owners), F32)
    id_row = jnp.zeros((1, LANES), F32)
    id_col = jnp.zeros((items, 1), F32)
    for h in range(heads):
        ends += dot(counts[h], flags((at_cols[h] == me) & (level_cols[h] + h * owned <= lane)))
        ends_t += dot_t(flags((at_rows[h] == me) & (level_rows[h] + h * owned <= item)), counts[h])
        hit = (at_cols[h] == me) & (level_cols[h] + h * owned == lane)
        id_row += jnp.sum(jnp.where(hit, iota(lane.shape, 0).astype(F32), 0.0), axis=0, keepdims=True)
        hit = (at_rows[h] == me) & (level_rows[h] + h * owned == item)
        id_col += jnp.sum(jnp.where(hit, cluster_row, 0.0), axis=1, keepdims=True)
    rows = key_ref.shape[0]
    inside = ids_down(room, rows, items, ends)
    query_ref[...] = jnp.where(inside, 0.0, -FAR).astype(BF16)
    key_ref[...] = flags(inside)
    id_along = ids_along(room, rows, ends_t)
    member_ref[...] = flags(iota((items, rows), 0).astype(F32) == id_along)

    back_row = id_row.astype(I32) // owned
    back_col = id_col.astype(I32) // owned
    earlier = (back_col == back_row) & (iota((items, LANES), 0) < iota((items, LANES), 1))
    queue = jnp.sum(jnp.where(earlier, 1.0, 0.0), axis=0, keepdims=True)
    used = jnp.sum(
        jnp.where(iota((owners, LANES), 0) == back_row, ends[:, items - 1 : items], 0.0),
        axis=0,
        keepdims=True,
    )
    row = back_row * room + (queue + used).astype(I32)
    sums_row_ref[...] = jnp.broadcast_to(jnp.where(iota((1, LANES), 1) < items, row, -1), sums_row_ref.shape)

    at_lane = jnp.zeros((1, LANES), F32)
    turn_lane = jnp.zeros((1, LANES), F32)
    at_item = jnp.zeros((items, 1), F32)
    turn_item = jnp.zeros((items, 1), F32)
    sent = jnp.zeros((8, LANES), F32)
    for h in range(heads):
        low = me * owned - h * owned
        hit = (iota(lane.shape, 0) == lane + low) & (lane >= h * owned) & (lane < (h + 1) * owned)
        at_lane += jnp.sum(jnp.where(hit, at_cols[h].astype(F32), 0.0), axis=0, keepdims=True)
        turn_lane += jnp.sum(
            jnp.where(hit, (level_cols[h] + h * owned).astype(F32), 0.0), axis=0, keepdims=True
        )
        hit = (iota(item.shape, 1) == item + low) & (item >= h * owned) & (item < (h + 1) * owned)
        at_item += jnp.sum(jnp.where(hit, at_rows[h].astype(F32), 0.0), axis=1, keepdims=True)
        turn_item += jnp.sum(
            jnp.where(hit, (level_rows[h] + h * owned).astype(F32), 0.0), axis=1, keepdims=True
        )
        sent += dot(owns[h], flags(at_cols[h] == lane))
    small = iota((items, LANES), 1)
    ahead = (at_lane == at_item) & (turn_lane < turn_item) & (small < items)
    queue = jnp.sum(jnp.where(ahead, 1.0, 0.0), axis=1, keepdims=True)
    used = jnp.sum(
        jnp.where(small == at_item.astype(I32), sent[0:1], 0.0), axis=1, keepdims=True
    )
    sums_col_ref[...] = jnp.broadcast_to(
        at_item.astype(I32) * room + (queue + used).astype(I32), sums_col_ref.shape
    )


def make_plan(everyone, own, cluster_ids, rank, room):
    heads, toks = cluster_ids.shape
    owners = everyone.shape[0]
    return pl.pallas_call(
        functools.partial(plan_kernel, room),
        out_shape=(
            jax.ShapeDtypeStruct((heads, toks), I32),
            jax.ShapeDtypeStruct((8, CLUSTERS), I32),
            jax.ShapeDtypeStruct((CLUSTERS, LANES), I32),
            jax.ShapeDtypeStruct((8, LANES), F32),
            jax.ShapeDtypeStruct((8, LANES), F32),
        ),
        scratch_shapes=[
            pltpu.VMEM((owners, CLUSTERS), BF16),
            pltpu.VMEM((owners, CLUSTERS), BF16),
            pltpu.VMEM((CLUSTERS, LANES), BF16),
            pltpu.VMEM((CLUSTERS, owners), BF16),
            pltpu.VMEM((LANES, LANES), BF16),
            pltpu.VMEM((8, CLUSTERS), I32),
            pltpu.VMEM((CLUSTERS, LANES), I32),
            pltpu.VMEM((owners, LANES), F32),
            pltpu.VMEM((owners, owners), F32),
            pltpu.VMEM((LANES, LANES), F32),
            pltpu.VMEM((LANES, LANES), F32),
        ],
        compiler_params=PARAMS,
        cost_estimate=pl.CostEstimate(flops=10**9, bytes_accessed=10**6, transcendentals=0),
    )(everyone, own, cluster_ids, rank)


def arrive(me, everyone, own, rows, cols, room):
    owners = everyone.shape[0]
    items = own.shape[0] * CLUSTERS // owners
    vmem = pl.BlockSpec(memory_space=pltpu.VMEM)
    return pl.pallas_call(
        functools.partial(arrive_kernel, room),
        in_specs=[pl.BlockSpec(memory_space=pltpu.SMEM)] + [vmem] * 4,
        out_specs=[vmem] * 5,
        out_shape=(
            jax.ShapeDtypeStruct((8, LANES), I32),
            jax.ShapeDtypeStruct((items, LANES), I32),
            jax.ShapeDtypeStruct((owners * room, LANES), BF16),
            jax.ShapeDtypeStruct((owners * room, LANES), BF16),
            jax.ShapeDtypeStruct((items, owners * room), BF16),
        ),
        compiler_params=PARAMS,
        cost_estimate=pl.CostEstimate(flops=10**9, bytes_accessed=10**6, transcendentals=0),
    )(me, everyone, own, rows, cols)


def of_first(room, rows, base, first_ref):
    place = iota((rows, LANES), 0) + base
    here = (place >> shift_of(room)) == iota((rows, LANES), 1)
    first = jnp.sum(jnp.where(here, first_ref[0:1, :], 0.0), axis=1, keepdims=True)
    return (place[:, 0:1] & (room - 1)).astype(F32) < first


def pack_kernel(room, place_ref, first_ref, q_ref, k_ref, v_ref, out_ref):
    rows, toks = out_ref.shape[0], q_ref.shape[0]
    width = out_ref.shape[1] // 3
    base = pl.program_id(0) * rows
    wanted = iota((rows, toks), 0) + base
    pick = flags((wanted == place_ref[0:1, :]) | (wanted == place_ref[1:2, :]))
    is_first = of_first(room, rows, base, first_ref)
    for part, ref in enumerate((q_ref, k_ref, v_ref)):
        moved = dot(pick, ref[...])
        moved = jnp.where(is_first, moved[:, 0:width], moved[:, width:])
        out_ref[:, part * width : (part + 1) * width] = moved.astype(out_ref.dtype)


def pack(place, first, queries, keys, values, room, owners):
    toks, width = queries.shape
    heads = place.shape[0]
    rows_all = owners * room
    tile = 1024
    whole = pl.BlockSpec((toks, width), lambda i: (0, 0))
    return pl.pallas_call(
        functools.partial(pack_kernel, room),
        grid=(rows_all // tile,),
        in_specs=[
            pl.BlockSpec((heads, toks), lambda i: (0, 0)),
            pl.BlockSpec(first.shape, lambda i: (0, 0)),
            whole,
            whole,
            whole,
        ],
        out_specs=pl.BlockSpec((tile, 3 * width // heads), lambda i: (i, 0)),
        out_shape=jax.ShapeDtypeStruct((rows_all, 3 * width // heads), queries.dtype),
        compiler_params=PARAMS,
        cost_estimate=pl.CostEstimate(
            flops=6 * rows_all * toks * width,
            bytes_accessed=rows_all * width * 3,
            transcendentals=0,
        ),
    )(place, first, queries, keys, values)


def ids_along(room, rows, ends_t):
    items, sources = ends_t.shape
    spread = flags((iota((sources, rows), 1) >> shift_of(room)) == iota((sources, rows), 0))
    ends_row = dot(ends_t.astype(BF16), spread)
    slot_row = (iota((items, rows), 1) & (room - 1)).astype(F32)
    return jnp.sum(jnp.where(ends_row <= slot_row, 1.0, 0.0), axis=0, keepdims=True)


def ids_down(room, rows, items, ends):
    sources = ends.shape[0]
    spread = flags((iota((rows, sources), 0) >> shift_of(room)) == iota((rows, sources), 1))
    lane = iota(ends.shape, 1)
    ends = jnp.where(lane < items, ends, float(2 * LANES))
    starts = jnp.where(lane == 0, 0.0, pltpu.roll(ends, 1, 1))
    bounds = dot(spread, jnp.concatenate([starts, ends], axis=1).astype(BF16))
    slot = (iota((rows, LANES), 0) & (room - 1)).astype(F32)
    return (bounds[:, 0:LANES] <= slot) & (slot < bounds[:, LANES:])


def unit_sums(key_rows, member):
    key_float = key_rows.astype(F32)
    unit = key_float * lax.rsqrt(jnp.sum(key_float * key_float, axis=1, keepdims=True) + 1e-06)
    high = unit.astype(BF16)
    low = (unit - high.astype(F32)).astype(BF16)
    return (dot(member, high) + dot(member, low)).astype(BF16)


def fill(query_ref, key_ref, member_ref, x_ref, query_scr, key_scr, value_scr):
    rows, width = x_ref.shape[0], x_ref.shape[1] // 3
    query_scr[:, 0:width] = x_ref[:, 0:width]
    query_scr[:, width:] = query_ref[...]
    key_scr[:, 0:width] = x_ref[:, width : 2 * width]
    key_scr[:, width:] = key_ref[...]
    value_scr[:, 0:width] = x_ref[:, 2 * width : 3 * width]
    value_scr[:, width:] = jnp.ones((rows, LANES), BF16)
    return unit_sums(x_ref[:, width : 2 * width], member_ref[...])


def weigh(pieces, values, width):
    scale = math.log2(math.e) / math.sqrt(width)
    highest = jnp.max(pieces[0], axis=1, keepdims=True)
    for scores in pieces[1:]:
        highest = jnp.maximum(highest, jnp.max(scores, axis=1, keepdims=True))
    result = jnp.zeros((highest.shape[0], width + LANES), F32)
    for scores, value in zip(pieces, values):
        raised = jnp.exp2((scores - highest) * scale)
        result += dot(raised.astype(BF16), value)
    return result[:, 0:width] / result[:, width : width + 1]


def homeward(begin, tile, sums_row_ref, sums):
    pick = flags(iota((tile, LANES), 0) + begin == sums_row_ref[0:1, :])
    return dot(pick[:, 0 : sums.shape[0]], sums)


def attend_kernel(
    query_ref, key_ref, member_ref, sums_row_ref, x_ref, out_ref, query_scr, key_scr, value_scr
):
    rows, width = out_ref.shape
    sums = fill(query_ref, key_ref, member_ref, x_ref, query_scr, key_scr, value_scr)

    def scores_of(begin):
        end = begin + TILE
        query = query_scr[begin:end, :]
        pieces = [dot_t(query, key_scr[0:begin, :])] if begin else []
        scores = dot_t(query, key_scr[begin:end, :])
        allowed = iota((TILE, TILE), 1) <= iota((TILE, TILE), 0)
        return pieces + [jnp.where(allowed, scores, -FAR)]

    ahead = scores_of(0)
    for begin in range(0, rows, TILE):
        end = begin + TILE
        pieces = ahead
        ahead = scores_of(end) if end < rows else None
        values = [value_scr[0:begin, :]] if begin else []
        values.append(value_scr[begin:end, :])
        result = weigh(pieces, values, width) + homeward(begin, TILE, sums_row_ref, sums)
        out_ref[begin:end] = result.astype(out_ref.dtype)


def attend_tile_kernel(
    query_ref,
    key_ref,
    member_ref,
    sums_row_ref,
    x_ref,
    out_ref,
    query_scr,
    key_scr,
    value_scr,
    sums_scr,
):
    tile, width = out_ref.shape
    rows = x_ref.shape[0]

    @pl.when(pl.program_id(0) == 0)
    def _():
        sums_scr[...] = fill(query_ref, key_ref, member_ref, x_ref, query_scr, key_scr, value_scr)

    begin = pl.multiple_of(pl.program_id(0) * tile, tile)
    scores = dot_t(query_scr[pl.ds(begin, tile), :], key_scr[...])
    allowed = iota((tile, rows), 1) <= iota((tile, rows), 0) + begin
    result = weigh([jnp.where(allowed, scores, -FAR)], [value_scr[...]], width)
    out_ref[...] = (result + homeward(begin, tile, sums_row_ref, sums_scr[...])).astype(out_ref.dtype)


def attend(query_far, key_far, member, sums_row, received):
    rows, width = received.shape[0], received.shape[1] // 3
    shape = jax.ShapeDtypeStruct((rows, width), received.dtype)
    cost = pl.CostEstimate(
        flops=2 * rows * rows * width,
        bytes_accessed=rows * width * 8,
        transcendentals=rows * rows // 2,
    )
    given = (query_far, key_far, member, sums_row, received)
    filled = [pltpu.VMEM((rows, width + LANES), BF16)] * 3
    if rows <= 4096:
        return pl.pallas_call(
            attend_kernel,
            out_shape=shape,
            scratch_shapes=filled,
            compiler_params=PARAMS,
            cost_estimate=cost,
        )(*given)
    tile = 128
    return pl.pallas_call(
        attend_tile_kernel,
        grid=(rows // tile,),
        in_specs=[pl.BlockSpec(x.shape, lambda i: (0, 0)) for x in given],
        out_specs=pl.BlockSpec((tile, width), lambda i: (i, 0)),
        out_shape=shape,
        scratch_shapes=filled + [pltpu.VMEM((member.shape[0], width), BF16)],
        compiler_params=PARAMS,
        cost_estimate=cost,
    )(*given)


def unpack_kernel(
    room, place_ref, sums_col_ref, first_ref, over_ref, back_ref, out_ref, sums_ref, pair_scr
):
    toks, heads = place_ref.shape
    rows, width = back_ref.shape
    groups, share, _ = out_ref.shape

    @pl.when(pl.program_id(0) == 0)
    def _():
        back = back_ref[...]
        is_first = of_first(room, rows, 0, first_ref)
        pair_scr[:, 0:width] = jnp.where(is_first, back.astype(F32), 0.0).astype(BF16)
        pair_scr[:, width:] = jnp.where(is_first, 0.0, back.astype(F32)).astype(BF16)
        items = sums_col_ref.shape[0]
        pick = flags(iota((items, rows), 1) == sums_col_ref[:, 0:1])
        sums_ref[...] = dot(pick, back)

    wanted = iota((toks, rows), 1)
    pick = flags((wanted == place_ref[:, 0:1]) | (wanted == place_ref[:, 1:2]))
    moved = dot(pick, pair_scr[...])
    moved = jnp.where(over_ref[0:1, 0:1] > 0.5, jnp.nan, moved).astype(out_ref.dtype)
    for g in range(groups):
        out_ref[g] = moved[g * share : (g + 1) * share]


def unpack(place, sums_col, first, over, back, groups, room):
    (toks, heads), (rows, width) = place.shape, back.shape
    share = toks // groups
    items = sums_col.shape[0]
    steps = max(1, min(groups, groups * rows // 8192))
    whole = lambda i: (0, 0)
    return pl.pallas_call(
        functools.partial(unpack_kernel, room),
        grid=(steps,),
        in_specs=[
            pl.BlockSpec((toks // steps, heads), lambda i: (i, 0)),
            pl.BlockSpec(sums_col.shape, whole),
            pl.BlockSpec(first.shape, whole),
            pl.BlockSpec(over.shape, whole),
            pl.BlockSpec((rows, width), whole),
        ],
        out_specs=(
            pl.BlockSpec((groups // steps, share, heads * width), lambda i: (i, 0, 0)),
            pl.BlockSpec((items, width), whole),
        ),
        out_shape=(
            jax.ShapeDtypeStruct((groups, share, heads * width), back.dtype),
            jax.ShapeDtypeStruct((items, width), F32),
        ),
        scratch_shapes=[pltpu.VMEM((rows, heads * width), BF16)],
        compiler_params=PARAMS,
        cost_estimate=pl.CostEstimate(
            flops=2 * rows * toks * width * heads,
            bytes_accessed=rows * width * 2,
            transcendentals=0,
        ),
    )(place, sums_col, first, over, back)


def exchange(rows, axis):
    return lax.all_to_all(rows, axis, split_axis=0, concat_axis=0, tiled=True)


def routed(room, queries, keys, values, cluster_ids, rank, own, everyone):
    heads = cluster_ids.shape[0]
    owners = everyone.shape[0]
    me = lax.axis_index("seq").astype(I32)[None]
    place, rows, cols, first, over = make_plan(everyone, own, cluster_ids, rank, room)
    received = exchange(pack(place, first, queries, keys, values, room, owners), "seq")
    sums_row, sums_col, query_far, key_far, member = arrive(me, everyone, own, rows, cols, room)
    back = exchange(attend(query_far, key_far, member, sums_row, received), "seq")
    share, sums = unpack(place.T, sums_col, first, over, back, lax.axis_size("head"), room)
    parts = exchange(share, "head")
    owned = CLUSTERS // owners
    sums = jnp.concatenate([sums[h * owned : (h + 1) * owned] for h in range(heads)], axis=1)
    return parts, sums


def project(parts, weight):
    weight = weight.reshape(parts.shape[0], parts.shape[2], weight.shape[1])
    total = jnp.einsum("gtd,gdn->tn", parts, weight, preferred_element_type=F32)
    return total.astype(BF16)


def count_kernel(ids_ref, own_ref, told_ref, member_scr):
    heads, toks = ids_ref.shape
    chunks = []
    for h in range(heads):
        member_scr[h] = flags(iota((CLUSTERS, toks), 0) == ids_ref[h : h + 1, :])
        own = dot_t(jnp.ones((8, toks), BF16), member_scr[h])
        own_ref[h : h + 1, :] = own[0:1]
        chunks += [own[0:1, at : at + LANES] for at in range(0, CLUSTERS, LANES)]
    told_ref[...] = jnp.broadcast_to(jnp.concatenate(chunks, axis=0)[None], told_ref.shape).astype(BF16)


def count(cluster_ids, owners):
    heads, toks = cluster_ids.shape
    return pl.pallas_call(
        count_kernel,
        out_shape=(
            jax.ShapeDtypeStruct((heads, CLUSTERS), F32),
            jax.ShapeDtypeStruct((owners, heads * CLUSTERS // LANES, LANES), BF16),
        ),
        scratch_shapes=[pltpu.VMEM((heads, CLUSTERS, toks), BF16)],
        compiler_params=PARAMS,
        cost_estimate=pl.CostEstimate(flops=10**8, bytes_accessed=10**5, transcendentals=0),
    )(cluster_ids)


def body(queries, keys, values, cluster_ids, out_weight):
    heads, toks = cluster_ids.shape
    owners = lax.axis_size("seq")
    own, told = count(cluster_ids, owners)
    everyone = exchange(told, "seq").reshape(owners, heads * CLUSTERS)
    own, out_weight = lax.optimization_barrier((own, out_weight))
    full_weight = lax.all_gather(out_weight, "head", axis=0, tiled=True)

    spot = jnp.arange(toks, dtype=I32)
    same = cluster_ids[:, :, None] == cluster_ids[:, None, :]
    rank = jnp.sum((same & (spot[:, None] < spot[None, :])[None]).astype(I32), axis=1)
    given = (queries, keys, values, cluster_ids, rank, own, everyone)
    parts, key_sums = routed(ROOM, *given)
    full_room = 1 << (heads * CLUSTERS // owners * (MOST + 1) - 1).bit_length()

    def again():
        wide, wide_sums = routed(full_room, *given)
        return project(wide, full_weight), wide_sums

    def done():
        return project(parts, full_weight), key_sums

    return lax.cond(jnp.any(jnp.isnan(parts[:, 0, 0])), again, done)


def solution(mesh):
    placed = (
        P("seq", "head"),
        P("seq", "head"),
        P("seq", "head"),
        P("head", "seq"),
        P("head", None),
    )
    return jax.shard_map(
        body,
        mesh=mesh,
        in_specs=placed,
        out_specs=(P(("seq", "head"), None), P("seq", "head")),
        check_vma=False,
    )
```

```python
import functools
import math

import jax
import jax.numpy as jnp
from jax import lax
from jax.experimental import pallas as pl
from jax.experimental.pallas import tpu as pltpu
from jax.sharding import PartitionSpec as P

CLUSTERS = 512
MOST = 5
ROOM = 32
TILE = 256
FAR = 2.0**100
LANES = 128
PARAMS = pltpu.CompilerParams(vmem_limit_bytes=40 * 1024 * 1024)
F32 = jnp.float32
BF16 = jnp.bfloat16
I32 = jnp.int32


def iota(shape, dim):
    return lax.broadcasted_iota(I32, shape, dim)


def flags(mask):
    return jnp.where(mask, 1.0, 0.0).astype(BF16)


def dot(a, b):
    return jnp.dot(a, b, preferred_element_type=F32)


def dot_t(a, b):
    return lax.dot_general(a, b, (((1,), (1,)), ((), ())), preferred_element_type=F32)


def shift_of(room):
    return room.bit_length() - 1


def to_col(row):
    size = row.shape[1]
    eye = iota((size, size), 0) == iota((size, size), 1)
    return jnp.sum(jnp.where(eye, row, 0.0), axis=1, keepdims=True)


def deal(position, owners, turn):
    bits = owners.bit_length() - 1
    level = position >> bits
    spot = position & (owners - 1)
    spot = jnp.where((level & 1) == 1, owners - 1 - spot, spot)
    return (spot + level * (turn * 11)) & (owners - 1), level


def match(room, counts, spot_rows, spot_cols, scr):
    set_scr, flip_scr, move_scr, row_scr, col_scr, first_scr, first_t_scr, state_scr, turned_scr = scr
    owners = counts[0].shape[0]
    shape = (owners, LANES)
    square = (LANES, LANES)
    tall = (CLUSTERS, LANES)
    wide = (owners, CLUSTERS)
    rows, cols, level_rows, level_cols = [], [], [], []
    for h in range(2):
        for spot, at, levels in ((spot_rows, rows, level_rows), (spot_cols, cols, level_cols)):
            chosen, level = deal(spot[h], owners, 0)
            at.append(chosen)
            levels.append(level)
    count_scr = counts[1]
    row_scr[...] = jnp.broadcast_to(spot_rows[1], row_scr.shape)
    col_scr[...] = jnp.broadcast_to(spot_cols[1], col_scr.shape)
    first_t_scr[...] = dot_t(flags(iota(wide, 0) == rows[0]), counts[0][...])
    eye = flags(iota((CLUSTERS, CLUSTERS), 0) == iota((CLUSTERS, CLUSTERS), 1))
    flip_scr[...] = dot_t(eye, counts[1][...]).astype(BF16)
    set_scr[...] = flags(iota(tall, 1) == cols[0])
    first_scr[...] = dot(counts[0][...], set_scr[...])

    def misfits():
        eye = iota(shape, 0) == iota(shape, 1)
        return float(owners) - jnp.sum(jnp.where(eye, state_scr[0:owners, :], 0.0))

    def fits(by_row, by_lane):
        most = jnp.zeros(shape, F32)
        for s in range(owners):
            most = jnp.maximum(most, by_row[:, s : s + 1] + by_lane[s : s + 1, :])
        return jnp.where((most <= float(room)) & (iota(shape, 1) < owners), 1.0, 0.0)

    def trade(step):
        eye = iota(shape, 0) == iota(shape, 1)
        fit = state_scr[0:owners, :]
        pairs = fit * turned_scr[0:owners, :]
        fine = jnp.where(eye, fit, 0.0)
        fine_row = jnp.sum(fine, axis=0, keepdims=True)
        fine_col = jnp.sum(fine, axis=1, keepdims=True)

        def granted(asker, asked, bad, good, axis):
            order = (asker * 37 + asked * 11 + step * 7) & (owners - 1)
            asks = pairs * (1.0 - bad) * good * (order + 1).astype(F32)
            asks = jnp.where(asks == jnp.max(asks, axis=axis, keepdims=True), asks, 0.0)
            asks = jnp.where(asks == jnp.max(asks, axis=1 - axis, keepdims=True), asks, 0.0)
            return jnp.minimum(asks, 1.0)

        both = granted(iota(shape, 0), iota(shape, 1), fine_col, fine_row, 1)
        both += granted(iota(shape, 1), iota(shape, 0), fine_row, fine_col, 0)
        settled = 1.0 - jnp.sum(both, axis=0, keepdims=True)
        move_scr[...] = jnp.where(
            iota(square, 0) == iota(square, 1), settled, 0.0
        ).astype(BF16)
        move_scr[0:owners, :] = (both + jnp.where(eye, settled, 0.0)).astype(BF16)
        state_scr[...] = dot(state_scr[...].astype(BF16), move_scr[...])
        turned_scr[...] = dot(move_scr[...], turned_scr[...].astype(BF16))

    def attempt(carry):
        turn, _ = carry
        at_row, _ = deal(row_scr[0:1, :], owners, turn)
        at_col, _ = deal(col_scr[...], owners, turn)
        set_scr[...] = flags(iota(tall, 1) == at_col)
        second = dot(count_scr[...], set_scr[...])
        second_t = dot(flags(iota(wide, 0) == at_row), flip_scr[...])
        state_scr[...] = iota(square, 1).astype(F32)
        state_scr[0:owners, :] = fits(first_t_scr[...], second)
        turned_scr[...] = jnp.zeros(square, F32)
        turned_scr[0:owners, :] = fits(second_t, first_scr[...])

        def trades(carry):
            step, _ = carry
            trade(step)
            return step + 1, misfits()

        _, left = lax.while_loop(
            lambda c: (c[1] > 0.5) & (c[0] < 6), trades, (jnp.int32(0), misfits())
        )
        return turn + 1, left

    turn, left = lax.while_loop(
        lambda c: (c[1] > 0.5) & (c[0] < 8), attempt, (jnp.int32(0), jnp.float32(1.0))
    )
    label = state_scr[owners : owners + 1, :]
    eye = iota(shape, 0) == iota(shape, 1)
    label_col = jnp.sum(jnp.where(eye, label, 0.0), axis=1, keepdims=True).astype(I32)
    at_row, _ = deal(row_scr[0:1, :], owners, turn - 1)
    at_col, _ = deal(col_scr[...], owners, turn - 1)
    row = jnp.where(label_col == at_row, iota(wide, 0).astype(F32), 0.0)
    rows[1] = jnp.sum(row, axis=0, keepdims=True).astype(I32)
    col = jnp.where(label.astype(I32) == at_col, iota(tall, 1).astype(F32), 0.0)
    cols[1] = jnp.sum(col, axis=1, keepdims=True).astype(I32)
    return rows, cols, level_rows, level_cols, left


def plan_kernel(
    room, all_ref, own_ref, ids_ref, rank_ref, place_ref, rows_ref, cols_ref, first_ref, over_ref, *scratch
):
    owners = all_ref.shape[0]
    owned = CLUSTERS // owners
    heads = ids_ref.shape[0]
    cluster_row = iota((1, CLUSTERS), 1).astype(F32)
    home = flags(iota((owners, CLUSTERS), 1) // owned == iota((owners, CLUSTERS), 0))
    counts, spot_rows, spot_cols = [], [], []
    for h in range(heads):
        count = all_ref[:, h * CLUSTERS : (h + 1) * CLUSTERS]
        total = jnp.sum(count.astype(F32), axis=0, keepdims=True)
        order_row = total * CLUSTERS + (CLUSTERS - 1 - cluster_row)
        order_col = to_col(order_row)
        spot_row = jnp.sum(jnp.where(order_col > order_row, 1.0, 0.0), axis=0, keepdims=True)
        spot_col = jnp.sum(jnp.where(order_row > order_col, 1.0, 0.0), axis=1, keepdims=True)
        counts.append(count)
        spot_rows.append(spot_row.astype(I32))
        spot_cols.append(spot_col.astype(I32))
    for scr, count in zip(scratch[:heads], counts):
        scr[...] = (count.astype(F32) + home.astype(F32)).astype(BF16)
    at_rows, at_cols, level_rows, level_cols, left = match(
        room, scratch[:heads], spot_rows, spot_cols, scratch[heads:]
    )
    over_ref[...] = jnp.full(over_ref.shape, jnp.where(left > 0.5, 1.0, 0.0))

    owns = [jnp.broadcast_to(own_ref[h : h + 1, :], (8, CLUSTERS)).astype(BF16) for h in range(heads)]
    for h in range(heads):
        before = flags((at_cols[h] == at_rows[h]) & (level_cols[h] < level_rows[h]))
        offset = dot(owns[h], before)
        if h == 1:
            offset = offset + dot(owns[0], flags(at_cols[0] == at_rows[1]))
        row_id = iota((8, CLUSTERS), 0)
        table = jnp.where(row_id == 0, at_rows[h].astype(F32), offset).astype(BF16)
        toks = ids_ref.shape[1]
        member = flags(iota((CLUSTERS, toks), 0) == ids_ref[h : h + 1, :])
        found = dot(table, member).astype(I32)
        place_ref[h : h + 1, :] = found[0:1] * room + found[1:2] + rank_ref[h : h + 1, :]

    rows_ref[...] = jnp.concatenate(at_rows + level_rows + [jnp.zeros((4, CLUSTERS), I32)], axis=0)
    column = iota((CLUSTERS, LANES), 1)
    found = jnp.zeros((CLUSTERS, LANES), I32)
    for i, values in enumerate(at_cols + level_cols):
        found = jnp.where(column == i, values, found)
    cols_ref[...] = found
    set_scr = scratch[heads]
    set_scr[...] = flags(at_cols[0] == column)
    first_ref[...] = dot(owns[0], set_scr[...])


def arrive_kernel(
    room,
    me_ref,
    all_ref,
    own_ref,
    rows_ref,
    cols_ref,
    sums_row_ref,
    sums_col_ref,
    query_ref,
    key_ref,
    member_ref,
):
    me = me_ref[0]
    owners = all_ref.shape[0]
    owned = CLUSTERS // owners
    heads = own_ref.shape[0]
    cluster_row = iota((1, CLUSTERS), 1).astype(F32)
    counts = [all_ref[:, h * CLUSTERS : (h + 1) * CLUSTERS] for h in range(heads)]
    owns = [jnp.broadcast_to(own_ref[h : h + 1, :], (8, CLUSTERS)).astype(BF16) for h in range(heads)]
    at_rows = [rows_ref[h : h + 1, :] for h in range(heads)]
    level_rows = [rows_ref[heads + h : heads + h + 1, :] for h in range(heads)]
    at_cols = [cols_ref[:, h : h + 1] for h in range(heads)]
    level_cols = [cols_ref[:, heads + h : heads + h + 1] for h in range(heads)]

    items = heads * owned
    lane = iota((CLUSTERS, LANES), 1)
    item = iota((items, CLUSTERS), 0)
    ends = jnp.zeros((owners, LANES), F32)
    ends_t = jnp.zeros((items, owners), F32)
    id_row = jnp.zeros((1, LANES), F32)
    id_col = jnp.zeros((items, 1), F32)
    for h in range(heads):
        ends += dot(counts[h], flags((at_cols[h] == me) & (level_cols[h] + h * owned <= lane)))
        ends_t += dot_t(flags((at_rows[h] == me) & (level_rows[h] + h * owned <= item)), counts[h])
        hit = (at_cols[h] == me) & (level_cols[h] + h * owned == lane)
        id_row += jnp.sum(jnp.where(hit, iota(lane.shape, 0).astype(F32), 0.0), axis=0, keepdims=True)
        hit = (at_rows[h] == me) & (level_rows[h] + h * owned == item)
        id_col += jnp.sum(jnp.where(hit, cluster_row, 0.0), axis=1, keepdims=True)
    rows = key_ref.shape[0]
    inside = ids_down(room, rows, items, ends)
    query_ref[...] = jnp.where(inside, 0.0, -FAR).astype(BF16)
    key_ref[...] = flags(inside)
    id_along = ids_along(room, rows, ends_t)
    member_ref[...] = flags(iota((items, rows), 0).astype(F32) == id_along)

    back_row = id_row.astype(I32) // owned
    back_col = id_col.astype(I32) // owned
    earlier = (back_col == back_row) & (iota((items, LANES), 0) < iota((items, LANES), 1))
    queue = jnp.sum(jnp.where(earlier, 1.0, 0.0), axis=0, keepdims=True)
    used = jnp.sum(
        jnp.where(iota((owners, LANES), 0) == back_row, ends[:, items - 1 : items], 0.0),
        axis=0,
        keepdims=True,
    )
    row = back_row * room + (queue + used).astype(I32)
    sums_row_ref[...] = jnp.broadcast_to(jnp.where(iota((1, LANES), 1) < items, row, -1), sums_row_ref.shape)

    at_lane = jnp.zeros((1, LANES), F32)
    turn_lane = jnp.zeros((1, LANES), F32)
    at_item = jnp.zeros((items, 1), F32)
    turn_item = jnp.zeros((items, 1), F32)
    sent = jnp.zeros((8, LANES), F32)
    for h in range(heads):
        low = me * owned - h * owned
        hit = (iota(lane.shape, 0) == lane + low) & (lane >= h * owned) & (lane < (h + 1) * owned)
        at_lane += jnp.sum(jnp.where(hit, at_cols[h].astype(F32), 0.0), axis=0, keepdims=True)
        turn_lane += jnp.sum(
            jnp.where(hit, (level_cols[h] + h * owned).astype(F32), 0.0), axis=0, keepdims=True
        )
        hit = (iota(item.shape, 1) == item + low) & (item >= h * owned) & (item < (h + 1) * owned)
        at_item += jnp.sum(jnp.where(hit, at_rows[h].astype(F32), 0.0), axis=1, keepdims=True)
        turn_item += jnp.sum(
            jnp.where(hit, (level_rows[h] + h * owned).astype(F32), 0.0), axis=1, keepdims=True
        )
        sent += dot(owns[h], flags(at_cols[h] == lane))
    small = iota((items, LANES), 1)
    ahead = (at_lane == at_item) & (turn_lane < turn_item) & (small < items)
    queue = jnp.sum(jnp.where(ahead, 1.0, 0.0), axis=1, keepdims=True)
    used = jnp.sum(
        jnp.where(small == at_item.astype(I32), sent[0:1], 0.0), axis=1, keepdims=True
    )
    sums_col_ref[...] = jnp.broadcast_to(
        at_item.astype(I32) * room + (queue + used).astype(I32), sums_col_ref.shape
    )


def make_plan(everyone, own, cluster_ids, rank, room):
    heads, toks = cluster_ids.shape
    owners = everyone.shape[0]
    return pl.pallas_call(
        functools.partial(plan_kernel, room),
        out_shape=(
            jax.ShapeDtypeStruct((heads, toks), I32),
            jax.ShapeDtypeStruct((8, CLUSTERS), I32),
            jax.ShapeDtypeStruct((CLUSTERS, LANES), I32),
            jax.ShapeDtypeStruct((8, LANES), F32),
            jax.ShapeDtypeStruct((8, LANES), F32),
        ),
        scratch_shapes=[
            pltpu.VMEM((owners, CLUSTERS), BF16),
            pltpu.VMEM((owners, CLUSTERS), BF16),
            pltpu.VMEM((CLUSTERS, LANES), BF16),
            pltpu.VMEM((CLUSTERS, owners), BF16),
            pltpu.VMEM((LANES, LANES), BF16),
            pltpu.VMEM((8, CLUSTERS), I32),
            pltpu.VMEM((CLUSTERS, LANES), I32),
            pltpu.VMEM((owners, LANES), F32),
            pltpu.VMEM((owners, owners), F32),
            pltpu.VMEM((LANES, LANES), F32),
            pltpu.VMEM((LANES, LANES), F32),
        ],
        compiler_params=PARAMS,
        cost_estimate=pl.CostEstimate(flops=10**9, bytes_accessed=10**6, transcendentals=0),
    )(everyone, own, cluster_ids, rank)


def arrive(me, everyone, own, rows, cols, room):
    owners = everyone.shape[0]
    items = own.shape[0] * CLUSTERS // owners
    vmem = pl.BlockSpec(memory_space=pltpu.VMEM)
    return pl.pallas_call(
        functools.partial(arrive_kernel, room),
        in_specs=[pl.BlockSpec(memory_space=pltpu.SMEM)] + [vmem] * 4,
        out_specs=[vmem] * 5,
        out_shape=(
            jax.ShapeDtypeStruct((8, LANES), I32),
            jax.ShapeDtypeStruct((items, LANES), I32),
            jax.ShapeDtypeStruct((owners * room, LANES), BF16),
            jax.ShapeDtypeStruct((owners * room, LANES), BF16),
            jax.ShapeDtypeStruct((items, owners * room), BF16),
        ),
        compiler_params=PARAMS,
        cost_estimate=pl.CostEstimate(flops=10**9, bytes_accessed=10**6, transcendentals=0),
    )(me, everyone, own, rows, cols)


def of_first(room, rows, base, first_ref):
    place = iota((rows, LANES), 0) + base
    here = (place >> shift_of(room)) == iota((rows, LANES), 1)
    first = jnp.sum(jnp.where(here, first_ref[0:1, :], 0.0), axis=1, keepdims=True)
    return (place[:, 0:1] & (room - 1)).astype(F32) < first


def pack_kernel(room, place_ref, first_ref, q_ref, k_ref, v_ref, out_ref):
    rows, toks = out_ref.shape[0], q_ref.shape[0]
    width = out_ref.shape[1] // 3
    base = pl.program_id(0) * rows
    wanted = iota((rows, toks), 0) + base
    pick = flags((wanted == place_ref[0:1, :]) | (wanted == place_ref[1:2, :]))
    is_first = of_first(room, rows, base, first_ref)
    for part, ref in enumerate((q_ref, k_ref, v_ref)):
        moved = dot(pick, ref[...])
        moved = jnp.where(is_first, moved[:, 0:width], moved[:, width:])
        out_ref[:, part * width : (part + 1) * width] = moved.astype(out_ref.dtype)


def pack(place, first, queries, keys, values, room, owners):
    toks, width = queries.shape
    heads = place.shape[0]
    rows_all = owners * room
    tile = 1024
    whole = pl.BlockSpec((toks, width), lambda i: (0, 0))
    return pl.pallas_call(
        functools.partial(pack_kernel, room),
        grid=(rows_all // tile,),
        in_specs=[
            pl.BlockSpec((heads, toks), lambda i: (0, 0)),
            pl.BlockSpec(first.shape, lambda i: (0, 0)),
            whole,
            whole,
            whole,
        ],
        out_specs=pl.BlockSpec((tile, 3 * width // heads), lambda i: (i, 0)),
        out_shape=jax.ShapeDtypeStruct((rows_all, 3 * width // heads), queries.dtype),
        compiler_params=PARAMS,
        cost_estimate=pl.CostEstimate(
            flops=6 * rows_all * toks * width,
            bytes_accessed=rows_all * width * 3,
            transcendentals=0,
        ),
    )(place, first, queries, keys, values)


def ids_along(room, rows, ends_t):
    items, sources = ends_t.shape
    spread = flags((iota((sources, rows), 1) >> shift_of(room)) == iota((sources, rows), 0))
    ends_row = dot(ends_t.astype(BF16), spread)
    slot_row = (iota((items, rows), 1) & (room - 1)).astype(F32)
    return jnp.sum(jnp.where(ends_row <= slot_row, 1.0, 0.0), axis=0, keepdims=True)


def ids_down(room, rows, items, ends):
    sources = ends.shape[0]
    spread = flags((iota((rows, sources), 0) >> shift_of(room)) == iota((rows, sources), 1))
    lane = iota(ends.shape, 1)
    ends = jnp.where(lane < items, ends, float(2 * LANES))
    starts = jnp.where(lane == 0, 0.0, pltpu.roll(ends, 1, 1))
    bounds = dot(spread, jnp.concatenate([starts, ends], axis=1).astype(BF16))
    slot = (iota((rows, LANES), 0) & (room - 1)).astype(F32)
    return (bounds[:, 0:LANES] <= slot) & (slot < bounds[:, LANES:])


def unit_sums(key_rows, member):
    key_float = key_rows.astype(F32)
    unit = key_float * lax.rsqrt(jnp.sum(key_float * key_float, axis=1, keepdims=True) + 1e-06)
    high = unit.astype(BF16)
    low = (unit - high.astype(F32)).astype(BF16)
    return (dot(member, high) + dot(member, low)).astype(BF16)


def fill(query_ref, key_ref, member_ref, x_ref, query_scr, key_scr, value_scr):
    rows, width = x_ref.shape[0], x_ref.shape[1] // 3
    query_scr[:, 0:width] = x_ref[:, 0:width]
    query_scr[:, width:] = query_ref[...]
    key_scr[:, 0:width] = x_ref[:, width : 2 * width]
    key_scr[:, width:] = key_ref[...]
    value_scr[:, 0:width] = x_ref[:, 2 * width : 3 * width]
    value_scr[:, width:] = jnp.ones((rows, LANES), BF16)
    return unit_sums(x_ref[:, width : 2 * width], member_ref[...])


def weigh(pieces, values, width):
    scale = math.log2(math.e) / math.sqrt(width)
    highest = jnp.max(pieces[0], axis=1, keepdims=True)
    for scores in pieces[1:]:
        highest = jnp.maximum(highest, jnp.max(scores, axis=1, keepdims=True))
    result = jnp.zeros((highest.shape[0], width + LANES), F32)
    for scores, value in zip(pieces, values):
        raised = jnp.exp2((scores - highest) * scale)
        result += dot(raised.astype(BF16), value)
    return result[:, 0:width] / result[:, width : width + 1]


def homeward(begin, tile, sums_row_ref, sums):
    pick = flags(iota((tile, LANES), 0) + begin == sums_row_ref[0:1, :])
    return dot(pick[:, 0 : sums.shape[0]], sums)


def attend_kernel(
    query_ref, key_ref, member_ref, sums_row_ref, x_ref, out_ref, query_scr, key_scr, value_scr
):
    rows, width = out_ref.shape
    sums = fill(query_ref, key_ref, member_ref, x_ref, query_scr, key_scr, value_scr)

    def scores_of(begin):
        end = begin + TILE
        query = query_scr[begin:end, :]
        pieces = [dot_t(query, key_scr[0:begin, :])] if begin else []
        scores = dot_t(query, key_scr[begin:end, :])
        allowed = iota((TILE, TILE), 1) <= iota((TILE, TILE), 0)
        return pieces + [jnp.where(allowed, scores, -FAR)]

    ahead = scores_of(0)
    for begin in range(0, rows, TILE):
        end = begin + TILE
        pieces = ahead
        ahead = scores_of(end) if end < rows else None
        values = [value_scr[0:begin, :]] if begin else []
        values.append(value_scr[begin:end, :])
        result = weigh(pieces, values, width) + homeward(begin, TILE, sums_row_ref, sums)
        out_ref[begin:end] = result.astype(out_ref.dtype)


def attend_tile_kernel(
    query_ref,
    key_ref,
    member_ref,
    sums_row_ref,
    x_ref,
    out_ref,
    query_scr,
    key_scr,
    value_scr,
    sums_scr,
):
    tile, width = out_ref.shape
    rows = x_ref.shape[0]

    @pl.when(pl.program_id(0) == 0)
    def _():
        sums_scr[...] = fill(query_ref, key_ref, member_ref, x_ref, query_scr, key_scr, value_scr)

    begin = pl.multiple_of(pl.program_id(0) * tile, tile)
    scores = dot_t(query_scr[pl.ds(begin, tile), :], key_scr[...])
    allowed = iota((tile, rows), 1) <= iota((tile, rows), 0) + begin
    result = weigh([jnp.where(allowed, scores, -FAR)], [value_scr[...]], width)
    out_ref[...] = (result + homeward(begin, tile, sums_row_ref, sums_scr[...])).astype(out_ref.dtype)


def attend(query_far, key_far, member, sums_row, received):
    rows, width = received.shape[0], received.shape[1] // 3
    shape = jax.ShapeDtypeStruct((rows, width), received.dtype)
    cost = pl.CostEstimate(
        flops=2 * rows * rows * width,
        bytes_accessed=rows * width * 8,
        transcendentals=rows * rows // 2,
    )
    given = (query_far, key_far, member, sums_row, received)
    filled = [pltpu.VMEM((rows, width + LANES), BF16)] * 3
    if rows <= 4096:
        return pl.pallas_call(
            attend_kernel,
            out_shape=shape,
            scratch_shapes=filled,
            compiler_params=PARAMS,
            cost_estimate=cost,
        )(*given)
    tile = 128
    return pl.pallas_call(
        attend_tile_kernel,
        grid=(rows // tile,),
        in_specs=[pl.BlockSpec(x.shape, lambda i: (0, 0)) for x in given],
        out_specs=pl.BlockSpec((tile, width), lambda i: (i, 0)),
        out_shape=shape,
        scratch_shapes=filled + [pltpu.VMEM((member.shape[0], width), BF16)],
        compiler_params=PARAMS,
        cost_estimate=cost,
    )(*given)


def unpack_kernel(
    room, place_ref, sums_col_ref, first_ref, over_ref, back_ref, out_ref, sums_ref, pair_scr
):
    toks, heads = place_ref.shape
    rows, width = back_ref.shape
    groups, share, _ = out_ref.shape

    @pl.when(pl.program_id(0) == 0)
    def _():
        back = back_ref[...]
        is_first = of_first(room, rows, 0, first_ref)
        pair_scr[:, 0:width] = jnp.where(is_first, back.astype(F32), 0.0).astype(BF16)
        pair_scr[:, width:] = jnp.where(is_first, 0.0, back.astype(F32)).astype(BF16)
        items = sums_col_ref.shape[0]
        pick = flags(iota((items, rows), 1) == sums_col_ref[:, 0:1])
        sums_ref[...] = dot(pick, back)

    wanted = iota((toks, rows), 1)
    pick = flags((wanted == place_ref[:, 0:1]) | (wanted == place_ref[:, 1:2]))
    moved = dot(pick, pair_scr[...])
    moved = jnp.where(over_ref[0:1, 0:1] > 0.5, jnp.nan, moved).astype(out_ref.dtype)
    for g in range(groups):
        out_ref[g] = moved[g * share : (g + 1) * share]


def unpack(place, sums_col, first, over, back, groups, room):
    (toks, heads), (rows, width) = place.shape, back.shape
    share = toks // groups
    items = sums_col.shape[0]
    steps = max(1, min(groups, groups * rows // 16384))
    whole = lambda i: (0, 0)
    return pl.pallas_call(
        functools.partial(unpack_kernel, room),
        grid=(steps,),
        in_specs=[
            pl.BlockSpec((toks // steps, heads), lambda i: (i, 0)),
            pl.BlockSpec(sums_col.shape, whole),
            pl.BlockSpec(first.shape, whole),
            pl.BlockSpec(over.shape, whole),
            pl.BlockSpec((rows, width), whole),
        ],
        out_specs=(
            pl.BlockSpec((groups // steps, share, heads * width), lambda i: (i, 0, 0)),
            pl.BlockSpec((items, width), whole),
        ),
        out_shape=(
            jax.ShapeDtypeStruct((groups, share, heads * width), back.dtype),
            jax.ShapeDtypeStruct((items, width), F32),
        ),
        scratch_shapes=[pltpu.VMEM((rows, heads * width), BF16)],
        compiler_params=PARAMS,
        cost_estimate=pl.CostEstimate(
            flops=2 * rows * toks * width * heads,
            bytes_accessed=rows * width * 2,
            transcendentals=0,
        ),
    )(place, sums_col, first, over, back)


def exchange(rows, axis):
    return lax.all_to_all(rows, axis, split_axis=0, concat_axis=0, tiled=True)


def routed(room, queries, keys, values, cluster_ids, rank, own, everyone):
    heads = cluster_ids.shape[0]
    owners = everyone.shape[0]
    me = lax.axis_index("seq").astype(I32)[None]
    place, rows, cols, first, over = make_plan(everyone, own, cluster_ids, rank, room)
    received = exchange(pack(place, first, queries, keys, values, room, owners), "seq")
    sums_row, sums_col, query_far, key_far, member = arrive(me, everyone, own, rows, cols, room)
    back = exchange(attend(query_far, key_far, member, sums_row, received), "seq")
    share, sums = unpack(place.T, sums_col, first, over, back, lax.axis_size("head"), room)
    parts = exchange(share, "head")
    owned = CLUSTERS // owners
    sums = jnp.concatenate([sums[h * owned : (h + 1) * owned] for h in range(heads)], axis=1)
    return parts, sums


def project(parts, weight):
    weight = weight.reshape(parts.shape[0], parts.shape[2], weight.shape[1])
    total = jnp.einsum("gtd,gdn->tn", parts, weight, preferred_element_type=F32)
    return total.astype(BF16)


def count_kernel(ids_ref, own_ref, told_ref, member_scr):
    heads, toks = ids_ref.shape
    chunks = []
    for h in range(heads):
        member_scr[h] = flags(iota((CLUSTERS, toks), 0) == ids_ref[h : h + 1, :])
        own = dot_t(jnp.ones((8, toks), BF16), member_scr[h])
        own_ref[h : h + 1, :] = own[0:1]
        chunks += [own[0:1, at : at + LANES] for at in range(0, CLUSTERS, LANES)]
    told_ref[...] = jnp.broadcast_to(jnp.concatenate(chunks, axis=0)[None], told_ref.shape).astype(BF16)


def count(cluster_ids, owners):
    heads, toks = cluster_ids.shape
    return pl.pallas_call(
        count_kernel,
        out_shape=(
            jax.ShapeDtypeStruct((heads, CLUSTERS), F32),
            jax.ShapeDtypeStruct((owners, heads * CLUSTERS // LANES, LANES), BF16),
        ),
        scratch_shapes=[pltpu.VMEM((heads, CLUSTERS, toks), BF16)],
        compiler_params=PARAMS,
        cost_estimate=pl.CostEstimate(flops=10**8, bytes_accessed=10**5, transcendentals=0),
    )(cluster_ids)


def body(queries, keys, values, cluster_ids, out_weight):
    heads, toks = cluster_ids.shape
    owners = lax.axis_size("seq")
    own, told = count(cluster_ids, owners)
    everyone = exchange(told, "seq").reshape(owners, heads * CLUSTERS)
    own, out_weight = lax.optimization_barrier((own, out_weight))
    full_weight = lax.all_gather(out_weight, "head", axis=0, tiled=True)

    spot = jnp.arange(toks, dtype=I32)
    same = cluster_ids[:, :, None] == cluster_ids[:, None, :]
    rank = jnp.sum((same & (spot[:, None] < spot[None, :])[None]).astype(I32), axis=1)
    given = (queries, keys, values, cluster_ids, rank, own, everyone)
    parts, key_sums = routed(ROOM, *given)
    full_room = 1 << (heads * CLUSTERS // owners * (MOST + 1) - 1).bit_length()

    def again():
        wide, wide_sums = routed(full_room, *given)
        return project(wide, full_weight), wide_sums

    def done():
        return project(parts, full_weight), key_sums

    return lax.cond(jnp.any(jnp.isnan(parts[:, 0, 0])), again, done)


def solution(mesh):
    placed = (
        P("seq", "head"),
        P("seq", "head"),
        P("seq", "head"),
        P("head", "seq"),
        P("head", None),
    )
    return jax.shard_map(
        body,
        mesh=mesh,
        in_specs=placed,
        out_specs=(P(("seq", "head"), None), P("seq", "head")),
        check_vma=False,
    )
```

```python
import functools
import math

import jax
import jax.numpy as jnp
from jax import lax
from jax.experimental import pallas as pl
from jax.experimental.pallas import tpu as pltpu
from jax.sharding import PartitionSpec as P

CLUSTERS = 512
MOST = 5
ROOM = 32
TILE = 256
FAR = 2.0**100
LANES = 128
PARAMS = pltpu.CompilerParams(vmem_limit_bytes=40 * 1024 * 1024)
F32 = jnp.float32
BF16 = jnp.bfloat16
I32 = jnp.int32


def iota(shape, dim):
    return lax.broadcasted_iota(I32, shape, dim)


def flags(mask):
    return jnp.where(mask, 1.0, 0.0).astype(BF16)


def dot(a, b):
    return jnp.dot(a, b, preferred_element_type=F32)


def dot_t(a, b):
    return lax.dot_general(a, b, (((1,), (1,)), ((), ())), preferred_element_type=F32)


def shift_of(room):
    return room.bit_length() - 1


def to_col(row):
    size = row.shape[1]
    eye = iota((size, size), 0) == iota((size, size), 1)
    return jnp.sum(jnp.where(eye, row, 0.0), axis=1, keepdims=True)


def deal(position, owners, turn):
    bits = owners.bit_length() - 1
    level = position >> bits
    spot = position & (owners - 1)
    spot = jnp.where((level & 1) == 1, owners - 1 - spot, spot)
    return (spot + level * (turn * 11)) & (owners - 1), level


def match(room, counts, spot_rows, spot_cols, scr):
    set_scr, flip_scr, move_scr, row_scr, col_scr, first_scr, first_t_scr, state_scr, turned_scr = scr
    owners = counts[0].shape[0]
    shape = (owners, LANES)
    square = (LANES, LANES)
    tall = (CLUSTERS, LANES)
    wide = (owners, CLUSTERS)
    rows, cols, level_rows, level_cols = [], [], [], []
    for h in range(2):
        for spot, at, levels in ((spot_rows, rows, level_rows), (spot_cols, cols, level_cols)):
            chosen, level = deal(spot[h], owners, 0)
            at.append(chosen)
            levels.append(level)
    count_scr = counts[1]
    row_scr[...] = jnp.broadcast_to(spot_rows[1], row_scr.shape)
    col_scr[...] = jnp.broadcast_to(spot_cols[1], col_scr.shape)
    first_t_scr[...] = dot_t(flags(iota(wide, 0) == rows[0]), counts[0][...])
    eye = flags(iota((CLUSTERS, CLUSTERS), 0) == iota((CLUSTERS, CLUSTERS), 1))
    flip_scr[...] = dot_t(eye, counts[1][...]).astype(BF16)
    set_scr[...] = flags(iota(tall, 1) == cols[0])
    first_scr[...] = dot(counts[0][...], set_scr[...])

    def misfits():
        eye = iota(shape, 0) == iota(shape, 1)
        return float(owners) - jnp.sum(jnp.where(eye, state_scr[0:owners, :], 0.0))

    def fits(by_row, by_lane):
        most = jnp.zeros(shape, F32)
        for s in range(owners):
            most = jnp.maximum(most, by_row[:, s : s + 1] + by_lane[s : s + 1, :])
        return jnp.where((most <= float(room)) & (iota(shape, 1) < owners), 1.0, 0.0)

    def trade(step):
        eye = iota(shape, 0) == iota(shape, 1)
        fit = state_scr[0:owners, :]
        pairs = fit * turned_scr[0:owners, :]
        fine = jnp.where(eye, fit, 0.0)
        fine_row = jnp.sum(fine, axis=0, keepdims=True)
        fine_col = jnp.sum(fine, axis=1, keepdims=True)

        def granted(asker, asked, bad, good, axis):
            order = (asker * 37 + asked * 11 + step * 7) & (owners - 1)
            asks = pairs * (1.0 - bad) * good * (order + 1).astype(F32)
            asks = jnp.where(asks == jnp.max(asks, axis=axis, keepdims=True), asks, 0.0)
            asks = jnp.where(asks == jnp.max(asks, axis=1 - axis, keepdims=True), asks, 0.0)
            return jnp.minimum(asks, 1.0)

        both = granted(iota(shape, 0), iota(shape, 1), fine_col, fine_row, 1)
        both += granted(iota(shape, 1), iota(shape, 0), fine_row, fine_col, 0)
        settled = 1.0 - jnp.sum(both, axis=0, keepdims=True)
        move_scr[...] = jnp.where(
            iota(square, 0) == iota(square, 1), settled, 0.0
        ).astype(BF16)
        move_scr[0:owners, :] = (both + jnp.where(eye, settled, 0.0)).astype(BF16)
        state_scr[...] = dot(state_scr[...].astype(BF16), move_scr[...])
        turned_scr[...] = dot(move_scr[...], turned_scr[...].astype(BF16))

    def attempt(carry):
        turn, _ = carry
        at_row, _ = deal(row_scr[0:1, :], owners, turn)
        at_col, _ = deal(col_scr[...], owners, turn)
        set_scr[...] = flags(iota(tall, 1) == at_col)
        second = dot(count_scr[...], set_scr[...])
        second_t = dot(flags(iota(wide, 0) == at_row), flip_scr[...])
        state_scr[...] = iota(square, 1).astype(F32)
        state_scr[0:owners, :] = fits(first_t_scr[...], second)
        turned_scr[...] = jnp.zeros(square, F32)
        turned_scr[0:owners, :] = fits(second_t, first_scr[...])

        def trades(carry):
            step, _ = carry
            trade(step)
            return step + 1, misfits()

        _, left = lax.while_loop(
            lambda c: (c[1] > 0.5) & (c[0] < 6), trades, (jnp.int32(0), misfits())
        )
        return turn + 1, left

    turn, left = lax.while_loop(
        lambda c: (c[1] > 0.5) & (c[0] < 8), attempt, (jnp.int32(0), jnp.float32(1.0))
    )
    label = state_scr[owners : owners + 1, :]
    eye = iota(shape, 0) == iota(shape, 1)
    label_col = jnp.sum(jnp.where(eye, label, 0.0), axis=1, keepdims=True).astype(I32)
    at_row, _ = deal(row_scr[0:1, :], owners, turn - 1)
    at_col, _ = deal(col_scr[...], owners, turn - 1)
    row = jnp.where(label_col == at_row, iota(wide, 0).astype(F32), 0.0)
    rows[1] = jnp.sum(row, axis=0, keepdims=True).astype(I32)
    col = jnp.where(label.astype(I32) == at_col, iota(tall, 1).astype(F32), 0.0)
    cols[1] = jnp.sum(col, axis=1, keepdims=True).astype(I32)
    return rows, cols, level_rows, level_cols, left


def plan_kernel(
    room, all_ref, own_ref, ids_ref, rank_ref, place_ref, rows_ref, cols_ref, first_ref, over_ref, *scratch
):
    owners = all_ref.shape[0]
    owned = CLUSTERS // owners
    heads = ids_ref.shape[0]
    cluster_row = iota((1, CLUSTERS), 1).astype(F32)
    home = flags(iota((owners, CLUSTERS), 1) // owned == iota((owners, CLUSTERS), 0))
    counts, spot_rows, spot_cols = [], [], []
    for h in range(heads):
        count = all_ref[:, h * CLUSTERS : (h + 1) * CLUSTERS]
        total = jnp.sum(count.astype(F32), axis=0, keepdims=True)
        order_row = total * CLUSTERS + (CLUSTERS - 1 - cluster_row)
        order_col = to_col(order_row)
        spot_row = jnp.sum(jnp.where(order_col > order_row, 1.0, 0.0), axis=0, keepdims=True)
        spot_col = jnp.sum(jnp.where(order_row > order_col, 1.0, 0.0), axis=1, keepdims=True)
        counts.append(count)
        spot_rows.append(spot_row.astype(I32))
        spot_cols.append(spot_col.astype(I32))
    for scr, count in zip(scratch[:heads], counts):
        scr[...] = (count.astype(F32) + home.astype(F32)).astype(BF16)
    at_rows, at_cols, level_rows, level_cols, left = match(
        room, scratch[:heads], spot_rows, spot_cols, scratch[heads:]
    )
    over_ref[...] = jnp.full(over_ref.shape, jnp.where(left > 0.5, 1.0, 0.0))

    owns = [jnp.broadcast_to(own_ref[h : h + 1, :], (8, CLUSTERS)).astype(BF16) for h in range(heads)]
    for h in range(heads):
        before = flags((at_cols[h] == at_rows[h]) & (level_cols[h] < level_rows[h]))
        offset = dot(owns[h], before)
        if h == 1:
            offset = offset + dot(owns[0], flags(at_cols[0] == at_rows[1]))
        row_id = iota((8, CLUSTERS), 0)
        table = jnp.where(row_id == 0, at_rows[h].astype(F32), offset).astype(BF16)
        toks = ids_ref.shape[1]
        member = flags(iota((CLUSTERS, toks), 0) == ids_ref[h : h + 1, :])
        found = dot(table, member).astype(I32)
        place_ref[h : h + 1, :] = found[0:1] * room + found[1:2] + rank_ref[h : h + 1, :]

    rows_ref[...] = jnp.concatenate(at_rows + level_rows + [jnp.zeros((4, CLUSTERS), I32)], axis=0)
    column = iota((CLUSTERS, LANES), 1)
    found = jnp.zeros((CLUSTERS, LANES), I32)
    for i, values in enumerate(at_cols + level_cols):
        found = jnp.where(column == i, values, found)
    cols_ref[...] = found
    set_scr = scratch[heads]
    set_scr[...] = flags(at_cols[0] == column)
    first_ref[...] = dot(owns[0], set_scr[...])


def arrive_kernel(
    room,
    me_ref,
    all_ref,
    own_ref,
    rows_ref,
    cols_ref,
    sums_row_ref,
    sums_col_ref,
    query_ref,
    key_ref,
    member_ref,
):
    me = me_ref[0]
    owners = all_ref.shape[0]
    owned = CLUSTERS // owners
    heads = own_ref.shape[0]
    cluster_row = iota((1, CLUSTERS), 1).astype(F32)
    counts = [all_ref[:, h * CLUSTERS : (h + 1) * CLUSTERS] for h in range(heads)]
    owns = [jnp.broadcast_to(own_ref[h : h + 1, :], (8, CLUSTERS)).astype(BF16) for h in range(heads)]
    at_rows = [rows_ref[h : h + 1, :] for h in range(heads)]
    level_rows = [rows_ref[heads + h : heads + h + 1, :] for h in range(heads)]
    at_cols = [cols_ref[:, h : h + 1] for h in range(heads)]
    level_cols = [cols_ref[:, heads + h : heads + h + 1] for h in range(heads)]

    items = heads * owned
    lane = iota((CLUSTERS, LANES), 1)
    item = iota((items, CLUSTERS), 0)
    ends = jnp.zeros((owners, LANES), F32)
    ends_t = jnp.zeros((items, owners), F32)
    id_row = jnp.zeros((1, LANES), F32)
    id_col = jnp.zeros((items, 1), F32)
    for h in range(heads):
        ends += dot(counts[h], flags((at_cols[h] == me) & (level_cols[h] + h * owned <= lane)))
        ends_t += dot_t(flags((at_rows[h] == me) & (level_rows[h] + h * owned <= item)), counts[h])
        hit = (at_cols[h] == me) & (level_cols[h] + h * owned == lane)
        id_row += jnp.sum(jnp.where(hit, iota(lane.shape, 0).astype(F32), 0.0), axis=0, keepdims=True)
        hit = (at_rows[h] == me) & (level_rows[h] + h * owned == item)
        id_col += jnp.sum(jnp.where(hit, cluster_row, 0.0), axis=1, keepdims=True)
    rows = key_ref.shape[0]
    inside = ids_down(room, rows, items, ends)
    query_ref[...] = jnp.where(inside, 0.0, -FAR).astype(BF16)
    key_ref[...] = flags(inside)
    id_along = ids_along(room, rows, ends_t)
    member_ref[...] = flags(iota((items, rows), 0).astype(F32) == id_along)

    back_row = id_row.astype(I32) // owned
    back_col = id_col.astype(I32) // owned
    earlier = (back_col == back_row) & (iota((items, LANES), 0) < iota((items, LANES), 1))
    queue = jnp.sum(jnp.where(earlier, 1.0, 0.0), axis=0, keepdims=True)
    used = jnp.sum(
        jnp.where(iota((owners, LANES), 0) == back_row, ends[:, items - 1 : items], 0.0),
        axis=0,
        keepdims=True,
    )
    row = back_row * room + (queue + used).astype(I32)
    sums_row_ref[...] = jnp.broadcast_to(jnp.where(iota((1, LANES), 1) < items, row, -1), sums_row_ref.shape)

    at_lane = jnp.zeros((1, LANES), F32)
    turn_lane = jnp.zeros((1, LANES), F32)
    at_item = jnp.zeros((items, 1), F32)
    turn_item = jnp.zeros((items, 1), F32)
    sent = jnp.zeros((8, LANES), F32)
    for h in range(heads):
        low = me * owned - h * owned
        hit = (iota(lane.shape, 0) == lane + low) & (lane >= h * owned) & (lane < (h + 1) * owned)
        at_lane += jnp.sum(jnp.where(hit, at_cols[h].astype(F32), 0.0), axis=0, keepdims=True)
        turn_lane += jnp.sum(
            jnp.where(hit, (level_cols[h] + h * owned).astype(F32), 0.0), axis=0, keepdims=True
        )
        hit = (iota(item.shape, 1) == item + low) & (item >= h * owned) & (item < (h + 1) * owned)
        at_item += jnp.sum(jnp.where(hit, at_rows[h].astype(F32), 0.0), axis=1, keepdims=True)
        turn_item += jnp.sum(
            jnp.where(hit, (level_rows[h] + h * owned).astype(F32), 0.0), axis=1, keepdims=True
        )
        sent += dot(owns[h], flags(at_cols[h] == lane))
    small = iota((items, LANES), 1)
    ahead = (at_lane == at_item) & (turn_lane < turn_item) & (small < items)
    queue = jnp.sum(jnp.where(ahead, 1.0, 0.0), axis=1, keepdims=True)
    used = jnp.sum(
        jnp.where(small == at_item.astype(I32), sent[0:1], 0.0), axis=1, keepdims=True
    )
    sums_col_ref[...] = jnp.broadcast_to(
        at_item.astype(I32) * room + (queue + used).astype(I32), sums_col_ref.shape
    )


def make_plan(everyone, own, cluster_ids, rank, room):
    heads, toks = cluster_ids.shape
    owners = everyone.shape[0]
    return pl.pallas_call(
        functools.partial(plan_kernel, room),
        out_shape=(
            jax.ShapeDtypeStruct((heads, toks), I32),
            jax.ShapeDtypeStruct((8, CLUSTERS), I32),
            jax.ShapeDtypeStruct((CLUSTERS, LANES), I32),
            jax.ShapeDtypeStruct((8, LANES), F32),
            jax.ShapeDtypeStruct((8, LANES), F32),
        ),
        scratch_shapes=[
            pltpu.VMEM((owners, CLUSTERS), BF16),
            pltpu.VMEM((owners, CLUSTERS), BF16),
            pltpu.VMEM((CLUSTERS, LANES), BF16),
            pltpu.VMEM((CLUSTERS, owners), BF16),
            pltpu.VMEM((LANES, LANES), BF16),
            pltpu.VMEM((8, CLUSTERS), I32),
            pltpu.VMEM((CLUSTERS, LANES), I32),
            pltpu.VMEM((owners, LANES), F32),
            pltpu.VMEM((owners, owners), F32),
            pltpu.VMEM((LANES, LANES), F32),
            pltpu.VMEM((LANES, LANES), F32),
        ],
        compiler_params=PARAMS,
        cost_estimate=pl.CostEstimate(flops=10**9, bytes_accessed=10**6, transcendentals=0),
    )(everyone, own, cluster_ids, rank)


def arrive(me, everyone, own, rows, cols, room):
    owners = everyone.shape[0]
    items = own.shape[0] * CLUSTERS // owners
    vmem = pl.BlockSpec(memory_space=pltpu.VMEM)
    return pl.pallas_call(
        functools.partial(arrive_kernel, room),
        in_specs=[pl.BlockSpec(memory_space=pltpu.SMEM)] + [vmem] * 4,
        out_specs=[vmem] * 5,
        out_shape=(
            jax.ShapeDtypeStruct((8, LANES), I32),
            jax.ShapeDtypeStruct((items, LANES), I32),
            jax.ShapeDtypeStruct((owners * room, LANES), BF16),
            jax.ShapeDtypeStruct((owners * room, LANES), BF16),
            jax.ShapeDtypeStruct((items, owners * room), BF16),
        ),
        compiler_params=PARAMS,
        cost_estimate=pl.CostEstimate(flops=10**9, bytes_accessed=10**6, transcendentals=0),
    )(me, everyone, own, rows, cols)


def of_first(room, rows, base, first_ref):
    place = iota((rows, LANES), 0) + base
    here = (place >> shift_of(room)) == iota((rows, LANES), 1)
    first = jnp.sum(jnp.where(here, first_ref[0:1, :], 0.0), axis=1, keepdims=True)
    return (place[:, 0:1] & (room - 1)).astype(F32) < first


def pack_kernel(room, place_ref, first_ref, q_ref, k_ref, v_ref, out_ref):
    rows, toks = out_ref.shape[0], q_ref.shape[0]
    width = out_ref.shape[1] // 3
    base = pl.program_id(0) * rows
    wanted = iota((rows, toks), 0) + base
    pick = flags((wanted == place_ref[0:1, :]) | (wanted == place_ref[1:2, :]))
    is_first = of_first(room, rows, base, first_ref)
    for part, ref in enumerate((q_ref, k_ref, v_ref)):
        moved = dot(pick, ref[...])
        moved = jnp.where(is_first, moved[:, 0:width], moved[:, width:])
        out_ref[:, part * width : (part + 1) * width] = moved.astype(out_ref.dtype)


def pack(place, first, queries, keys, values, room, owners):
    toks, width = queries.shape
    heads = place.shape[0]
    rows_all = owners * room
    tile = 1024
    whole = pl.BlockSpec((toks, width), lambda i: (0, 0))
    return pl.pallas_call(
        functools.partial(pack_kernel, room),
        grid=(rows_all // tile,),
        in_specs=[
            pl.BlockSpec((heads, toks), lambda i: (0, 0)),
            pl.BlockSpec(first.shape, lambda i: (0, 0)),
            whole,
            whole,
            whole,
        ],
        out_specs=pl.BlockSpec((tile, 3 * width // heads), lambda i: (i, 0)),
        out_shape=jax.ShapeDtypeStruct((rows_all, 3 * width // heads), queries.dtype),
        compiler_params=PARAMS,
        cost_estimate=pl.CostEstimate(
            flops=6 * rows_all * toks * width,
            bytes_accessed=rows_all * width * 3,
            transcendentals=0,
        ),
    )(place, first, queries, keys, values)


def ids_along(room, rows, ends_t):
    items, sources = ends_t.shape
    spread = flags((iota((sources, rows), 1) >> shift_of(room)) == iota((sources, rows), 0))
    ends_row = dot(ends_t.astype(BF16), spread)
    slot_row = (iota((items, rows), 1) & (room - 1)).astype(F32)
    return jnp.sum(jnp.where(ends_row <= slot_row, 1.0, 0.0), axis=0, keepdims=True)


def ids_down(room, rows, items, ends):
    sources = ends.shape[0]
    spread = flags((iota((rows, sources), 0) >> shift_of(room)) == iota((rows, sources), 1))
    lane = iota(ends.shape, 1)
    ends = jnp.where(lane < items, ends, float(2 * LANES))
    starts = jnp.where(lane == 0, 0.0, pltpu.roll(ends, 1, 1))
    bounds = dot(spread, jnp.concatenate([starts, ends], axis=1).astype(BF16))
    slot = (iota((rows, LANES), 0) & (room - 1)).astype(F32)
    return (bounds[:, 0:LANES] <= slot) & (slot < bounds[:, LANES:])


def unit_sums(key_rows, member):
    key_float = key_rows.astype(F32)
    unit = key_float * lax.rsqrt(jnp.sum(key_float * key_float, axis=1, keepdims=True) + 1e-06)
    high = unit.astype(BF16)
    low = (unit - high.astype(F32)).astype(BF16)
    halves = dot(member, jnp.concatenate([high, low], axis=1))
    return (halves[:, 0 : high.shape[1]] + halves[:, high.shape[1] :]).astype(BF16)


def fill(query_ref, key_ref, member_ref, x_ref, query_scr, key_scr, value_scr):
    rows, width = x_ref.shape[0], x_ref.shape[1] // 3
    query_scr[:, 0:width] = x_ref[:, 0:width]
    query_scr[:, width:] = query_ref[...]
    key_scr[:, 0:width] = x_ref[:, width : 2 * width]
    key_scr[:, width:] = key_ref[...]
    value_scr[:, 0:width] = x_ref[:, 2 * width : 3 * width]
    value_scr[:, width:] = jnp.ones((rows, LANES), BF16)
    return unit_sums(x_ref[:, width : 2 * width], member_ref[...])


def weigh(pieces, values, width):
    scale = math.log2(math.e) / math.sqrt(width)
    highest = jnp.max(pieces[0], axis=1, keepdims=True)
    for scores in pieces[1:]:
        highest = jnp.maximum(highest, jnp.max(scores, axis=1, keepdims=True))
    result = jnp.zeros((highest.shape[0], width + LANES), F32)
    for scores, value in zip(pieces, values):
        raised = jnp.exp2((scores - highest) * scale)
        result += dot(raised.astype(BF16), value)
    return result[:, 0:width] / result[:, width : width + 1]


def homeward(begin, tile, sums_row_ref, sums):
    pick = flags(iota((tile, LANES), 0) + begin == sums_row_ref[0:1, :])
    return dot(pick[:, 0 : sums.shape[0]], sums)


def attend_kernel(
    query_ref, key_ref, member_ref, sums_row_ref, x_ref, out_ref, query_scr, key_scr, value_scr
):
    rows, width = out_ref.shape
    sums = fill(query_ref, key_ref, member_ref, x_ref, query_scr, key_scr, value_scr)

    def scores_of(begin):
        end = begin + TILE
        query = query_scr[begin:end, :]
        pieces = [dot_t(query, key_scr[0:begin, :])] if begin else []
        scores = dot_t(query, key_scr[begin:end, :])
        allowed = iota((TILE, TILE), 1) <= iota((TILE, TILE), 0)
        return pieces + [jnp.where(allowed, scores, -FAR)]

    ahead = scores_of(0)
    for begin in range(0, rows, TILE):
        end = begin + TILE
        pieces = ahead
        ahead = scores_of(end) if end < rows else None
        values = [value_scr[0:begin, :]] if begin else []
        values.append(value_scr[begin:end, :])
        result = weigh(pieces, values, width) + homeward(begin, TILE, sums_row_ref, sums)
        out_ref[begin:end] = result.astype(out_ref.dtype)


def attend_tile_kernel(
    query_ref,
    key_ref,
    member_ref,
    sums_row_ref,
    x_ref,
    out_ref,
    query_scr,
    key_scr,
    value_scr,
    sums_scr,
):
    tile, width = out_ref.shape
    rows = x_ref.shape[0]

    @pl.when(pl.program_id(0) == 0)
    def _():
        sums_scr[...] = fill(query_ref, key_ref, member_ref, x_ref, query_scr, key_scr, value_scr)

    begin = pl.multiple_of(pl.program_id(0) * tile, tile)
    scores = dot_t(query_scr[pl.ds(begin, tile), :], key_scr[...])
    allowed = iota((tile, rows), 1) <= iota((tile, rows), 0) + begin
    result = weigh([jnp.where(allowed, scores, -FAR)], [value_scr[...]], width)
    out_ref[...] = (result + homeward(begin, tile, sums_row_ref, sums_scr[...])).astype(out_ref.dtype)


def attend(query_far, key_far, member, sums_row, received):
    rows, width = received.shape[0], received.shape[1] // 3
    shape = jax.ShapeDtypeStruct((rows, width), received.dtype)
    cost = pl.CostEstimate(
        flops=2 * rows * rows * width,
        bytes_accessed=rows * width * 8,
        transcendentals=rows * rows // 2,
    )
    given = (query_far, key_far, member, sums_row, received)
    filled = [pltpu.VMEM((rows, width + LANES), BF16)] * 3
    if rows <= 4096:
        return pl.pallas_call(
            attend_kernel,
            out_shape=shape,
            scratch_shapes=filled,
            compiler_params=PARAMS,
            cost_estimate=cost,
        )(*given)
    tile = 128
    return pl.pallas_call(
        attend_tile_kernel,
        grid=(rows // tile,),
        in_specs=[pl.BlockSpec(x.shape, lambda i: (0, 0)) for x in given],
        out_specs=pl.BlockSpec((tile, width), lambda i: (i, 0)),
        out_shape=shape,
        scratch_shapes=filled + [pltpu.VMEM((member.shape[0], width), BF16)],
        compiler_params=PARAMS,
        cost_estimate=cost,
    )(*given)


def unpack_kernel(
    room, place_ref, sums_col_ref, first_ref, over_ref, back_ref, out_ref, sums_ref, pair_scr
):
    toks, heads = place_ref.shape
    rows, width = back_ref.shape
    groups, share, _ = out_ref.shape

    @pl.when(pl.program_id(0) == 0)
    def _():
        back = back_ref[...]
        is_first = of_first(room, rows, 0, first_ref)
        pair_scr[:, 0:width] = jnp.where(is_first, back.astype(F32), 0.0).astype(BF16)
        pair_scr[:, width:] = jnp.where(is_first, 0.0, back.astype(F32)).astype(BF16)
        items = sums_col_ref.shape[0]
        pick = flags(iota((items, rows), 1) == sums_col_ref[:, 0:1])
        sums_ref[...] = dot(pick, back)

    wanted = iota((toks, rows), 1)
    pick = flags((wanted == place_ref[:, 0:1]) | (wanted == place_ref[:, 1:2]))
    moved = dot(pick, pair_scr[...])
    moved = jnp.where(over_ref[0:1, 0:1] > 0.5, jnp.nan, moved).astype(out_ref.dtype)
    for g in range(groups):
        out_ref[g] = moved[g * share : (g + 1) * share]


def unpack(place, sums_col, first, over, back, groups, room):
    (toks, heads), (rows, width) = place.shape, back.shape
    share = toks // groups
    items = sums_col.shape[0]
    steps = max(1, min(groups, groups * rows // 8192))
    whole = lambda i: (0, 0)
    return pl.pallas_call(
        functools.partial(unpack_kernel, room),
        grid=(steps,),
        in_specs=[
            pl.BlockSpec((toks // steps, heads), lambda i: (i, 0)),
            pl.BlockSpec(sums_col.shape, whole),
            pl.BlockSpec(first.shape, whole),
            pl.BlockSpec(over.shape, whole),
            pl.BlockSpec((rows, width), whole),
        ],
        out_specs=(
            pl.BlockSpec((groups // steps, share, heads * width), lambda i: (i, 0, 0)),
            pl.BlockSpec((items, width), whole),
        ),
        out_shape=(
            jax.ShapeDtypeStruct((groups, share, heads * width), back.dtype),
            jax.ShapeDtypeStruct((items, width), F32),
        ),
        scratch_shapes=[pltpu.VMEM((rows, heads * width), BF16)],
        compiler_params=PARAMS,
        cost_estimate=pl.CostEstimate(
            flops=2 * rows * toks * width * heads,
            bytes_accessed=rows * width * 2,
            transcendentals=0,
        ),
    )(place, sums_col, first, over, back)


def exchange(rows, axis):
    return lax.all_to_all(rows, axis, split_axis=0, concat_axis=0, tiled=True)


def routed(room, queries, keys, values, cluster_ids, rank, own, everyone):
    heads = cluster_ids.shape[0]
    owners = everyone.shape[0]
    me = lax.axis_index("seq").astype(I32)[None]
    place, rows, cols, first, over = make_plan(everyone, own, cluster_ids, rank, room)
    received = exchange(pack(place, first, queries, keys, values, room, owners), "seq")
    sums_row, sums_col, query_far, key_far, member = arrive(me, everyone, own, rows, cols, room)
    back = exchange(attend(query_far, key_far, member, sums_row, received), "seq")
    share, sums = unpack(place.T, sums_col, first, over, back, lax.axis_size("head"), room)
    parts = exchange(share, "head")
    owned = CLUSTERS // owners
    sums = jnp.concatenate([sums[h * owned : (h + 1) * owned] for h in range(heads)], axis=1)
    return parts, sums


def project(parts, weight):
    weight = weight.reshape(parts.shape[0], parts.shape[2], weight.shape[1])
    total = jnp.einsum("gtd,gdn->tn", parts, weight, preferred_element_type=F32)
    return total.astype(BF16)


def count_kernel(ids_ref, own_ref, told_ref, member_scr):
    heads, toks = ids_ref.shape
    chunks = []
    for h in range(heads):
        member_scr[h] = flags(iota((CLUSTERS, toks), 0) == ids_ref[h : h + 1, :])
        own = dot_t(jnp.ones((8, toks), BF16), member_scr[h])
        own_ref[h : h + 1, :] = own[0:1]
        chunks += [own[0:1, at : at + LANES] for at in range(0, CLUSTERS, LANES)]
    told_ref[...] = jnp.broadcast_to(jnp.concatenate(chunks, axis=0)[None], told_ref.shape).astype(BF16)


def count(cluster_ids, owners):
    heads, toks = cluster_ids.shape
    return pl.pallas_call(
        count_kernel,
        out_shape=(
            jax.ShapeDtypeStruct((heads, CLUSTERS), F32),
            jax.ShapeDtypeStruct((owners, heads * CLUSTERS // LANES, LANES), BF16),
        ),
        scratch_shapes=[pltpu.VMEM((heads, CLUSTERS, toks), BF16)],
        compiler_params=PARAMS,
        cost_estimate=pl.CostEstimate(flops=10**8, bytes_accessed=10**5, transcendentals=0),
    )(cluster_ids)


def body(queries, keys, values, cluster_ids, out_weight):
    heads, toks = cluster_ids.shape
    owners = lax.axis_size("seq")
    own, told = count(cluster_ids, owners)
    everyone = exchange(told, "seq").reshape(owners, heads * CLUSTERS)
    own, out_weight = lax.optimization_barrier((own, out_weight))
    full_weight = lax.all_gather(out_weight, "head", axis=0, tiled=True)

    spot = jnp.arange(toks, dtype=I32)
    same = cluster_ids[:, :, None] == cluster_ids[:, None, :]
    rank = jnp.sum((same & (spot[:, None] < spot[None, :])[None]).astype(I32), axis=1)
    given = (queries, keys, values, cluster_ids, rank, own, everyone)
    parts, key_sums = routed(ROOM, *given)
    full_room = 1 << (heads * CLUSTERS // owners * (MOST + 1) - 1).bit_length()

    def again():
        wide, wide_sums = routed(full_room, *given)
        return project(wide, full_weight), wide_sums

    def done():
        return project(parts, full_weight), key_sums

    return lax.cond(jnp.any(jnp.isnan(parts[:, 0, 0])), again, done)


def solution(mesh):
    placed = (
        P("seq", "head"),
        P("seq", "head"),
        P("seq", "head"),
        P("head", "seq"),
        P("head", None),
    )
    return jax.shard_map(
        body,
        mesh=mesh,
        in_specs=placed,
        out_specs=(P(("seq", "head"), None), P("seq", "head")),
        check_vma=False,
    )
```
